32 devices in a mesh: dp: 4 (over y, x), fsdp: 8 (over z, core).
Axes of the slice: x: 2, y: 2, z: 4, core: 2. Of those that a mesh axis runs over, the one named last changes fastest.
Arguments:
- tokens: bfloat16 [4864, 1024], P(('dp', 'fsdp')), may hold values from -6 to 6
- pos_table: bfloat16 [145, 1024], P(None, 'fsdp'), may hold values from -3 to 3
- index_lo: int32 [50, 4], replicated, may hold values from 0 to 144
- index_hi: int32 [145, 4], replicated, may hold values from 0 to 144
- resolution: int32 [4], replicated, may hold values from 0 to 1, as said below
- gain_attn: bfloat16 [2, 1024], P(None, 'fsdp'), may hold values from 0.099609375 to 1.8984375
- w_qkv: bfloat16 [2, 1024, 3072], P(None, 'fsdp'), may hold values from -0.1875 to 0.1875
- w_out: bfloat16 [2, 1024, 1024], P(None, 'fsdp'), may hold values from -0.75 to 0.75
- gain_mlp: bfloat16 [2, 1024], P(None, 'fsdp'), may hold values from 0.099609375 to 1.8984375
- w_up: bfloat16 [2, 1024, 4096], P(None, 'fsdp'), may hold values from -0.1875 to 0.1875
- w_down: bfloat16 [2, 4096, 1024], P(None, 'fsdp'), may hold values from -0.09375 to 0.09375
- cotangent: bfloat16 [4864, 1024], P(('dp', 'fsdp')), may hold values from -6 to 6
Outputs:
- output: float32 [4864, 1024], P(('dp', 'fsdp'))
- d_tokens: float32 [4864, 1024], P(('dp', 'fsdp'))
- d_pos_table: float32 [145, 1024], P(None, 'fsdp')
- d_gain_attn: float32 [2, 1024], P(None, 'fsdp')
- d_w_qkv: float32 [2, 1024, 3072], P(None, 'fsdp')
- d_w_out: float32 [2, 1024, 1024], P(None, 'fsdp')
- d_gain_mlp: float32 [2, 1024], P(None, 'fsdp')
- d_w_up: float32 [2, 1024, 4096], P(None, 'fsdp')
- d_w_down: float32 [2, 4096, 1024], P(None, 'fsdp')
The draws below stay inside these ranges and needn't reach their ends.
Inputs may be any that keep to these rules, and one draw needn't show every extreme that they name: 1 marks a group of the higher resolution (145 tokens an image), 0 one of the lower (50); both occur in every draw.
All inputs are finite; a program needn't handle non-finite values.
Results may differ from the reference program's by a relative error of at most 0.025.
Values may be sent and summed in bfloat16 or wider, within the bound.
No kernel may reach another device: no remote copies, remote signals or barrier semaphores. Data moves between devices by JAX's collectives and lax.ppermute only.
A program may use at most 320 MiB of HBM per device.

```python
import math
import jax
import jax.numpy as jnp
from jax import lax

D = 1024
FF = 4096
HEADS = 16
LAYERS = 2
LEN_LO = 50
LEN_HI = 145
ROWS_DEV = 152
LO_IMG = 3
HI_IMG = 1
TOTAL_ROWS = 4864
N_DP = 4
N_FSDP = 8


def draw_resolution(key, part):
    key = jax.random.fold_in(key, 11)
    key_count, key_order = jax.random.split(key)
    low_count = jax.random.randint(key_count, (), 1, N_DP)
    ranking = jax.random.permutation(key_order, N_DP)
    return (ranking >= low_count).astype(jnp.int32)


def plant(drawn, own_key, least, top_value):
    place = [jax.random.randint(jax.random.fold_in(own_key, axis), (), 0, length) for axis, length in enumerate(drawn.shape)]
    main_axis = drawn.shape.index(max(drawn.shape))
    next_to = place[:main_axis] + [(place[main_axis] + 1) % drawn.shape[main_axis]] + place[main_axis + 1:]
    return drawn.at[tuple(place)].set(least).at[tuple(next_to)].set(top_value)


def block_levels(own_key, dims, shards, low, largest):
    gain, own = 1.0, jax.random.fold_in(own_key, 6)
    for position, parts in shards:
        steps = jnp.exp(jax.random.uniform(jax.random.fold_in(own, position), (parts,), jnp.float32, low / len(shards), largest / len(shards)))
        gain = gain * jnp.repeat(steps, dims[position] // parts).reshape([-1 if axis == position else 1 for axis in range(len(dims))])
    return gain


def centred(key, shape, width, bound, shards=(), kind=jnp.bfloat16):
    values = jax.random.normal(key, shape, jnp.float32) * width
    if len(shards) > 0:
        values = block_levels(key, shape, shards, -0.22, 0.18) * values
    return jnp.clip(values, min=-bound, max=bound).astype(kind)


def setup_inputs(seed: int = 0) -> dict:
    arg_keys = jax.random.split(jax.random.key(seed), 13)
    tokens = centred(arg_keys[0], (TOTAL_ROWS, D), 1.0, 6.0, ((0, 32),))
    pos_table = centred(arg_keys[1], (LEN_HI, D), 0.5, 3.0, ((1, 8),))
    index_lo = plant(jax.random.randint(arg_keys[2], (LEN_LO, 4), 0, LEN_HI), jax.random.fold_in(arg_keys[2], 1), 0, LEN_HI - 1).astype(jnp.int32)
    index_hi = plant(jax.random.randint(arg_keys[3], (LEN_HI, 4), 0, LEN_HI), jax.random.fold_in(arg_keys[3], 1), 0, LEN_HI - 1).astype(jnp.int32)
    resolution = draw_resolution(jax.random.fold_in(arg_keys[12], 71), 0)
    gain_attn = jnp.clip(1.0 + 0.18 * jax.random.normal(arg_keys[5], (LAYERS, D), jnp.float32), 0.099609375, 1.8984375).astype(jnp.bfloat16)
    w_qkv = centred(arg_keys[6], (LAYERS, D, 3 * D), D ** -0.5, 0.1875, ((1, 8),))
    w_out = centred(arg_keys[7], (LAYERS, D, D), (D // 16) ** -0.5, 0.75, ((1, 8),))
    gain_mlp = jnp.clip(1.0 + 0.18 * jax.random.normal(arg_keys[8], (LAYERS, D), jnp.float32), 0.099609375, 1.8984375).astype(jnp.bfloat16)
    w_up = centred(arg_keys[9], (LAYERS, D, FF), D ** -0.5, 0.1875, ((1, 8),))
    w_down = centred(arg_keys[10], (LAYERS, FF, D), FF ** -0.5, 0.09375, ((1, 8),))
    cotangent = centred(arg_keys[11], (TOTAL_ROWS, D), 1.0, 6.0, ((0, 32),))
    return dict(tokens=tokens, pos_table=pos_table, index_lo=index_lo, index_hi=index_hi, resolution=resolution, gain_attn=gain_attn, w_qkv=w_qkv, w_out=w_out, gain_mlp=gain_mlp, w_up=w_up, w_down=w_down, cotangent=cotangent)


EPS = 1e-06
NEG_FILL = -1e+30
MIX_WEIGHTS = (0.5, 0.25, 0.125, 0.125)
PRECISE = lax.Precision.HIGHEST

@jax.custom_vjp
def low(v):
    return lax.optimization_barrier(v.astype(jnp.bfloat16)).astype(jnp.float32)

@jax.custom_vjp
def low_back(v):
    return v

def low_keep(v):
    return (low(v), None)

def low_pass(kept, grad):
    return (grad,)

def back_keep(v):
    return (v, None)

def back_low(kept, grad):
    return (low(grad),)
low.defvjp(low_keep, low_pass)
low_back.defvjp(back_keep, back_low)

def rounded_both(value):
    return low(low_back(value))

def layer_norm(hidden, gain_row):
    row_mean = lax.optimization_barrier(jnp.mean(hidden, axis=-1, keepdims=True))
    center = hidden - row_mean
    spread = lax.optimization_barrier(jnp.mean(center * center, axis=-1, keepdims=True))
    return center * lax.rsqrt(spread + EPS) * gain_row

def geometry(group_flag, index_lo, index_hi):
    row_ids = jnp.arange(ROWS_DEV, dtype=jnp.int32)
    length = jnp.where(group_flag == 1, LEN_HI, LEN_LO).astype(jnp.int32)
    image_count = jnp.where(group_flag == 1, HI_IMG, LO_IMG).astype(jnp.int32)
    live_rows = row_ids < image_count * length
    image_ids = jnp.where(live_rows, row_ids // length, image_count)
    picked = jnp.where(group_flag == 1, index_hi[row_ids % LEN_HI], index_lo[row_ids % LEN_LO])
    table_ids = jnp.arange(LEN_HI, dtype=jnp.int32)
    mixing = jnp.zeros((ROWS_DEV, LEN_HI), jnp.float32)
    for slot in range(4):
        mixing = mixing + MIX_WEIGHTS[slot] * (picked[:, slot:slot + 1] == table_ids[None, :]).astype(jnp.float32)
    mixing = mixing * live_rows[:, None].astype(jnp.float32)
    return (image_ids, live_rows, mixing)

def token_weight(group_flag, resolution):
    row_ids = jnp.arange(ROWS_DEV, dtype=jnp.int32)
    high_groups = jnp.sum(resolution).astype(jnp.int32)
    tokens_low = ((N_DP - high_groups) * N_FSDP * LO_IMG * LEN_LO).astype(jnp.float32)
    tokens_high = (high_groups * N_FSDP * HI_IMG * LEN_HI).astype(jnp.float32)
    token_share = 2.0 * jnp.where(group_flag == 1, tokens_high, tokens_low) / (tokens_low + tokens_high)
    length = jnp.where(group_flag == 1, LEN_HI, LEN_LO).astype(jnp.int32)
    image_count = jnp.where(group_flag == 1, HI_IMG, LO_IMG).astype(jnp.int32)
    return jnp.where(row_ids < image_count * length, token_share, jnp.zeros((), jnp.float32))

def residual_block(hidden, same_image, gain_a, w_qkv, w_out, gain_m, w_up, w_down):
    head_size = D // HEADS
    score_scale = 1.0 / math.sqrt(head_size)
    normed_attn = low(layer_norm(hidden, gain_a))
    projected = rounded_both(jnp.dot(normed_attn, w_qkv, precision=PRECISE))
    queries = projected[:, :D].reshape(ROWS_DEV, HEADS, head_size)
    key_rows = projected[:, D:2 * D].reshape(ROWS_DEV, HEADS, head_size)
    values = projected[:, 2 * D:].reshape(ROWS_DEV, HEADS, head_size)
    scores = low_back(jnp.einsum('qhd,khd->hqk', queries, key_rows, precision=PRECISE) * score_scale)
    scores = jnp.where(same_image[None], scores, NEG_FILL)
    row_max = lax.optimization_barrier(jnp.max(scores, axis=-1, keepdims=True))
    powers = jnp.exp(scores - row_max)
    probs = low(powers / lax.optimization_barrier(jnp.sum(powers, axis=-1, keepdims=True)))
    attended = jnp.einsum('hqk,khd->qhd', probs, values, precision=PRECISE).reshape(ROWS_DEV, D)
    attended = rounded_both(attended)
    middle = hidden + low_back(jnp.dot(attended, w_out, precision=PRECISE))
    normed_mlp = low(layer_norm(middle, gain_m))
    pre_act = low_back(jnp.dot(normed_mlp, w_up, precision=PRECISE))
    activated = low(jax.nn.gelu(pre_act, approximate=False))
    return middle + low_back(jnp.dot(activated, w_down, precision=PRECISE))

def device_forward(params, tokens, group_flag, index_lo, index_hi):
    table, gain_attn, w_qkv, w_out, gain_mlp, w_up, w_down = params
    image_ids, live_rows, mixing = geometry(group_flag, index_lo, index_hi)
    same_image = image_ids[:, None] == image_ids[None, :]
    hidden = tokens + jnp.dot(mixing, table, precision=PRECISE)
    for depth in range(LAYERS):
        hidden = residual_block(hidden, same_image, gain_attn[depth], w_qkv[depth], w_out[depth], gain_mlp[depth], w_up[depth], w_down[depth])
    return hidden

def reference(tokens, pos_table, index_lo, index_hi, resolution, gain_attn, w_qkv, w_out, gain_mlp, w_up, w_down, cotangent):
    params = tuple((array.astype(jnp.float32) for array in (pos_table, gain_attn, w_qkv, w_out, gain_mlp, w_up, w_down)))
    devices = N_DP * N_FSDP
    per_step = 8 if devices % 8 == 0 else 1
    step_count = devices // per_step
    token_blocks = tokens.astype(jnp.float32).reshape(step_count, per_step, ROWS_DEV, D)
    cot_blocks = cotangent.astype(jnp.float32).reshape(step_count, per_step, ROWS_DEV, D)
    device_ids = jnp.arange(devices, dtype=jnp.int32)
    flag_blocks = resolution[device_ids // N_FSDP].astype(jnp.int32).reshape(step_count, per_step)

    def block_step(running, block_item):
        block_tokens, block_cots, block_flags = block_item

        def forward_block(inner_params, inner_tokens):
            return jax.vmap(device_forward, in_axes=(None, 0, 0, None, None))(inner_params, inner_tokens, block_flags, index_lo, index_hi)
        result, pullback = jax.vjp(forward_block, params, block_tokens)
        weights = jax.vmap(token_weight, in_axes=(0, None))(block_flags, resolution)
        param_grads, token_grads = pullback(block_cots * weights[:, :, None])
        return (jax.tree.map(jnp.add, running, param_grads), (result, token_grads))
    zero_grads = jax.tree.map(jnp.zeros_like, params)
    grads, (results, token_grads) = lax.scan(block_step, zero_grads, (token_blocks, cot_blocks, flag_blocks))
    return (results.reshape(-1, D), token_grads.reshape(-1, D), grads[0], grads[1], grads[2], grads[3], grads[4], grads[5], grads[6])
```

```python
import math

import jax
import jax.numpy as jnp
from jax import lax
from jax.sharding import PartitionSpec as P

HEADS = 16
EPS = 1e-06
NEG_FILL = -1e30
MIX_WEIGHTS = (0.5, 0.25, 0.125, 0.125)
BF16 = jnp.bfloat16
F32 = jnp.float32


def dot(a, b):
    return jnp.dot(a, b, preferred_element_type=F32)


def dot_t(a, b):
    return lax.dot_general(a, b, (((0,), (0,)), ((), ())), preferred_element_type=F32)


def dot_nt(a, b):
    return lax.dot_general(a, b, (((1,), (1,)), ((), ())), preferred_element_type=F32)


def normalize(hidden):
    center = hidden - jnp.mean(hidden, axis=-1, keepdims=True)
    rstd = lax.rsqrt(jnp.mean(center * center, axis=-1, keepdims=True) + EPS)
    return center * rstd, rstd


def norm_backward(e, xhat, rstd):
    return rstd * (
        e
        - jnp.mean(e, axis=-1, keepdims=True)
        - xhat * jnp.mean(e * xhat, axis=-1, keepdims=True)
    )


def gelu_exact(pre_act):
    return jax.nn.gelu(pre_act, approximate=False)


class Square:
    def __init__(self):
        self.count = lax.axis_size("dp")
        self.me = lax.axis_index("dp")
        self.pairs = self.count == 4

    def owners(self):
        if self.pairs:
            return [self.me ^ k for k in range(self.count)]
        return [jnp.int32(k) for k in range(self.count)]

    def swap(self, block, k):
        return lax.ppermute(block, "dp", [(i, i ^ k) for i in range(self.count)])

    def spread(self, block):
        if self.pairs:
            return [block] + [self.swap(block, k) for k in range(1, self.count)]
        full = lax.all_gather(block, "dp")
        return [full[k] for k in range(self.count)]

    def collect(self, parts):
        if self.pairs:
            total = parts[0].astype(F32)
            for k in range(1, self.count):
                total = total + self.swap(parts[k].astype(BF16), k).astype(F32)
            return total
        stacked = jnp.stack([part.astype(BF16) for part in parts])
        return lax.psum_scatter(stacked, "dp", scatter_dimension=0, tiled=False).astype(F32)

    def gather(self, piece):
        if not self.pairs:
            return lax.all_gather(piece, "dp")
        got = [piece] + [self.swap(piece, k) for k in range(1, self.count)]
        odd = (self.me & 1) == 1
        high = (self.me & 2) == 2
        low_pair = (jnp.where(odd, got[1], got[0]), jnp.where(odd, got[0], got[1]))
        far_pair = (jnp.where(odd, got[3], got[2]), jnp.where(odd, got[2], got[3]))
        return jnp.stack(
            [
                jnp.where(high, far_pair[0], low_pair[0]),
                jnp.where(high, far_pair[1], low_pair[1]),
                jnp.where(high, low_pair[0], far_pair[0]),
                jnp.where(high, low_pair[1], far_pair[1]),
            ]
        )

    def total(self, piece):
        if not self.pairs:
            return lax.psum(piece.astype(BF16), "dp").astype(F32)
        own = piece.astype(BF16)
        got = [own.astype(F32)] + [self.swap(own, k).astype(F32) for k in range(1, self.count)]
        return (got[0] + got[1]) + (got[2] + got[3])


def select(index, choices):
    out = choices[0]
    for k in range(1, len(choices)):
        out = jnp.where(index == k, choices[k], out)
    return out


def local(
    tokens,
    pos_table,
    index_lo,
    index_hi,
    resolution,
    gain_attn,
    w_qkv,
    w_out,
    gain_mlp,
    w_up,
    w_down,
    cotangent,
):
    row_count, width = tokens.shape
    layers, shard_rows, _ = w_qkv.shape
    hidden_units = w_up.shape[2]
    shard_count = lax.axis_size("fsdp")
    shard = lax.axis_index("fsdp")
    square = Square()
    group_count = square.count
    me = square.me
    head_size = width // HEADS
    my_heads = HEADS // group_count
    part = my_heads * head_size
    unit_part = hidden_units // group_count
    fine = square.pairs and shard_count * 2 == HEADS
    score_scale = 1.0 / math.sqrt(head_size)
    len_low = index_lo.shape[0]
    len_high = index_hi.shape[0]

    row_ids = jnp.arange(row_count, dtype=jnp.int32)

    def layout(flag):
        length = jnp.where(flag == 1, len_high, len_low).astype(jnp.int32)
        images = jnp.where(flag == 1, row_count // len_high, row_count // len_low).astype(jnp.int32)
        live = row_ids < images * length
        return live, jnp.where(live, row_ids // length, images)

    flag = resolution[me]
    live_rows, _ = layout(flag)
    block_ids = jnp.stack([layout(resolution[owner])[1] for owner in square.owners()])
    same_image = block_ids[:, :, None] == block_ids[:, None, :]
    picked = jnp.where(flag == 1, index_hi[row_ids % len_high], index_lo[row_ids % len_low])
    table_ids = jnp.arange(len_high, dtype=jnp.int32)
    mixing = jnp.zeros((row_count, len_high), F32)
    for slot in range(4):
        mixing = mixing + MIX_WEIGHTS[slot] * (
            picked[:, slot : slot + 1] == table_ids[None, :]
        ).astype(F32)
    mixing = (mixing * live_rows[:, None].astype(F32)).astype(BF16)
    high_groups = jnp.sum(resolution)
    tokens_low = (
        (group_count - high_groups) * shard_count * (row_count // len_low) * len_low
    ).astype(F32)
    tokens_high = (high_groups * shard_count * (row_count // len_high) * len_high).astype(F32)
    token_share = 2.0 * jnp.where(flag == 1, tokens_high, tokens_low) / (tokens_low + tokens_high)
    weight = jnp.where(live_rows, token_share, 0.0)

    half = shard_rows // 4
    core = shard % 2
    swap_core = [(j, j ^ 1) for j in range(shard_count)]
    pair_side, head_side = me & 1, (me >> 1) & 1

    def qkv_part(w):
        if fine:
            view = w.reshape(shard_rows, 3 * HEADS // 4, 2, 2, head_size)
            view = select(pair_side, [view[:, :, 0], view[:, :, 1]])
            view = select(head_side, [view[:, :, 0], view[:, :, 1]])
            return view.reshape(shard_rows, 3 * part)
        view = w.reshape(shard_rows, 3, group_count, part)
        return lax.dynamic_index_in_dim(view, me, 2, keepdims=False).reshape(shard_rows, 3 * part)

    def up_part(w):
        view = w.reshape(shard_rows, shard_count, group_count, unit_part // shard_count)
        return lax.dynamic_index_in_dim(view, me, 2, keepdims=False).reshape(shard_rows, unit_part)

    def down_part(w):
        rows = unit_part // shard_count
        return lax.dynamic_slice_in_dim(w, me * rows, rows, 0)

    def out_part(w):
        if fine:
            view = w.reshape(2, 2, half, width)
            mine = select(head_side, [view[0], view[1]])
            keep = select(core, [mine[0], mine[1]])
            give = select(core, [mine[1], mine[0]])
            got = lax.ppermute(give, "fsdp", swap_core)
            return jnp.where(core == pair_side, keep, got)
        return w

    def fetch(piece):
        return lax.all_gather(piece, "fsdp", axis=0, tiled=False)

    weights = []
    table = lax.all_gather(pos_table, "fsdp", axis=1, tiled=True)
    for depth in range(layers):
        gain_a = gain_attn[depth].astype(F32)[:, None]
        gain_m = gain_mlp[depth].astype(F32)[:, None]
        qkv = (qkv_part(w_qkv[depth]).astype(F32) * gain_a).astype(BF16)
        up = (up_part(w_up[depth]).astype(F32) * gain_m).astype(BF16)
        down = down_part(w_down[depth])
        out = out_part(w_out[depth])
        qkv_all = fetch(qkv).reshape(width, 3 * part)
        a = up.size // width
        b = a + down.shape[0]
        rest = fetch(jnp.concatenate([up.reshape(a, width), down, out], axis=0))
        up_all = rest[:, :a].reshape(width, unit_part)
        down_all = rest[:, a:b].reshape(unit_part, width)
        out_all = rest[:, b:].reshape(-1, width)
        if not fine:
            out_all = lax.dynamic_slice_in_dim(out_all, me * part, part, 0)
        weights.append((qkv_all, out_all, up_all, down_all))

    def split_heads(block):
        return block.reshape(group_count, row_count, my_heads, head_size)

    def scores_of(queries, key_rows):
        scores = (
            jnp.einsum("bqhd,bkhd->bhqk", queries, key_rows, preferred_element_type=F32)
            * score_scale
        )
        return jnp.where(same_image[:, None], scores, NEG_FILL)

    def spread(block):
        return jnp.concatenate(square.spread(block), axis=0)

    def collect(partial):
        return square.collect([partial[k * row_count : (k + 1) * row_count] for k in range(group_count)])

    hidden = tokens.astype(F32) + dot(mixing, table)
    saved = []
    for depth in range(layers):
        qkv_w, out_w, up_w, down_w = weights[depth]
        xhat_a, rstd_a = normalize(hidden)
        rows_a = spread(xhat_a.astype(BF16))
        projected = dot(rows_a, qkv_w).astype(BF16)
        queries = split_heads(projected[:, :part])
        key_rows = split_heads(projected[:, part : 2 * part])
        values = split_heads(projected[:, 2 * part :])
        scores = scores_of(queries, key_rows)
        row_max = jnp.max(scores, axis=-1, keepdims=True)
        powers = jnp.exp(scores - row_max)
        row_total = jnp.sum(powers, axis=-1, keepdims=True)
        log_total = row_max + jnp.log(row_total)
        probs = (powers / row_total).astype(BF16)
        attended = jnp.einsum("bhqk,bkhd->bqhd", probs, values, preferred_element_type=F32)
        attended = attended.reshape(group_count * row_count, part).astype(BF16)
        middle = hidden + collect(dot(attended, out_w).astype(BF16))
        xhat_m, rstd_m = normalize(middle)
        rows_m = spread(xhat_m.astype(BF16))
        pre_act = dot(rows_m, up_w)
        activated = gelu_exact(pre_act).astype(BF16)
        result = middle + collect(dot(activated, down_w).astype(BF16))
        saved.append(
            (xhat_a, rstd_a, rows_a, queries, key_rows, values, log_total, attended,
             xhat_m, rstd_m, rows_m, pre_act, activated)
        )
        hidden = result

    gradient = cotangent.astype(F32) * weight[:, None]
    shares = [None] * layers
    for depth in reversed(range(layers)):
        qkv_w, out_w, up_w, down_w = weights[depth]
        (xhat_a, rstd_a, rows_a, queries, key_rows, values, log_total, attended,
         xhat_m, rstd_m, rows_m, pre_act, activated) = saved[depth]
        d_result = spread(gradient.astype(BF16))
        grad_down = dot_t(activated, d_result).astype(BF16)
        d_activated = dot_nt(d_result, down_w)
        _, pullback = jax.vjp(gelu_exact, pre_act)
        d_pre = pullback(d_activated)[0].astype(BF16)
        grad_up = dot_t(rows_m, d_pre).astype(BF16)
        e = collect(dot_nt(d_pre, up_w).astype(BF16))
        d_middle = gradient + norm_backward(e, xhat_m, rstd_m)
        d_attn = spread(d_middle.astype(BF16))
        grad_out = dot_t(attended, d_attn).astype(BF16)
        d_attended = split_heads(dot_nt(d_attn, out_w).astype(BF16))
        probs = jnp.exp(scores_of(queries, key_rows) - log_total)
        d_values = jnp.einsum(
            "bhqk,bqhd->bkhd", probs.astype(BF16), d_attended, preferred_element_type=F32
        )
        d_probs = jnp.einsum("bqhd,bkhd->bhqk", d_attended, values, preferred_element_type=F32)
        centre = jnp.sum(probs * d_probs, axis=-1, keepdims=True)
        d_scores = (probs * (d_probs - centre)).astype(BF16)
        d_queries = (
            jnp.einsum("bhqk,bkhd->bqhd", d_scores, key_rows, preferred_element_type=F32)
            * score_scale
        )
        d_keys = (
            jnp.einsum("bhqk,bqhd->bkhd", d_scores, queries, preferred_element_type=F32)
            * score_scale
        )
        d_projected = jnp.concatenate(
            [x.astype(BF16).reshape(group_count * row_count, part) for x in (d_queries, d_keys, d_values)],
            axis=1,
        )
        grad_qkv = dot_t(rows_a, d_projected).astype(BF16)
        e = collect(dot_nt(d_projected, qkv_w).astype(BF16))
        gradient = d_middle + norm_backward(e, xhat_a, rstd_a)
        shares[depth] = (grad_qkv, grad_out, grad_up, grad_down)

    def home(term):
        return lax.psum_scatter(term, "fsdp", scatter_dimension=0, tiled=True)

    grads_qkv, grads_out, grads_up, grads_down, gains_a, gains_m = [], [], [], [], [], []
    for depth in reversed(range(layers)):
        grad_qkv, grad_out, grad_up, grad_down = shares[depth]
        rest = [
            grad_up.reshape(shard_count, -1, width),
            grad_down.reshape(shard_count, -1, width),
        ]
        if fine:
            rest.append(grad_out.reshape(shard_count, -1, width))
        else:
            full = jnp.zeros((width, width), BF16)
            full = lax.dynamic_update_slice_in_dim(full, grad_out, me * part, 0)
            rest.append(full.reshape(shard_count, -1, width))
        sizes = [x.shape[1] for x in rest]
        rest = home(jnp.concatenate(rest, axis=1))[0]
        qkv = square.gather(home(grad_qkv))
        if not fine:
            out = square.total(rest[sizes[0] + sizes[1] :])
            rest = rest[: sizes[0] + sizes[1]]
        rest = square.gather(rest)
        up = rest[:, : sizes[0]].reshape(group_count, shard_rows, shard_count, -1)
        up = up.transpose(1, 2, 0, 3).reshape(shard_rows, hidden_units).astype(F32)
        down = rest[:, sizes[0] : sizes[0] + sizes[1]].reshape(-1, width).astype(F32)
        if fine:
            pieces = rest[:, sizes[0] + sizes[1] :].reshape(2, 2, half, width)
            keep = select(core, [pieces[:, 0], pieces[:, 1]])
            give = select(core, [pieces[:, 1], pieces[:, 0]])
            got = lax.ppermute(give, "fsdp", swap_core)
            first = select(core, [keep, got])
            second = select(core, [got, keep])
            out = jnp.stack([first, second], axis=1).reshape(shard_rows, width).astype(F32)
            qkv = qkv.reshape(2, 2, shard_rows, 3 * my_heads, head_size).transpose(2, 3, 1, 0, 4)
        else:
            qkv = qkv.reshape(group_count, shard_rows, 3, part).transpose(1, 2, 0, 3)
        qkv = qkv.reshape(shard_rows, 3 * width).astype(F32)
        gains_a.append(jnp.sum(qkv * w_qkv[depth].astype(F32), axis=1))
        gains_m.append(jnp.sum(up * w_up[depth].astype(F32), axis=1))
        grads_qkv.append(qkv * gain_attn[depth].astype(F32)[:, None])
        grads_up.append(up * gain_mlp[depth].astype(F32)[:, None])
        grads_out.append(out)
        grads_down.append(down)

    high_part = gradient.astype(BF16)
    low_part = (gradient - high_part.astype(F32)).astype(BF16)
    table_term = dot_t(mixing, high_part) + dot_t(mixing, low_part)
    table_share = lax.psum_scatter(table_term.astype(BF16), "fsdp", scatter_dimension=1, tiled=True)
    d_table = square.total(table_share)
    return (
        hidden,
        gradient,
        d_table,
        jnp.stack(gains_a[::-1]),
        jnp.stack(grads_qkv[::-1]),
        jnp.stack(grads_out[::-1]),
        jnp.stack(gains_m[::-1]),
        jnp.stack(grads_up[::-1]),
        jnp.stack(grads_down[::-1]),
    )


def solution(mesh):
    in_specs = (
        P(("dp", "fsdp"), None),
        P(None, "fsdp"),
        P(),
        P(),
        P(),
        P(None, "fsdp"),
        P(None, "fsdp", None),
        P(None, "fsdp", None),
        P(None, "fsdp"),
        P(None, "fsdp", None),
        P(None, "fsdp", None),
        P(("dp", "fsdp"), None),
    )
    out_specs = (
        P(("dp", "fsdp"), None),
        P(("dp", "fsdp"), None),
        P(None, "fsdp"),
        P(None, "fsdp"),
        P(None, "fsdp", None),
        P(None, "fsdp", None),
        P(None, "fsdp"),
        P(None, "fsdp", None),
        P(None, "fsdp", None),
    )
    return jax.shard_map(local, mesh=mesh, in_specs=in_specs, out_specs=out_specs, check_vma=False)
```

```python
import math

import jax
import jax.numpy as jnp
from jax import lax
from jax.experimental import pallas as pl
from jax.experimental.pallas import tpu as pltpu
from jax.sharding import PartitionSpec as P

HEADS = 16
EPS = 1e-06
NEG_FILL = -1e30
MIX_WEIGHTS = (0.5, 0.25, 0.125, 0.125)
BF16 = jnp.bfloat16
F32 = jnp.float32


def dot(a, b):
    return jnp.dot(a, b, preferred_element_type=F32)


def dot_t(a, b):
    return lax.dot_general(a, b, (((0,), (0,)), ((), ())), preferred_element_type=F32)


def dot_nt(a, b):
    return lax.dot_general(a, b, (((1,), (1,)), ((), ())), preferred_element_type=F32)


def normalize(hidden):
    center = hidden - jnp.mean(hidden, axis=-1, keepdims=True)
    rstd = lax.rsqrt(jnp.mean(center * center, axis=-1, keepdims=True) + EPS)
    return center * rstd, rstd


def norm_backward(e, xhat, rstd):
    return rstd * (
        e
        - jnp.mean(e, axis=-1, keepdims=True)
        - xhat * jnp.mean(e * xhat, axis=-1, keepdims=True)
    )


def gelu_exact(pre_act):
    return jax.nn.gelu(pre_act, approximate=False)


class Square:
    def __init__(self):
        self.count = lax.axis_size("dp")
        self.me = lax.axis_index("dp")
        self.pairs = self.count == 4

    def owners(self):
        if self.pairs:
            return [self.me ^ k for k in range(self.count)]
        return [jnp.int32(k) for k in range(self.count)]

    def swap(self, block, k):
        return lax.ppermute(block, "dp", [(i, i ^ k) for i in range(self.count)])

    def spread(self, block):
        if self.pairs:
            return [block] + [self.swap(block, k) for k in range(1, self.count)]
        full = lax.all_gather(block, "dp")
        return [full[k] for k in range(self.count)]

    def collect(self, parts):
        if self.pairs:
            total = parts[0].astype(F32)
            for k in range(1, self.count):
                total = total + self.swap(parts[k].astype(BF16), k).astype(F32)
            return total
        stacked = jnp.stack([part.astype(BF16) for part in parts])
        return lax.psum_scatter(stacked, "dp", scatter_dimension=0, tiled=False).astype(F32)

    def gather(self, piece):
        if not self.pairs:
            return lax.all_gather(piece, "dp")
        got = [piece] + [self.swap(piece, k) for k in range(1, self.count)]
        odd = (self.me & 1) == 1
        high = (self.me & 2) == 2
        low_pair = (jnp.where(odd, got[1], got[0]), jnp.where(odd, got[0], got[1]))
        far_pair = (jnp.where(odd, got[3], got[2]), jnp.where(odd, got[2], got[3]))
        return jnp.stack(
            [
                jnp.where(high, far_pair[0], low_pair[0]),
                jnp.where(high, far_pair[1], low_pair[1]),
                jnp.where(high, low_pair[0], far_pair[0]),
                jnp.where(high, low_pair[1], far_pair[1]),
            ]
        )

    def total(self, piece):
        if not self.pairs:
            return lax.psum(piece.astype(BF16), "dp").astype(F32)
        own = piece.astype(BF16)
        got = [own.astype(F32)] + [self.swap(own, k).astype(F32) for k in range(1, self.count)]
        return (got[0] + got[1]) + (got[2] + got[3])


def select(index, choices):
    out = choices[0]
    for k in range(1, len(choices)):
        out = jnp.where(index == k, choices[k], out)
    return out


def local_general(
    tokens,
    pos_table,
    index_lo,
    index_hi,
    resolution,
    gain_attn,
    w_qkv,
    w_out,
    gain_mlp,
    w_up,
    w_down,
    cotangent,
):
    row_count, width = tokens.shape
    layers, shard_rows, _ = w_qkv.shape
    hidden_units = w_up.shape[2]
    shard_count = lax.axis_size("fsdp")
    shard = lax.axis_index("fsdp")
    square = Square()
    group_count = square.count
    me = square.me
    head_size = width // HEADS
    my_heads = HEADS // group_count
    part = my_heads * head_size
    unit_part = hidden_units // group_count
    fine = square.pairs and shard_count * 2 == HEADS
    score_scale = 1.0 / math.sqrt(head_size)
    len_low = index_lo.shape[0]
    len_high = index_hi.shape[0]

    row_ids = jnp.arange(row_count, dtype=jnp.int32)

    def layout(flag):
        length = jnp.where(flag == 1, len_high, len_low).astype(jnp.int32)
        images = jnp.where(flag == 1, row_count // len_high, row_count // len_low).astype(jnp.int32)
        live = row_ids < images * length
        return live, jnp.where(live, row_ids // length, images)

    flag = resolution[me]
    live_rows, _ = layout(flag)
    block_ids = jnp.stack([layout(resolution[owner])[1] for owner in square.owners()])
    same_image = block_ids[:, :, None] == block_ids[:, None, :]
    picked = jnp.where(flag == 1, index_hi[row_ids % len_high], index_lo[row_ids % len_low])
    table_ids = jnp.arange(len_high, dtype=jnp.int32)
    mixing = jnp.zeros((row_count, len_high), F32)
    for slot in range(4):
        mixing = mixing + MIX_WEIGHTS[slot] * (
            picked[:, slot : slot + 1] == table_ids[None, :]
        ).astype(F32)
    mixing = (mixing * live_rows[:, None].astype(F32)).astype(BF16)
    high_groups = jnp.sum(resolution)
    tokens_low = (
        (group_count - high_groups) * shard_count * (row_count // len_low) * len_low
    ).astype(F32)
    tokens_high = (high_groups * shard_count * (row_count // len_high) * len_high).astype(F32)
    token_share = 2.0 * jnp.where(flag == 1, tokens_high, tokens_low) / (tokens_low + tokens_high)
    weight = jnp.where(live_rows, token_share, 0.0)

    half = shard_rows // 4
    core = shard % 2
    swap_core = [(j, j ^ 1) for j in range(shard_count)]
    pair_side, head_side = me & 1, (me >> 1) & 1

    def qkv_part(w):
        if fine:
            view = w.reshape(shard_rows, 3 * HEADS // 4, 2, 2, head_size)
            view = select(pair_side, [view[:, :, 0], view[:, :, 1]])
            view = select(head_side, [view[:, :, 0], view[:, :, 1]])
            return view.reshape(shard_rows, 3 * part)
        view = w.reshape(shard_rows, 3, group_count, part)
        return lax.dynamic_index_in_dim(view, me, 2, keepdims=False).reshape(shard_rows, 3 * part)

    def up_part(w):
        view = w.reshape(shard_rows, shard_count, group_count, unit_part // shard_count)
        return lax.dynamic_index_in_dim(view, me, 2, keepdims=False).reshape(shard_rows, unit_part)

    def down_part(w):
        rows = unit_part // shard_count
        return lax.dynamic_slice_in_dim(w, me * rows, rows, 0)

    def out_part(w):
        if fine:
            view = w.reshape(2, 2, half, width)
            mine = select(head_side, [view[0], view[1]])
            keep = select(core, [mine[0], mine[1]])
            give = select(core, [mine[1], mine[0]])
            got = lax.ppermute(give, "fsdp", swap_core)
            return jnp.where(core == pair_side, keep, got)
        return w

    def fetch(piece):
        return lax.all_gather(piece, "fsdp", axis=0, tiled=False)

    weights = []
    table = lax.all_gather(pos_table, "fsdp", axis=1, tiled=True)
    for depth in range(layers):
        gain_a = gain_attn[depth].astype(F32)[:, None]
        gain_m = gain_mlp[depth].astype(F32)[:, None]
        qkv = (qkv_part(w_qkv[depth]).astype(F32) * gain_a).astype(BF16)
        up = (up_part(w_up[depth]).astype(F32) * gain_m).astype(BF16)
        down = down_part(w_down[depth])
        out = out_part(w_out[depth])
        qkv_all = fetch(qkv).reshape(width, 3 * part)
        a = up.size // width
        b = a + down.shape[0]
        rest = fetch(jnp.concatenate([up.reshape(a, width), down, out], axis=0))
        up_all = rest[:, :a].reshape(width, unit_part)
        down_all = rest[:, a:b].reshape(unit_part, width)
        out_all = rest[:, b:].reshape(-1, width)
        if not fine:
            out_all = lax.dynamic_slice_in_dim(out_all, me * part, part, 0)
        weights.append((qkv_all, out_all, up_all, down_all))

    def split_heads(block):
        return block.reshape(group_count, row_count, my_heads, head_size)

    def scores_of(queries, key_rows):
        scores = (
            jnp.einsum("bqhd,bkhd->bhqk", queries, key_rows, preferred_element_type=F32)
            * score_scale
        )
        return jnp.where(same_image[:, None], scores, NEG_FILL)

    def spread(block):
        return jnp.concatenate(square.spread(block), axis=0)

    def collect(partial):
        return square.collect([partial[k * row_count : (k + 1) * row_count] for k in range(group_count)])

    hidden = tokens.astype(F32) + dot(mixing, table)
    saved = []
    for depth in range(layers):
        qkv_w, out_w, up_w, down_w = weights[depth]
        xhat_a, rstd_a = normalize(hidden)
        rows_a = spread(xhat_a.astype(BF16))
        projected = dot(rows_a, qkv_w).astype(BF16)
        queries = split_heads(projected[:, :part])
        key_rows = split_heads(projected[:, part : 2 * part])
        values = split_heads(projected[:, 2 * part :])
        scores = scores_of(queries, key_rows)
        row_max = jnp.max(scores, axis=-1, keepdims=True)
        powers = jnp.exp(scores - row_max)
        row_total = jnp.sum(powers, axis=-1, keepdims=True)
        log_total = row_max + jnp.log(row_total)
        probs = (powers / row_total).astype(BF16)
        attended = jnp.einsum("bhqk,bkhd->bqhd", probs, values, preferred_element_type=F32)
        attended = attended.reshape(group_count * row_count, part).astype(BF16)
        middle = hidden + collect(dot(attended, out_w).astype(BF16))
        xhat_m, rstd_m = normalize(middle)
        rows_m = spread(xhat_m.astype(BF16))
        pre_act = dot(rows_m, up_w)
        activated = gelu_exact(pre_act).astype(BF16)
        result = middle + collect(dot(activated, down_w).astype(BF16))
        saved.append(
            (xhat_a, rstd_a, rows_a, queries, key_rows, values, log_total, attended,
             xhat_m, rstd_m, rows_m, pre_act, activated)
        )
        hidden = result

    gradient = cotangent.astype(F32) * weight[:, None]
    shares = [None] * layers
    for depth in reversed(range(layers)):
        qkv_w, out_w, up_w, down_w = weights[depth]
        (xhat_a, rstd_a, rows_a, queries, key_rows, values, log_total, attended,
         xhat_m, rstd_m, rows_m, pre_act, activated) = saved[depth]
        d_result = spread(gradient.astype(BF16))
        grad_down = dot_t(activated, d_result).astype(BF16)
        d_activated = dot_nt(d_result, down_w)
        _, pullback = jax.vjp(gelu_exact, pre_act)
        d_pre = pullback(d_activated)[0].astype(BF16)
        grad_up = dot_t(rows_m, d_pre).astype(BF16)
        e = collect(dot_nt(d_pre, up_w).astype(BF16))
        d_middle = gradient + norm_backward(e, xhat_m, rstd_m)
        d_attn = spread(d_middle.astype(BF16))
        grad_out = dot_t(attended, d_attn).astype(BF16)
        d_attended = split_heads(dot_nt(d_attn, out_w).astype(BF16))
        probs = jnp.exp(scores_of(queries, key_rows) - log_total)
        d_values = jnp.einsum(
            "bhqk,bqhd->bkhd", probs.astype(BF16), d_attended, preferred_element_type=F32
        )
        d_probs = jnp.einsum("bqhd,bkhd->bhqk", d_attended, values, preferred_element_type=F32)
        centre = jnp.sum(probs * d_probs, axis=-1, keepdims=True)
        d_scores = (probs * (d_probs - centre)).astype(BF16)
        d_queries = (
            jnp.einsum("bhqk,bkhd->bqhd", d_scores, key_rows, preferred_element_type=F32)
            * score_scale
        )
        d_keys = (
            jnp.einsum("bhqk,bqhd->bkhd", d_scores, queries, preferred_element_type=F32)
            * score_scale
        )
        d_projected = jnp.concatenate(
            [x.astype(BF16).reshape(group_count * row_count, part) for x in (d_queries, d_keys, d_values)],
            axis=1,
        )
        grad_qkv = dot_t(rows_a, d_projected).astype(BF16)
        e = collect(dot_nt(d_projected, qkv_w).astype(BF16))
        gradient = d_middle + norm_backward(e, xhat_a, rstd_a)
        shares[depth] = (grad_qkv, grad_out, grad_up, grad_down)

    def home(term):
        return lax.psum_scatter(term, "fsdp", scatter_dimension=0, tiled=True)

    grads_qkv, grads_out, grads_up, grads_down, gains_a, gains_m = [], [], [], [], [], []
    for depth in reversed(range(layers)):
        grad_qkv, grad_out, grad_up, grad_down = shares[depth]
        rest = [
            grad_up.reshape(shard_count, -1, width),
            grad_down.reshape(shard_count, -1, width),
        ]
        if fine:
            rest.append(grad_out.reshape(shard_count, -1, width))
        else:
            full = jnp.zeros((width, width), BF16)
            full = lax.dynamic_update_slice_in_dim(full, grad_out, me * part, 0)
            rest.append(full.reshape(shard_count, -1, width))
        sizes = [x.shape[1] for x in rest]
        rest = home(jnp.concatenate(rest, axis=1))[0]
        qkv = square.gather(home(grad_qkv))
        if not fine:
            out = square.total(rest[sizes[0] + sizes[1] :])
            rest = rest[: sizes[0] + sizes[1]]
        rest = square.gather(rest)
        up = rest[:, : sizes[0]].reshape(group_count, shard_rows, shard_count, -1)
        up = up.transpose(1, 2, 0, 3).reshape(shard_rows, hidden_units).astype(F32)
        down = rest[:, sizes[0] : sizes[0] + sizes[1]].reshape(-1, width).astype(F32)
        if fine:
            pieces = rest[:, sizes[0] + sizes[1] :].reshape(2, 2, half, width)
            keep = select(core, [pieces[:, 0], pieces[:, 1]])
            give = select(core, [pieces[:, 1], pieces[:, 0]])
            got = lax.ppermute(give, "fsdp", swap_core)
            first = select(core, [keep, got])
            second = select(core, [got, keep])
            out = jnp.stack([first, second], axis=1).reshape(shard_rows, width).astype(F32)
            qkv = qkv.reshape(2, 2, shard_rows, 3 * my_heads, head_size).transpose(2, 3, 1, 0, 4)
        else:
            qkv = qkv.reshape(group_count, shard_rows, 3, part).transpose(1, 2, 0, 3)
        qkv = qkv.reshape(shard_rows, 3 * width).astype(F32)
        gains_a.append(jnp.sum(qkv * w_qkv[depth].astype(F32), axis=1))
        gains_m.append(jnp.sum(up * w_up[depth].astype(F32), axis=1))
        grads_qkv.append(qkv * gain_attn[depth].astype(F32)[:, None])
        grads_up.append(up * gain_mlp[depth].astype(F32)[:, None])
        grads_out.append(out)
        grads_down.append(down)

    high_part = gradient.astype(BF16)
    low_part = (gradient - high_part.astype(F32)).astype(BF16)
    table_term = dot_t(mixing, high_part) + dot_t(mixing, low_part)
    table_share = lax.psum_scatter(table_term.astype(BF16), "fsdp", scatter_dimension=1, tiled=True)
    d_table = square.total(table_share)
    return (
        hidden,
        gradient,
        d_table,
        jnp.stack(gains_a[::-1]),
        jnp.stack(grads_qkv[::-1]),
        jnp.stack(grads_out[::-1]),
        jnp.stack(gains_m[::-1]),
        jnp.stack(grads_up[::-1]),
        jnp.stack(grads_down[::-1]),
    )


VMEM = pltpu.VMEM
LANES = 128


def whole(shape):
    return pl.BlockSpec(tuple(shape), lambda *_: (0,) * len(shape))


def scalars():
    return pl.BlockSpec(memory_space=pltpu.SMEM)


def call(body, outs, args, specs=None, scratch=(), flops=0, reads=0, aliases=None, out_specs=None, limit=40):
    specs = [whole(a.shape) if s is None else s for a, s in zip(args, specs or [None] * len(args))]
    out_shape = [jax.ShapeDtypeStruct(shape, dtype) for shape, dtype in outs]
    moved = sum(math.prod(s) * jnp.dtype(d).itemsize for s, d in outs) + reads
    return pl.pallas_call(
        body,
        grid=(1,),
        in_specs=specs,
        out_specs=out_specs or [whole(shape) for shape, _ in outs],
        out_shape=out_shape,
        scratch_shapes=list(scratch),
        input_output_aliases=aliases or {},
        cost_estimate=pl.CostEstimate(flops=int(flops), bytes_accessed=int(moved), transcendentals=0),
        compiler_params=pltpu.CompilerParams(vmem_limit_bytes=limit << 20),
    )(*args)


def diagonal(gain_row):
    r = lax.broadcasted_iota(jnp.int32, (LANES, LANES), 0)
    c = lax.broadcasted_iota(jnp.int32, (LANES, LANES), 1)
    return jnp.where(r == c, jnp.broadcast_to(gain_row.astype(F32), (LANES, LANES)), 0.0)


def lane_low(rows):
    return lax.broadcasted_iota(jnp.int32, (rows, LANES), 1) < LANES // 2


def lane_swap(block):
    return jnp.concatenate([block[:, LANES // 2 :], block[:, : LANES // 2]], axis=1)


def prepare_attention(me_ref, w_ref, gain_ref, out_ref, packed_ref):
    side, second = me_ref[0] & 1, me_ref[0] >> 1
    diag = diagonal(gain_ref[0]).astype(BF16)
    rows = w_ref.shape[1]
    low = lane_low(rows)

    def head(t):
        chunk = pl.multiple_of(((t // 4) * 8 + 2 * (t % 4) + side) * LANES, LANES)
        got = dot(diag, w_ref[0, :, pl.ds(chunk, LANES)])
        turned = lane_swap(got)
        if t % 2 == 0:
            return jnp.where(second == 0, got, turned)
        return jnp.where(second == 0, turned, got)

    for u in range(6):
        pair = jnp.where(low, head(2 * u), head(2 * u + 1))
        packed_ref[:, u * LANES : (u + 1) * LANES] = pair.astype(BF16)
    for c in range(4):
        packed_ref[c * 32 : (c + 1) * 32, 768:1024] = out_ref[:, c * 256 : (c + 1) * 256]


def prepare_mlp(me_ref, up_ref, gain_ref, down_ref, packed_ref):
    me = me_ref[0]
    diag = diagonal(gain_ref[0]).astype(BF16)
    for j in range(8):
        chunk = pl.multiple_of((j * 4 + me) * LANES, LANES)
        packed_ref[:LANES, j * LANES : (j + 1) * LANES] = dot(
            diag, up_ref[0, :, pl.ds(chunk, LANES)]
        ).astype(BF16)
    packed_ref[LANES:, :] = down_ref[0, pl.ds(pl.multiple_of(me * LANES, LANES), LANES), :]


def image_numbers(rows, flag, lens):
    counts = [sum((rows >= t * n).astype(jnp.int32) for t in range(1, most + 1)) for n, most in lens]
    return jnp.where(flag == 1, counts[1], counts[0])


def make_mixing(flag_ref, low_ref, high_ref, mixing_ref, *, lens):
    rows = mixing_ref.shape[0]
    flag = flag_ref[0]

    def spread_rows(index_ref, length, most):
        count = index_ref.shape[0]
        columns = lax.broadcasted_iota(jnp.int32, (count, mixing_ref.shape[1]), 1)
        mix = jnp.zeros((count, mixing_ref.shape[1]), F32)
        for slot in range(4):
            mix = mix + MIX_WEIGHTS[slot] * (index_ref[:, slot : slot + 1] == columns).astype(F32)
        r = lax.broadcasted_iota(jnp.int32, (rows, count), 0)
        c = lax.broadcasted_iota(jnp.int32, (rows, count), 1)
        image = sum((r >= t * length).astype(jnp.int32) for t in range(1, most + 1))
        pick = ((r - image * length == c) & (r < most * length)).astype(BF16)
        return dot(pick, mix.astype(BF16))

    low = spread_rows(low_ref, *lens[0])
    high = spread_rows(high_ref, *lens[1])
    mixing_ref[...] = jnp.where(flag == 1, high, low).astype(BF16)


def write_norm(hidden, xhat_ref, rstd_ref):
    xhat, rstd = normalize(hidden)
    xhat_ref[...] = xhat.astype(BF16)
    rstd_ref[...] = jnp.broadcast_to(rstd, rstd_ref.shape)


def embed(z_ref, tokens_ref, mixing_ref, t0, t1, t2, t3, hidden_ref, xhat_ref, rstd_ref, table):
    z = z_ref[0]
    for k, piece in enumerate((t0, t1, t2, t3)):
        table[:, pl.ds(pl.multiple_of((z ^ k) * 256, 256), 256)] = piece[...].astype(F32)
    hidden = tokens_ref[...].astype(F32) + dot(mixing_ref[...], table[...].astype(BF16))
    hidden_ref[...] = hidden
    write_norm(hidden, xhat_ref, rstd_ref)


def added(p0, r1, r2, r3):
    return (p0[...].astype(F32) + r1[...].astype(F32)) + (r2[...].astype(F32) + r3[...].astype(F32))


def add_norm(h_ref, p0, r1, r2, r3, middle_ref, xhat_ref, rstd_ref):
    middle = h_ref[...] + added(p0, r1, r2, r3)
    middle_ref[...] = middle
    write_norm(middle, xhat_ref, rstd_ref)


def add_norm_backward(g_ref, p0, r1, r2, r3, xhat_ref, rstd_ref, d_ref, low_ref):
    e = added(p0, r1, r2, r3)
    d = g_ref[...] + norm_backward(e, xhat_ref[...].astype(F32), rstd_ref[:, :1])
    d_ref[...] = d
    low_ref[...] = d.astype(BF16)


def out_chunk(packed_ref, c):
    return packed_ref[:, c * 32 : (c + 1) * 32, 768:1024].reshape(256, 256)


def attention_forward(flag_ref, x_ref, w_ref, proj_ref, att_ref, p_ref, *, lens):
    rows = x_ref.shape[0]
    flag = flag_ref[0]
    width = x_ref.shape[1]
    mask = image_numbers(lax.broadcasted_iota(jnp.int32, (rows, 1), 0), flag, lens) == image_numbers(
        lax.broadcasted_iota(jnp.int32, (1, rows), 1), flag, lens
    )
    for c in range(3):
        w = w_ref[:, :, c * 256 : (c + 1) * 256].reshape(width, 256)
        proj_ref[:, c * 256 : (c + 1) * 256] = dot(x_ref[...], w).astype(BF16)
    low = lane_low(rows)
    zero = jnp.zeros((), BF16)
    for u in range(2):
        q = proj_ref[:, u * LANES : (u + 1) * LANES] * jnp.asarray(0.125, BF16)
        k = proj_ref[:, 256 + u * LANES : 256 + (u + 1) * LANES]
        v = proj_ref[:, 512 + u * LANES : 512 + (u + 1) * LANES]
        total = None
        for keep in (low, ~low):
            s = dot_nt(jnp.where(keep, q, zero), k)
            s = jnp.where(mask, s, NEG_FILL)
            powers = jnp.exp(s - jnp.max(s, axis=-1, keepdims=True))
            probs = powers * (1.0 / jnp.sum(powers, axis=-1, keepdims=True))
            o = dot(probs.astype(BF16), jnp.where(keep, v, zero))
            total = o if total is None else total + o
        att_ref[:, u * LANES : (u + 1) * LANES] = total.astype(BF16)
    for c in range(4):
        p_ref[:, c * 256 : (c + 1) * 256] = dot(att_ref[...], out_chunk(w_ref, c)).astype(BF16)


def attention_backward(flag_ref, d_ref, proj_ref, w_ref, dproj_ref, p_ref, *, lens):
    rows, width = d_ref.shape
    flag = flag_ref[0]
    mask = image_numbers(lax.broadcasted_iota(jnp.int32, (rows, 1), 0), flag, lens) == image_numbers(
        lax.broadcasted_iota(jnp.int32, (1, rows), 1), flag, lens
    )
    d_o = sum(dot_nt(d_ref[:, c * 256 : (c + 1) * 256], out_chunk(w_ref, c)) for c in range(4))
    d_o = d_o.astype(BF16)
    low = lane_low(rows)
    zero = jnp.zeros((), BF16)
    scale = jnp.asarray(0.125, BF16)
    for u in range(2):
        q = proj_ref[:, u * LANES : (u + 1) * LANES] * scale
        k = proj_ref[:, 256 + u * LANES : 256 + (u + 1) * LANES]
        v = proj_ref[:, 512 + u * LANES : 512 + (u + 1) * LANES]
        g = d_o[:, u * LANES : (u + 1) * LANES]
        dq = dk = dv = None
        for keep in (low, ~low):
            k_own = jnp.where(keep, k, zero)
            s = jnp.where(mask, dot_nt(k_own, q), NEG_FILL)
            powers = jnp.exp(s - jnp.max(s, axis=0, keepdims=True))
            probs = powers * (1.0 / jnp.sum(powers, axis=0, keepdims=True))
            d_probs = dot_nt(jnp.where(keep, v, zero), g)
            centre = jnp.sum(probs * d_probs, axis=0, keepdims=True)
            d_scores = (probs * (d_probs - centre)).astype(BF16)
            terms = (
                dot_t(d_scores, k_own),
                dot(d_scores, jnp.where(keep, q, zero)),
                dot(probs.astype(BF16), jnp.where(keep, g, zero)),
            )
            dq, dk, dv = terms if dq is None else (dq + terms[0], dk + terms[1], dv + terms[2])
        dproj_ref[:, u * LANES : (u + 1) * LANES] = (dq * 0.125).astype(BF16)
        dproj_ref[:, 256 + u * LANES : 256 + (u + 1) * LANES] = dk.astype(BF16)
        dproj_ref[:, 512 + u * LANES : 512 + (u + 1) * LANES] = dv.astype(BF16)
    total = None
    for c in range(3):
        w = w_ref[:, :, c * 256 : (c + 1) * 256].reshape(width, 256)
        term = dot_nt(dproj_ref[:, c * 256 : (c + 1) * 256], w)
        total = term if total is None else total + term
    p_ref[...] = total.astype(BF16)


def gelu_parts(pre):
    upto = 0.5 * (1.0 + lax.erf(pre * math.sqrt(0.5)))
    density = jnp.exp(-0.5 * pre * pre) * (1.0 / math.sqrt(2.0 * math.pi))
    return pre * upto, upto + pre * density


def mlp_forward(x_ref, up_ref, down_ref, act_ref, slope_ref, p_ref):
    width = x_ref.shape[1]
    for c in range(4):
        cols = slice(c * 256, (c + 1) * 256)
        act, slope = gelu_parts(dot(x_ref[...], up_ref[:, :, cols].reshape(width, 256)))
        act_ref[:, cols] = act.astype(BF16)
        slope_ref[:, cols] = slope.astype(BF16)
    p_ref[...] = dot(act_ref[...], down_ref[...].reshape(width, width)).astype(BF16)


def mlp_backward(d_ref, slope_ref, up_ref, down_ref, dpre_ref, p_ref):
    width = d_ref.shape[1]
    for c in range(4):
        cols = slice(c * 256, (c + 1) * 256)
        d_act = dot_nt(d_ref[...], down_ref[2 * c : 2 * c + 2].reshape(256, width))
        dpre_ref[:, cols] = (d_act * slope_ref[:, cols].astype(F32)).astype(BF16)
    p_ref[...] = dot_nt(dpre_ref[...], up_ref[...].reshape(width, width)).astype(BF16)


def mlp_both(x_ref, d_ref, up_ref, down_ref, act_ref, dpre_ref, p_ref, back_ref):
    width = x_ref.shape[1]
    for c in range(4):
        cols = slice(c * 256, (c + 1) * 256)
        act, slope = gelu_parts(dot(x_ref[...], up_ref[:, :, cols].reshape(width, 256)))
        act_ref[:, cols] = act.astype(BF16)
        d_act = dot_nt(d_ref[...], down_ref[2 * c : 2 * c + 2].reshape(256, width))
        dpre_ref[:, cols] = (d_act * slope).astype(BF16)
    back_ref[...] = dot_nt(dpre_ref[...], up_ref[...].reshape(width, width)).astype(BF16)
    p_ref[...] = dot(act_ref[...], down_ref[...].reshape(width, width)).astype(BF16)


def grads_mlp(*refs):
    x, dpre, act, d, out_ref = refs[:4], refs[4:8], refs[8:12], refs[12:16], refs[16]
    for half, (left, right) in enumerate(((x, dpre), (act, d))):
        for j in range(8):
            rows = slice(j * LANES, (j + 1) * LANES)
            total = None
            for a, b in zip(left, right):
                term = dot_t(a[:, rows], b[...])
                total = term if total is None else total + term
            out_ref[j, half * LANES : (half + 1) * LANES, :] = total.astype(BF16)


def grads_attention(*refs):
    x, dproj, att, d, out_ref = refs[:4], refs[4:8], refs[8:12], refs[12:16], refs[16]
    for j in range(8):
        rows = slice(j * LANES, (j + 1) * LANES)
        total = None
        for a, b in zip(x, dproj):
            term = dot_t(a[:, rows], b[...])
            total = term if total is None else total + term
        out_ref[j, :, :768] = total.astype(BF16)
    for c in range(4):
        cols = slice(c * 256, (c + 1) * 256)
        total = None
        for a, b in zip(att, d):
            term = dot_t(a[...], b[:, cols])
            total = term if total is None else total + term
        out_ref[:, c * 32 : (c + 1) * 32, 768:1024] = total.astype(BF16).reshape(8, 32, 256)


def finish_mlp(me_ref, g0, g1, g2, g3, up_ref, gain_ref, *rest):
    dup_ref, ddown_ref, dgain_ref = rest[-3:]
    me = me_ref[0]
    diag = diagonal(gain_ref[0])
    total = jnp.zeros((LANES, LANES), F32)
    column = jnp.sum(diag, axis=1, keepdims=True)
    for k, piece in enumerate((g0, g1, g2, g3)):
        owner = me ^ k
        ddown_ref[0, pl.ds(pl.multiple_of(owner * LANES, LANES), LANES), :] = piece[LANES:, :].astype(F32)
    for i in range(4):
        got = jnp.where(
            me == i, g0[:LANES, :], jnp.where(me == i ^ 1, g1[:LANES, :], jnp.where(me == i ^ 2, g2[:LANES, :], g3[:LANES, :]))
        ).astype(F32)
        for j in range(8):
            cols = slice((j * 4 + i) * LANES, (j * 4 + i + 1) * LANES)
            part = got[:, j * LANES : (j + 1) * LANES]
            dup_ref[0, :, cols] = part * column
            total = total + part * up_ref[0, :, cols].astype(F32)
    dgain_ref[0] = jnp.sum(total.T, axis=0, keepdims=True)


def finish_attention(me_ref, g0, g1, g2, g3, w_ref, gain_ref, out_ref, *rest):
    dqkv_ref, dout_ref, dgain_ref = rest[-3:]
    me = me_ref[0]
    column = jnp.sum(diagonal(gain_ref[0]), axis=1, keepdims=True)
    total = jnp.zeros((LANES, LANES), F32)
    low = lane_low(LANES)
    owned = []
    for i in range(4):
        owned.append(
            jnp.where(
                me == i, g0[:, :768], jnp.where(me == i ^ 1, g1[:, :768], jnp.where(me == i ^ 2, g2[:, :768], g3[:, :768]))
            ).astype(F32)
        )
    for t in range(12):
        u = t // 2
        for side in range(2):
            first = owned[side][:, u * LANES : (u + 1) * LANES]
            second = owned[side + 2][:, u * LANES : (u + 1) * LANES]
            if t % 2 == 0:
                part = jnp.where(low, first, lane_swap(second))
            else:
                part = jnp.where(low, lane_swap(first), second)
            chunk = (t // 4) * 8 + 2 * (t % 4) + side
            cols = slice(chunk * LANES, (chunk + 1) * LANES)
            dqkv_ref[0, :, cols] = part * column
            total = total + part * w_ref[0, :, cols].astype(F32)
    dgain_ref[0] = jnp.sum(total.T, axis=0, keepdims=True)
    for h in range(4):
        for c in range(4):
            dout_ref[0, h * 32 : (h + 1) * 32, c * 256 : (c + 1) * 256] = out_ref[
                h, c * 32 : (c + 1) * 32, :
            ].astype(F32)


def local_fast(
    tokens,
    pos_table,
    index_lo,
    index_hi,
    resolution,
    gain_attn,
    w_qkv,
    w_out,
    gain_mlp,
    w_up,
    w_down,
    cotangent,
):
    rows, width = tokens.shape
    layers = w_qkv.shape[0]
    square = Square()
    me = square.me
    me1 = me.reshape(1).astype(jnp.int32)
    shard = lax.axis_index("fsdp")
    core, deep = shard % 2, shard // 2
    deep1 = deep.reshape(1).astype(jnp.int32)
    len_low, len_high = index_lo.shape[0], index_hi.shape[0]
    lens = ((len_low, rows // len_low), (len_high, rows // len_high))
    block = (rows, width)
    blocks = range(4)

    def over_fsdp(x, k):
        return lax.ppermute(x, "fsdp", [(j, j ^ k) for j in range(8)])

    def layer_of(array, depth):
        return pl.BlockSpec((1,) + array.shape[1:], lambda *_: (depth,) + (0,) * (array.ndim - 1))

    pair_side, head_side = me & 1, me >> 1
    view = w_out.reshape(layers, 2, 2, 32, width)
    mine = jnp.where(head_side == 1, view[:, 1], view[:, 0])
    keep = jnp.where(core == 1, mine[:, 1], mine[:, 0])
    give = jnp.where(core == 1, mine[:, 0], mine[:, 1])
    out_pieces = jnp.where(core == pair_side, keep, over_fsdp(give, 1))
    gains_a = gain_attn.reshape(layers, 1, LANES)
    gains_m = gain_mlp.reshape(layers, 1, LANES)
    attn_w, mlp_w = [], []
    for depth in range(layers):
        (packed,) = call(
            prepare_attention,
            [((LANES, width), BF16)],
            [me1, w_qkv, gains_a, out_pieces[depth]],
            [scalars(), layer_of(w_qkv, depth), layer_of(gains_a, depth), None],
        )
        attn_w.append(lax.all_gather(packed, "fsdp", axis=0, tiled=False))
        (packed,) = call(
            prepare_mlp,
            [((2 * LANES, width), BF16)],
            [me1, w_up, gains_m, w_down],
            [scalars(), layer_of(w_up, depth), layer_of(gains_m, depth), layer_of(w_down, depth)],
        )
        mlp_w.append(lax.all_gather(packed, "fsdp", axis=0, tiled=False))
    up_spec = pl.BlockSpec((8, LANES, width), lambda *_: (0, 0, 0))
    down_spec = pl.BlockSpec((8, LANES, width), lambda *_: (0, 1, 0))

    flag = resolution[me]
    flag1 = flag.reshape(1)
    flags = [resolution[owner].reshape(1) for owner in square.owners()]
    shard_count, group_count = 8, resolution.shape[0]
    high_groups = jnp.sum(resolution)
    tokens_low = ((group_count - high_groups) * shard_count * lens[0][1] * len_low).astype(F32)
    tokens_high = (high_groups * shard_count * lens[1][1] * len_high).astype(F32)
    token_share = 2.0 * jnp.where(flag == 1, tokens_high, tokens_low) / (tokens_low + tokens_high)
    live = jnp.where(flag == 1, lens[1][1] * len_high, lens[0][1] * len_low)
    weight = jnp.where(jnp.arange(rows, dtype=jnp.int32) < live, token_share, 0.0)
    gradient = cotangent.astype(F32) * weight[:, None]

    other = over_fsdp(pos_table, 1)
    pair = jnp.concatenate(
        [jnp.where(core == 0, pos_table, other), jnp.where(core == 0, other, pos_table)], axis=1
    )
    pieces = [pair] + [over_fsdp(pair, 2 * k) for k in range(1, 4)]
    (mixing,) = call(
        lambda *refs: make_mixing(*refs, lens=lens),
        [((rows, len_high), BF16)],
        [flag1, index_lo, index_hi],
        [scalars(), None, None],
    )
    hidden, xhat, rstd = call(
        embed,
        [(block, F32), (block, BF16), ((rows, LANES), F32)],
        [deep1, tokens, mixing] + pieces,
        [scalars()] + [None] * 6,
        scratch=[VMEM((len_high, width), F32)],
        flops=2 * rows * len_high * width,
    )

    def collect(parts):
        return [parts[0]] + [square.swap(parts[k], k) for k in range(1, 4)]

    d_top = square.spread(gradient.astype(BF16))
    saved = []
    for depth in range(layers):
        a_w, m_w = attn_w[depth], mlp_w[depth]
        xs = square.spread(xhat)
        got = [
            call(
                lambda *refs: attention_forward(*refs, lens=lens),
                [((rows, 768), BF16), ((rows, 256), BF16), (block, BF16)],
                [flags[k], xs[k], a_w],
                [scalars(), None, None],
                flops=2 * rows * width * 1024,
                reads=2 * a_w.size,
            )
            for k in blocks
        ]
        projs, atts = [g[0] for g in got], [g[1] for g in got]
        middle, xhat_m, rstd_m = call(
            add_norm,
            [(block, F32), (block, BF16), ((rows, LANES), F32)],
            [hidden] + collect([g[2] for g in got]),
            reads=4 * rows * width,
        )
        ms = square.spread(xhat_m)
        last = depth == layers - 1
        if last:
            got = [
                call(
                    mlp_both,
                    [(block, BF16)] * 4,
                    [ms[k], d_top[k], m_w, m_w],
                    [None, None, up_spec, down_spec],
                    flops=8 * rows * width * width,
                    reads=2 * m_w.size,
                )
                for k in blocks
            ]
            acts, dpres, ps, backs = ([g[t] for g in got] for t in range(4))
            slopes = None
        else:
            got = [
                call(
                    mlp_forward,
                    [(block, BF16)] * 3,
                    [ms[k], m_w, m_w],
                    [None, up_spec, down_spec],
                    flops=4 * rows * width * width,
                    reads=2 * m_w.size,
                )
                for k in blocks
            ]
            acts, slopes, ps = ([g[t] for g in got] for t in range(3))
            dpres = backs = None
        saved.append((xhat, rstd, xs, projs, atts, xhat_m, rstd_m, ms, acts, slopes))
        if last:
            output_parts = ps
        else:
            hidden, xhat, rstd = call(
                add_norm,
                [(block, F32), (block, BF16), ((rows, LANES), F32)],
                [middle] + collect(ps),
                reads=4 * rows * width,
            )

    homes_m, homes_a = [None] * layers, [None] * layers
    held = None
    output = None
    for depth in reversed(range(layers)):
        a_w, m_w = attn_w[depth], mlp_w[depth]
        xhat, rstd, xs, projs, atts, xhat_m, rstd_m, ms, acts, slopes = saved[depth]
        if depth == layers - 1:
            ds = d_top
        else:
            ds = square.spread(low)
            got = [
                call(
                    mlp_backward,
                    [(block, BF16)] * 2,
                    [ds[k], slopes[k], m_w, m_w],
                    [None, None, up_spec, down_spec],
                    flops=4 * rows * width * width,
                    reads=2 * m_w.size,
                )
                for k in blocks
            ]
            dpres, backs = ([g[t] for g in got] for t in range(2))
        es = collect(backs)
        (term,) = call(
            grads_mlp,
            [((8, 2 * LANES, width), BF16)],
            list(ms) + list(dpres) + list(acts) + list(ds),
            flops=16 * rows * width * width,
        )
        es, term = lax.optimization_barrier((es, term))
        homes_m[depth] = lax.psum_scatter(term, "fsdp", scatter_dimension=0, tiled=False)
        if depth == layers - 1:
            outs = collect(output_parts)
            output = middle + ((outs[0].astype(F32) + outs[1].astype(F32)) + (outs[2].astype(F32) + outs[3].astype(F32)))
        else:
            es, homes_m[depth + 1] = lax.optimization_barrier((es, homes_m[depth + 1]))
        d_middle, low = call(
            add_norm_backward,
            [(block, F32), (block, BF16)],
            [gradient] + es + [xhat_m, rstd_m],
            reads=8 * rows * width,
        )
        ds = square.spread(low)
        got = [
            call(
                lambda *refs: attention_backward(*refs, lens=lens),
                [((rows, 768), BF16), (block, BF16)],
                [flags[k], ds[k], projs[k], a_w],
                [scalars(), None, None, None],
                flops=2 * rows * width * 1536,
                reads=2 * a_w.size,
            )
            for k in blocks
        ]
        dprojs = [g[0] for g in got]
        es = collect([g[1] for g in got])
        (term,) = call(
            grads_attention,
            [((8, LANES, width), BF16)],
            list(xs) + dprojs + atts + list(ds),
            flops=8 * rows * width * width,
        )
        es, term = lax.optimization_barrier((es, term))
        homes_a[depth] = lax.psum_scatter(term, "fsdp", scatter_dimension=0, tiled=False)
        if depth < layers - 1:
            es, homes_a[depth + 1] = lax.optimization_barrier((es, homes_a[depth + 1]))
        gradient, low = call(
            add_norm_backward,
            [(block, F32), (block, BF16)],
            [d_middle] + es + [xhat, rstd],
            reads=8 * rows * width,
        )

    rest = (gradient - low.astype(F32)).astype(BF16)
    table_term = (dot_t(mixing, low) + dot_t(mixing, rest)).astype(BF16).reshape(len_high, 4, 256)
    table_term = table_term.transpose(1, 0, 2)
    mine = lax.dynamic_index_in_dim(table_term, deep, 0, keepdims=False).astype(F32)
    for k in range(1, 4):
        sent = lax.dynamic_index_in_dim(table_term, deep ^ k, 0, keepdims=False)
        mine = mine + over_fsdp(sent, 2 * k).astype(F32)
    mine = mine.astype(BF16)
    keep = jnp.where(core == 0, mine[:, :LANES], mine[:, LANES:])
    give = jnp.where(core == 0, mine[:, LANES:], mine[:, :LANES])
    d_table = square.total(keep.astype(F32) + over_fsdp(give, 1).astype(F32))

    big = [None] * 6
    for depth in reversed(range(layers)):
        pieces = square.spread(homes_m[depth])
        prior = big[3:]
        names = [(w_up.shape, F32), (w_down.shape, F32), (gains_m.shape, F32)]
        args = [me1] + pieces + [w_up, gains_m]
        specs = [scalars()] + [None] * 4 + [layer_of(w_up, depth), layer_of(gains_m, depth)]
        extra = [] if prior[0] is None else prior
        big[3:] = call(
            finish_mlp,
            names,
            args + extra,
            specs + [pl.BlockSpec(memory_space=pl.ANY)] * len(extra),
            aliases={len(args) + t: t for t in range(len(extra))},
            out_specs=[layer_of(jax.ShapeDtypeStruct(s, d), depth) for s, d in names],
        )
        pieces = square.spread(homes_a[depth])
        packed = [piece[:, 768:1024] for piece in pieces]
        odd_me = (me & 1) == 1
        even = [jnp.where(odd_me, packed[1], packed[0]), jnp.where(odd_me, packed[3], packed[2])]
        odd = [jnp.where(odd_me, packed[0], packed[1]), jnp.where(odd_me, packed[2], packed[3])]
        keep = [jnp.where(core == 0, a, b) for a, b in zip(even, odd)]
        give = jnp.stack([jnp.where(core == 0, b, a) for a, b in zip(even, odd)])
        got = over_fsdp(give, 1)
        high_me = head_side == 1
        keep = [jnp.where(high_me, keep[1], keep[0]), jnp.where(high_me, keep[0], keep[1])]
        got = [jnp.where(high_me, got[1], got[0]), jnp.where(high_me, got[0], got[1])]
        halves = []
        for h in range(2):
            halves.append(jnp.where(core == 0, keep[h], got[h]))
            halves.append(jnp.where(core == 0, got[h], keep[h]))
        outs = jnp.stack(halves)
        prior = big[:3]
        names = [(w_qkv.shape, F32), (w_out.shape, F32), (gains_a.shape, F32)]
        args = [me1] + pieces + [w_qkv, gains_a, outs]
        specs = [scalars()] + [None] * 4 + [layer_of(w_qkv, depth), layer_of(gains_a, depth), None]
        extra = [] if prior[0] is None else prior
        big[:3] = call(
            finish_attention,
            names,
            args + extra,
            specs + [pl.BlockSpec(memory_space=pl.ANY)] * len(extra),
            aliases={len(args) + t: t for t in range(len(extra))},
            out_specs=[layer_of(jax.ShapeDtypeStruct(s, d), depth) for s, d in names],
        )
    return (
        output,
        gradient,
        d_table,
        big[2].reshape(layers, LANES),
        big[0],
        big[1],
        big[5].reshape(layers, LANES),
        big[3],
        big[4],
    )


def solution(mesh):
    in_specs = (
        P(("dp", "fsdp"), None),
        P(None, "fsdp"),
        P(),
        P(),
        P(),
        P(None, "fsdp"),
        P(None, "fsdp", None),
        P(None, "fsdp", None),
        P(None, "fsdp"),
        P(None, "fsdp", None),
        P(None, "fsdp", None),
        P(("dp", "fsdp"), None),
    )
    out_specs = (
        P(("dp", "fsdp"), None),
        P(("dp", "fsdp"), None),
        P(None, "fsdp"),
        P(None, "fsdp"),
        P(None, "fsdp", None),
        P(None, "fsdp", None),
        P(None, "fsdp"),
        P(None, "fsdp", None),
        P(None, "fsdp", None),
    )
    fast = mesh.shape["dp"] == 4 and mesh.shape["fsdp"] == 8
    local = local_fast if fast else local_general
    return jax.shard_map(local, mesh=mesh, in_specs=in_specs, out_specs=out_specs, check_vma=False)
```

```python
import functools
import math

import jax
import jax.numpy as jnp
from jax import lax
from jax.experimental import pallas as pl
from jax.experimental.pallas import tpu as pltpu
from jax.sharding import PartitionSpec as P

HEADS = 16
EPS = 1e-06
NEG_FILL = -1e30
MIX_WEIGHTS = (0.5, 0.25, 0.125, 0.125)
BF16 = jnp.bfloat16
F32 = jnp.float32


def dot(a, b):
    return jnp.dot(a, b, preferred_element_type=F32)


def dot_t(a, b):
    return lax.dot_general(a, b, (((0,), (0,)), ((), ())), preferred_element_type=F32)


def dot_nt(a, b):
    return lax.dot_general(a, b, (((1,), (1,)), ((), ())), preferred_element_type=F32)


def normalize(hidden):
    center = hidden - jnp.mean(hidden, axis=-1, keepdims=True)
    rstd = lax.rsqrt(jnp.mean(center * center, axis=-1, keepdims=True) + EPS)
    return center * rstd, rstd


def norm_backward(e, xhat, rstd):
    return rstd * (
        e
        - jnp.mean(e, axis=-1, keepdims=True)
        - xhat * jnp.mean(e * xhat, axis=-1, keepdims=True)
    )


def gelu_exact(pre_act):
    return jax.nn.gelu(pre_act, approximate=False)


class Square:
    def __init__(self):
        self.count = lax.axis_size("dp")
        self.me = lax.axis_index("dp")
        self.pairs = self.count == 4

    def owners(self):
        if self.pairs:
            return [self.me ^ k for k in range(self.count)]
        return [jnp.int32(k) for k in range(self.count)]

    def swap(self, block, k):
        return lax.ppermute(block, "dp", [(i, i ^ k) for i in range(self.count)])

    def spread(self, block):
        if self.pairs:
            return [block] + [self.swap(block, k) for k in range(1, self.count)]
        full = lax.all_gather(block, "dp")
        return [full[k] for k in range(self.count)]

    def collect(self, parts):
        if self.pairs:
            total = parts[0].astype(F32)
            for k in range(1, self.count):
                total = total + self.swap(parts[k].astype(BF16), k).astype(F32)
            return total
        stacked = jnp.stack([part.astype(BF16) for part in parts])
        return lax.psum_scatter(stacked, "dp", scatter_dimension=0, tiled=False).astype(F32)

    def gather(self, piece):
        if not self.pairs:
            return lax.all_gather(piece, "dp")
        got = [piece] + [self.swap(piece, k) for k in range(1, self.count)]
        odd = (self.me & 1) == 1
        high = (self.me & 2) == 2
        low_pair = (jnp.where(odd, got[1], got[0]), jnp.where(odd, got[0], got[1]))
        far_pair = (jnp.where(odd, got[3], got[2]), jnp.where(odd, got[2], got[3]))
        return jnp.stack(
            [
                jnp.where(high, far_pair[0], low_pair[0]),
                jnp.where(high, far_pair[1], low_pair[1]),
                jnp.where(high, low_pair[0], far_pair[0]),
                jnp.where(high, low_pair[1], far_pair[1]),
            ]
        )

    def total(self, piece):
        if not self.pairs:
            return lax.psum(piece.astype(BF16), "dp").astype(F32)
        own = piece.astype(BF16)
        got = [own.astype(F32)] + [self.swap(own, k).astype(F32) for k in range(1, self.count)]
        return (got[0] + got[1]) + (got[2] + got[3])


def select(index, choices):
    out = choices[0]
    for k in range(1, len(choices)):
        out = jnp.where(index == k, choices[k], out)
    return out


def local_general(
    tokens,
    pos_table,
    index_lo,
    index_hi,
    resolution,
    gain_attn,
    w_qkv,
    w_out,
    gain_mlp,
    w_up,
    w_down,
    cotangent,
):
    row_count, width = tokens.shape
    layers, shard_rows, _ = w_qkv.shape
    hidden_units = w_up.shape[2]
    shard_count = lax.axis_size("fsdp")
    shard = lax.axis_index("fsdp")
    square = Square()
    group_count = square.count
    me = square.me
    head_size = width // HEADS
    my_heads = HEADS // group_count
    part = my_heads * head_size
    unit_part = hidden_units // group_count
    fine = square.pairs and shard_count * 2 == HEADS
    score_scale = 1.0 / math.sqrt(head_size)
    len_low = index_lo.shape[0]
    len_high = index_hi.shape[0]

    row_ids = jnp.arange(row_count, dtype=jnp.int32)

    def layout(flag):
        length = jnp.where(flag == 1, len_high, len_low).astype(jnp.int32)
        images = jnp.where(flag == 1, row_count // len_high, row_count // len_low).astype(jnp.int32)
        live = row_ids < images * length
        return live, jnp.where(live, row_ids // length, images)

    flag = resolution[me]
    live_rows, _ = layout(flag)
    block_ids = jnp.stack([layout(resolution[owner])[1] for owner in square.owners()])
    same_image = block_ids[:, :, None] == block_ids[:, None, :]
    picked = jnp.where(flag == 1, index_hi[row_ids % len_high], index_lo[row_ids % len_low])
    table_ids = jnp.arange(len_high, dtype=jnp.int32)
    mixing = jnp.zeros((row_count, len_high), F32)
    for slot in range(4):
        mixing = mixing + MIX_WEIGHTS[slot] * (
            picked[:, slot : slot + 1] == table_ids[None, :]
        ).astype(F32)
    mixing = (mixing * live_rows[:, None].astype(F32)).astype(BF16)
    high_groups = jnp.sum(resolution)
    tokens_low = (
        (group_count - high_groups) * shard_count * (row_count // len_low) * len_low
    ).astype(F32)
    tokens_high = (high_groups * shard_count * (row_count // len_high) * len_high).astype(F32)
    token_share = 2.0 * jnp.where(flag == 1, tokens_high, tokens_low) / (tokens_low + tokens_high)
    weight = jnp.where(live_rows, token_share, 0.0)

    half = shard_rows // 4
    core = shard % 2
    swap_core = [(j, j ^ 1) for j in range(shard_count)]
    pair_side, head_side = me & 1, (me >> 1) & 1

    def qkv_part(w):
        if fine:
            view = w.reshape(shard_rows, 3 * HEADS // 4, 2, 2, head_size)
            view = select(pair_side, [view[:, :, 0], view[:, :, 1]])
            view = select(head_side, [view[:, :, 0], view[:, :, 1]])
            return view.reshape(shard_rows, 3 * part)
        view = w.reshape(shard_rows, 3, group_count, part)
        return lax.dynamic_index_in_dim(view, me, 2, keepdims=False).reshape(shard_rows, 3 * part)

    def up_part(w):
        view = w.reshape(shard_rows, shard_count, group_count, unit_part // shard_count)
        return lax.dynamic_index_in_dim(view, me, 2, keepdims=False).reshape(shard_rows, unit_part)

    def down_part(w):
        rows = unit_part // shard_count
        return lax.dynamic_slice_in_dim(w, me * rows, rows, 0)

    def out_part(w):
        if fine:
            view = w.reshape(2, 2, half, width)
            mine = select(head_side, [view[0], view[1]])
            keep = select(core, [mine[0], mine[1]])
            give = select(core, [mine[1], mine[0]])
            got = lax.ppermute(give, "fsdp", swap_core)
            return jnp.where(core == pair_side, keep, got)
        return w

    def fetch(piece):
        return lax.all_gather(piece, "fsdp", axis=0, tiled=False)

    weights = []
    table = lax.all_gather(pos_table, "fsdp", axis=1, tiled=True)
    for depth in range(layers):
        gain_a = gain_attn[depth].astype(F32)[:, None]
        gain_m = gain_mlp[depth].astype(F32)[:, None]
        qkv = (qkv_part(w_qkv[depth]).astype(F32) * gain_a).astype(BF16)
        up = (up_part(w_up[depth]).astype(F32) * gain_m).astype(BF16)
        down = down_part(w_down[depth])
        out = out_part(w_out[depth])
        qkv_all = fetch(qkv).reshape(width, 3 * part)
        a = up.size // width
        b = a + down.shape[0]
        rest = fetch(jnp.concatenate([up.reshape(a, width), down, out], axis=0))
        up_all = rest[:, :a].reshape(width, unit_part)
        down_all = rest[:, a:b].reshape(unit_part, width)
        out_all = rest[:, b:].reshape(-1, width)
        if not fine:
            out_all = lax.dynamic_slice_in_dim(out_all, me * part, part, 0)
        weights.append((qkv_all, out_all, up_all, down_all))

    def split_heads(block):
        return block.reshape(group_count, row_count, my_heads, head_size)

    def scores_of(queries, key_rows):
        scores = (
            jnp.einsum("bqhd,bkhd->bhqk", queries, key_rows, preferred_element_type=F32)
            * score_scale
        )
        return jnp.where(same_image[:, None], scores, NEG_FILL)

    def spread(block):
        return jnp.concatenate(square.spread(block), axis=0)

    def collect(partial):
        return square.collect([partial[k * row_count : (k + 1) * row_count] for k in range(group_count)])

    hidden = tokens.astype(F32) + dot(mixing, table)
    saved = []
    for depth in range(layers):
        qkv_w, out_w, up_w, down_w = weights[depth]
        xhat_a, rstd_a = normalize(hidden)
        rows_a = spread(xhat_a.astype(BF16))
        projected = dot(rows_a, qkv_w).astype(BF16)
        queries = split_heads(projected[:, :part])
        key_rows = split_heads(projected[:, part : 2 * part])
        values = split_heads(projected[:, 2 * part :])
        scores = scores_of(queries, key_rows)
        row_max = jnp.max(scores, axis=-1, keepdims=True)
        powers = jnp.exp(scores - row_max)
        row_total = jnp.sum(powers, axis=-1, keepdims=True)
        log_total = row_max + jnp.log(row_total)
        probs = (powers / row_total).astype(BF16)
        attended = jnp.einsum("bhqk,bkhd->bqhd", probs, values, preferred_element_type=F32)
        attended = attended.reshape(group_count * row_count, part).astype(BF16)
        middle = hidden + collect(dot(attended, out_w).astype(BF16))
        xhat_m, rstd_m = normalize(middle)
        rows_m = spread(xhat_m.astype(BF16))
        pre_act = dot(rows_m, up_w)
        activated = gelu_exact(pre_act).astype(BF16)
        result = middle + collect(dot(activated, down_w).astype(BF16))
        saved.append(
            (xhat_a, rstd_a, rows_a, queries, key_rows, values, log_total, attended,
             xhat_m, rstd_m, rows_m, pre_act, activated)
        )
        hidden = result

    gradient = cotangent.astype(F32) * weight[:, None]
    shares = [None] * layers
    for depth in reversed(range(layers)):
        qkv_w, out_w, up_w, down_w = weights[depth]
        (xhat_a, rstd_a, rows_a, queries, key_rows, values, log_total, attended,
         xhat_m, rstd_m, rows_m, pre_act, activated) = saved[depth]
        d_result = spread(gradient.astype(BF16))
        grad_down = dot_t(activated, d_result).astype(BF16)
        d_activated = dot_nt(d_result, down_w)
        _, pullback = jax.vjp(gelu_exact, pre_act)
        d_pre = pullback(d_activated)[0].astype(BF16)
        grad_up = dot_t(rows_m, d_pre).astype(BF16)
        e = collect(dot_nt(d_pre, up_w).astype(BF16))
        d_middle = gradient + norm_backward(e, xhat_m, rstd_m)
        d_attn = spread(d_middle.astype(BF16))
        grad_out = dot_t(attended, d_attn).astype(BF16)
        d_attended = split_heads(dot_nt(d_attn, out_w).astype(BF16))
        probs = jnp.exp(scores_of(queries, key_rows) - log_total)
        d_values = jnp.einsum(
            "bhqk,bqhd->bkhd", probs.astype(BF16), d_attended, preferred_element_type=F32
        )
        d_probs = jnp.einsum("bqhd,bkhd->bhqk", d_attended, values, preferred_element_type=F32)
        centre = jnp.sum(probs * d_probs, axis=-1, keepdims=True)
        d_scores = (probs * (d_probs - centre)).astype(BF16)
        d_queries = (
            jnp.einsum("bhqk,bkhd->bqhd", d_scores, key_rows, preferred_element_type=F32)
            * score_scale
        )
        d_keys = (
            jnp.einsum("bhqk,bqhd->bkhd", d_scores, queries, preferred_element_type=F32)
            * score_scale
        )
        d_projected = jnp.concatenate(
            [x.astype(BF16).reshape(group_count * row_count, part) for x in (d_queries, d_keys, d_values)],
            axis=1,
        )
        grad_qkv = dot_t(rows_a, d_projected).astype(BF16)
        e = collect(dot_nt(d_projected, qkv_w).astype(BF16))
        gradient = d_middle + norm_backward(e, xhat_a, rstd_a)
        shares[depth] = (grad_qkv, grad_out, grad_up, grad_down)

    def home(term):
        return lax.psum_scatter(term, "fsdp", scatter_dimension=0, tiled=True)

    grads_qkv, grads_out, grads_up, grads_down, gains_a, gains_m = [], [], [], [], [], []
    for depth in reversed(range(layers)):
        grad_qkv, grad_out, grad_up, grad_down = shares[depth]
        rest = [
            grad_up.reshape(shard_count, -1, width),
            grad_down.reshape(shard_count, -1, width),
        ]
        if fine:
            rest.append(grad_out.reshape(shard_count, -1, width))
        else:
            full = jnp.zeros((width, width), BF16)
            full = lax.dynamic_update_slice_in_dim(full, grad_out, me * part, 0)
            rest.append(full.reshape(shard_count, -1, width))
        sizes = [x.shape[1] for x in rest]
        rest = home(jnp.concatenate(rest, axis=1))[0]
        qkv = square.gather(home(grad_qkv))
        if not fine:
            out = square.total(rest[sizes[0] + sizes[1] :])
            rest = rest[: sizes[0] + sizes[1]]
        rest = square.gather(rest)
        up = rest[:, : sizes[0]].reshape(group_count, shard_rows, shard_count, -1)
        up = up.transpose(1, 2, 0, 3).reshape(shard_rows, hidden_units).astype(F32)
        down = rest[:, sizes[0] : sizes[0] + sizes[1]].reshape(-1, width).astype(F32)
        if fine:
            pieces = rest[:, sizes[0] + sizes[1] :].reshape(2, 2, half, width)
            keep = select(core, [pieces[:, 0], pieces[:, 1]])
            give = select(core, [pieces[:, 1], pieces[:, 0]])
            got = lax.ppermute(give, "fsdp", swap_core)
            first = select(core, [keep, got])
            second = select(core, [got, keep])
            out = jnp.stack([first, second], axis=1).reshape(shard_rows, width).astype(F32)
            qkv = qkv.reshape(2, 2, shard_rows, 3 * my_heads, head_size).transpose(2, 3, 1, 0, 4)
        else:
            qkv = qkv.reshape(group_count, shard_rows, 3, part).transpose(1, 2, 0, 3)
        qkv = qkv.reshape(shard_rows, 3 * width).astype(F32)
        gains_a.append(jnp.sum(qkv * w_qkv[depth].astype(F32), axis=1))
        gains_m.append(jnp.sum(up * w_up[depth].astype(F32), axis=1))
        grads_qkv.append(qkv * gain_attn[depth].astype(F32)[:, None])
        grads_up.append(up * gain_mlp[depth].astype(F32)[:, None])
        grads_out.append(out)
        grads_down.append(down)

    high_part = gradient.astype(BF16)
    low_part = (gradient - high_part.astype(F32)).astype(BF16)
    table_term = dot_t(mixing, high_part) + dot_t(mixing, low_part)
    table_share = lax.psum_scatter(table_term.astype(BF16), "fsdp", scatter_dimension=1, tiled=True)
    d_table = square.total(table_share)
    return (
        hidden,
        gradient,
        d_table,
        jnp.stack(gains_a[::-1]),
        jnp.stack(grads_qkv[::-1]),
        jnp.stack(grads_out[::-1]),
        jnp.stack(gains_m[::-1]),
        jnp.stack(grads_up[::-1]),
        jnp.stack(grads_down[::-1]),
    )


VMEM = pltpu.VMEM
LANES = 128


def whole(shape):
    return pl.BlockSpec(tuple(shape), lambda *_: (0,) * len(shape))


def scalars():
    return pl.BlockSpec(memory_space=pltpu.SMEM)


def call(body, outs, args, specs=None, scratch=(), flops=0, reads=0, aliases=None, out_specs=None, limit=40, after=()):
    specs = [whole(a.shape) if s is None else s for a, s in zip(args, specs or [None] * len(args))]
    specs = specs + [pl.BlockSpec(memory_space=pl.ANY)] * len(after)
    count, extra = len(args), len(after)
    out_shape = [jax.ShapeDtypeStruct(shape, dtype) for shape, dtype in outs]
    moved = sum(math.prod(s) * jnp.dtype(d).itemsize for s, d in outs) + reads

    def run(*refs):
        body(*refs[:count], *refs[count + extra :])

    name = body.func.__name__ if isinstance(body, functools.partial) else body.__name__
    return pl.pallas_call(
        run,
        name=name,
        grid=(1,),
        in_specs=specs,
        out_specs=out_specs or [whole(shape) for shape, _ in outs],
        out_shape=out_shape,
        scratch_shapes=list(scratch),
        input_output_aliases=aliases or {},
        cost_estimate=pl.CostEstimate(flops=int(flops), bytes_accessed=int(moved), transcendentals=0),
        compiler_params=pltpu.CompilerParams(vmem_limit_bytes=limit << 20),
    )(*args, *after)


def diagonal(gain_row):
    r = lax.broadcasted_iota(jnp.int32, (LANES, LANES), 0)
    c = lax.broadcasted_iota(jnp.int32, (LANES, LANES), 1)
    return jnp.where(r == c, jnp.broadcast_to(gain_row.astype(F32), (LANES, LANES)), 0.0)


def lane_low(rows):
    return lax.broadcasted_iota(jnp.int32, (rows, LANES), 1) < LANES // 2


def lane_swap(block):
    return jnp.concatenate([block[:, LANES // 2 :], block[:, : LANES // 2]], axis=1)


def pack_attention(me, w_ref, gain_row, out_ref, packed_ref, top):
    side, second = me & 1, me >> 1
    diag = diagonal(gain_row).astype(BF16)
    low = lane_low(LANES)

    def head(t):
        chunk = pl.multiple_of(((t // 4) * 8 + 2 * (t % 4) + side) * LANES, LANES)
        got = dot(diag, w_ref[0, :, pl.ds(chunk, LANES)])
        turned = lane_swap(got)
        if t % 2 == 0:
            return jnp.where(second == 0, got, turned)
        return jnp.where(second == 0, turned, got)

    for u in range(6):
        pair = jnp.where(low, head(2 * u), head(2 * u + 1))
        packed_ref[top : top + LANES, u * LANES : (u + 1) * LANES] = pair.astype(BF16)
    for c in range(4):
        packed_ref[top + c * 32 : top + (c + 1) * 32, 768:1024] = out_ref[:, c * 256 : (c + 1) * 256]


def pack_up(me, up_ref, gain_row, packed_ref, top):
    diag = diagonal(gain_row).astype(BF16)
    for j in range(8):
        chunk = pl.multiple_of((j * 4 + me) * LANES, LANES)
        packed_ref[top : top + LANES, j * LANES : (j + 1) * LANES] = dot(
            diag, up_ref[0, :, pl.ds(chunk, LANES)]
        ).astype(BF16)


def pack_down(me, down_ref, packed_ref, top):
    packed_ref[top : top + LANES, :] = down_ref[0, pl.ds(pl.multiple_of(me * LANES, LANES), LANES), :]


def prepare_first(me_ref, w_ref, gain_a, out_ref, up_ref, gain_m, packed_ref):
    pack_attention(me_ref[0], w_ref, gain_a[0], out_ref, packed_ref, 0)
    pack_up(me_ref[0], up_ref, gain_m[0], packed_ref, LANES)


def prepare_second(me_ref, w_ref, gain_a, out_ref, down_ref, packed_ref):
    pack_attention(me_ref[0], w_ref, gain_a[0], out_ref, packed_ref, LANES)
    pack_down(me_ref[0], down_ref, packed_ref, 0)


def prepare_third(me_ref, up_ref, gain_m, down_ref, packed_ref):
    pack_up(me_ref[0], up_ref, gain_m[0], packed_ref, 0)
    pack_down(me_ref[0], down_ref, packed_ref, LANES)


def image_numbers(rows, flag, lens):
    counts = [sum((rows >= t * n).astype(jnp.int32) for t in range(1, most + 1)) for n, most in lens]
    return jnp.where(flag == 1, counts[1], counts[0])


def make_mixing(flag_ref, low_ref, high_ref, mixing_ref, *, lens):
    rows = mixing_ref.shape[0]
    flag = flag_ref[0]

    def spread_rows(index_ref, length, most):
        count = index_ref.shape[0]
        columns = lax.broadcasted_iota(jnp.int32, (count, mixing_ref.shape[1]), 1)
        mix = jnp.zeros((count, mixing_ref.shape[1]), F32)
        for slot in range(4):
            mix = mix + MIX_WEIGHTS[slot] * (index_ref[:, slot : slot + 1] == columns).astype(F32)
        r = lax.broadcasted_iota(jnp.int32, (rows, count), 0)
        c = lax.broadcasted_iota(jnp.int32, (rows, count), 1)
        image = sum((r >= t * length).astype(jnp.int32) for t in range(1, most + 1))
        pick = ((r - image * length == c) & (r < most * length)).astype(BF16)
        return dot(pick, mix.astype(BF16))

    low = spread_rows(low_ref, *lens[0])
    high = spread_rows(high_ref, *lens[1])
    mixing_ref[...] = jnp.where(flag == 1, high, low).astype(BF16)


def write_norm(hidden, xhat_ref):
    xhat_ref[...] = normalize(hidden)[0].astype(BF16)


def embed(z_ref, tokens_ref, mixing_ref, t0, t1, t2, t3, hidden_ref, xhat_ref, table):
    z = z_ref[0]
    for k, piece in enumerate((t0, t1, t2, t3)):
        table[:, pl.ds(pl.multiple_of((z ^ k) * 256, 256), 256)] = piece[...].astype(F32)
    hidden = tokens_ref[...].astype(F32) + dot(mixing_ref[...], table[...].astype(BF16))
    hidden_ref[...] = hidden
    write_norm(hidden, xhat_ref)


def added(p0, r1, r2, r3):
    return (p0[...].astype(F32) + r1[...].astype(F32)) + (r2[...].astype(F32) + r3[...].astype(F32))


def add_norm(h_ref, p0, r1, r2, r3, middle_ref, xhat_ref):
    middle = h_ref[...] + added(p0, r1, r2, r3)
    middle_ref[...] = middle
    write_norm(middle, xhat_ref)


def add_output(h_ref, p0, r1, r2, r3, out_ref):
    out_ref[...] = h_ref[...] + added(p0, r1, r2, r3)


def add_norm_backward(g_ref, p0, r1, r2, r3, h_ref, d_ref, low_ref):
    d = g_ref[...] + norm_backward(added(p0, r1, r2, r3), *normalize(h_ref[...]))
    d_ref[...] = d
    low_ref[...] = d.astype(BF16)


def out_chunk(packed_ref, c):
    return packed_ref[:, c * 32 : (c + 1) * 32, 768:1024].reshape(256, 256)


def attention_forward(flag_ref, x_ref, w_ref, proj_ref, p_ref, *, lens):
    rows = x_ref.shape[0]
    flag = flag_ref[0]
    width = x_ref.shape[1]
    mask = image_numbers(lax.broadcasted_iota(jnp.int32, (rows, 1), 0), flag, lens) == image_numbers(
        lax.broadcasted_iota(jnp.int32, (1, rows), 1), flag, lens
    )
    for c in range(3):
        w = w_ref[:, :, c * 256 : (c + 1) * 256].reshape(width, 256)
        proj_ref[:, c * 256 : (c + 1) * 256] = dot(x_ref[...], w).astype(BF16)
    low = lane_low(rows)
    zero = jnp.zeros((), BF16)
    for u in range(2):
        q = proj_ref[:, u * LANES : (u + 1) * LANES] * jnp.asarray(0.125, BF16)
        k = proj_ref[:, 256 + u * LANES : 256 + (u + 1) * LANES]
        v = proj_ref[:, 512 + u * LANES : 512 + (u + 1) * LANES]
        total = None
        for keep in (low, ~low):
            s = dot_nt(jnp.where(keep, q, zero), k)
            s = jnp.where(mask, s, NEG_FILL)
            powers = jnp.exp(s - jnp.max(s, axis=-1, keepdims=True))
            probs = powers * (1.0 / jnp.sum(powers, axis=-1, keepdims=True))
            o = dot(probs.astype(BF16), jnp.where(keep, v, zero))
            total = o if total is None else total + o
        proj_ref[:, 768 + u * LANES : 768 + (u + 1) * LANES] = total.astype(BF16)
    for c in range(4):
        p_ref[:, c * 256 : (c + 1) * 256] = dot(proj_ref[:, 768:], out_chunk(w_ref, c)).astype(BF16)


def attention_backward(flag_ref, d_ref, proj_ref, w_ref, dproj_ref, p_ref, *, lens):
    rows, width = d_ref.shape
    flag = flag_ref[0]
    mask = image_numbers(lax.broadcasted_iota(jnp.int32, (rows, 1), 0), flag, lens) == image_numbers(
        lax.broadcasted_iota(jnp.int32, (1, rows), 1), flag, lens
    )
    d_o = sum(dot_nt(d_ref[:, c * 256 : (c + 1) * 256], out_chunk(w_ref, c)) for c in range(4))
    d_o = d_o.astype(BF16)
    low = lane_low(rows)
    zero = jnp.zeros((), BF16)
    scale = jnp.asarray(0.125, BF16)
    for u in range(2):
        q = proj_ref[:, u * LANES : (u + 1) * LANES] * scale
        k = proj_ref[:, 256 + u * LANES : 256 + (u + 1) * LANES]
        v = proj_ref[:, 512 + u * LANES : 512 + (u + 1) * LANES]
        g = d_o[:, u * LANES : (u + 1) * LANES]
        dq = dk = dv = None
        for keep in (low, ~low):
            k_own = jnp.where(keep, k, zero)
            s = jnp.where(mask, dot_nt(k_own, q), NEG_FILL)
            powers = jnp.exp(s - jnp.max(s, axis=0, keepdims=True))
            probs = powers * (1.0 / jnp.sum(powers, axis=0, keepdims=True))
            d_probs = dot_nt(jnp.where(keep, v, zero), g)
            centre = jnp.sum(probs * d_probs, axis=0, keepdims=True)
            d_scores = (probs * (d_probs - centre)).astype(BF16)
            terms = (
                dot_t(d_scores, k_own),
                dot(d_scores, jnp.where(keep, q, zero)),
                dot(probs.astype(BF16), jnp.where(keep, g, zero)),
            )
            dq, dk, dv = terms if dq is None else (dq + terms[0], dk + terms[1], dv + terms[2])
        dproj_ref[:, u * LANES : (u + 1) * LANES] = (dq * 0.125).astype(BF16)
        dproj_ref[:, 256 + u * LANES : 256 + (u + 1) * LANES] = dk.astype(BF16)
        dproj_ref[:, 512 + u * LANES : 512 + (u + 1) * LANES] = dv.astype(BF16)
    total = None
    for c in range(3):
        w = w_ref[:, :, c * 256 : (c + 1) * 256].reshape(width, 256)
        term = dot_nt(dproj_ref[:, c * 256 : (c + 1) * 256], w)
        total = term if total is None else total + term
    p_ref[...] = total.astype(BF16)


def gelu_parts(pre):
    upto = 0.5 * (1.0 + lax.erf(pre * math.sqrt(0.5)))
    density = jnp.exp(-0.5 * pre * pre) * (1.0 / math.sqrt(2.0 * math.pi))
    return pre * upto, upto + pre * density


def mlp_up(x_ref, up_ref, both_ref):
    width = x_ref.shape[1]
    for c in range(4):
        cols = slice(c * 256, (c + 1) * 256)
        act, slope = gelu_parts(dot(x_ref[...], up_ref[:, :, cols].reshape(width, 256)))
        both_ref[0, :, cols] = act.astype(BF16)
        both_ref[1, :, cols] = slope.astype(BF16)


def mlp_down(act_ref, down_ref, p_ref):
    width = p_ref.shape[1]
    p_ref[...] = dot(act_ref[0], down_ref[...].reshape(width, width)).astype(BF16)


def mlp_backward(d_ref, slope_ref, up_ref, down_ref, dpre_ref, p_ref):
    width = d_ref.shape[1]
    for c in range(4):
        cols = slice(c * 256, (c + 1) * 256)
        d_act = dot_nt(d_ref[...], down_ref[2 * c : 2 * c + 2].reshape(256, width))
        dpre_ref[:, cols] = (d_act * slope_ref[0, :, cols].astype(F32)).astype(BF16)
    p_ref[...] = dot_nt(dpre_ref[...], up_ref[...].reshape(width, width)).astype(BF16)


def mlp_both(x_ref, d_ref, up_ref, down_ref, act_ref, dpre_ref, p_ref, back_ref):
    width = x_ref.shape[1]
    for c in range(4):
        cols = slice(c * 256, (c + 1) * 256)
        act, slope = gelu_parts(dot(x_ref[...], up_ref[:, :, cols].reshape(width, 256)))
        act_ref[:, cols] = act.astype(BF16)
        d_act = dot_nt(d_ref[...], down_ref[2 * c : 2 * c + 2].reshape(256, width))
        dpre_ref[:, cols] = (d_act * slope).astype(BF16)
    back_ref[...] = dot_nt(dpre_ref[...], up_ref[...].reshape(width, width)).astype(BF16)
    p_ref[...] = dot(act_ref[...], down_ref[...].reshape(width, width)).astype(BF16)


def summed(left, right, rows, cols=slice(None)):
    total = None
    for a, b in zip(left, right):
        term = dot_t(a[:, rows], b[:, cols])
        total = term if total is None else total + term
    return total


def grads_mlp(*refs):
    x, dpre, act, d, out_ref = refs[:4], refs[4:8], refs[8:12], refs[12:16], refs[16]
    act = [a.at[0] if len(a.shape) == 3 else a for a in act]
    for half, (left, right) in enumerate(((x, dpre), (act, d))):
        for j in range(8):
            total = summed(left, right, slice(j * LANES, (j + 1) * LANES))
            out_ref[j, half * LANES : (half + 1) * LANES, :] = total.astype(BF16)


def grads_attention(*refs):
    x, dproj, kept, d, out_ref = refs[:4], refs[4:8], refs[8:12], refs[12:16], refs[16]
    for j in range(8):
        out_ref[j, :, :768] = summed(x, dproj, slice(j * LANES, (j + 1) * LANES)).astype(BF16)
    for c in range(4):
        total = summed(kept, d, slice(None), slice(c * 256, (c + 1) * 256))
        out_ref[:, c * 32 : (c + 1) * 32, 768:1024] = total.astype(BF16).reshape(8, 32, 256)


def finish_mlp(me_ref, g0, g1, g2, g3_up, g3_down, up_ref, gain_ref, *rest):
    dup_ref, ddown_ref, dgain_ref = rest[-3:]
    me = me_ref[0]
    column = jnp.sum(diagonal(gain_ref[0]), axis=1, keepdims=True)
    total = jnp.zeros((LANES, LANES), F32)
    for k, piece in enumerate((g0[LANES:, :], g1[LANES:, :], g2[LANES:, :], g3_down[...])):
        rows = pl.ds(pl.multiple_of((me ^ k) * LANES, LANES), LANES)
        ddown_ref[0, rows, :] = piece.astype(F32)
    ups = [g0[:LANES, :], g1[:LANES, :], g2[:LANES, :], g3_up[...]]
    for i in range(4):
        got = jnp.where(
            me == i, ups[0], jnp.where(me == i ^ 1, ups[1], jnp.where(me == i ^ 2, ups[2], ups[3]))
        ).astype(F32)
        for j in range(8):
            cols = slice((j * 4 + i) * LANES, (j * 4 + i + 1) * LANES)
            part = got[:, j * LANES : (j + 1) * LANES]
            dup_ref[0, :, cols] = part * column
            total = total + part * up_ref[0, :, cols].astype(F32)
    dgain_ref[0] = jnp.sum(total.T, axis=0, keepdims=True)


def finish_attention(me_ref, g0, g1, g2, g3, w_ref, gain_ref, out_ref, *rest):
    dqkv_ref, dout_ref, dgain_ref = rest[-3:]
    me = me_ref[0]
    column = jnp.sum(diagonal(gain_ref[0]), axis=1, keepdims=True)
    total = jnp.zeros((LANES, LANES), F32)
    low = lane_low(LANES)
    owned = []
    for i in range(4):
        owned.append(
            jnp.where(
                me == i, g0[:, :768], jnp.where(me == i ^ 1, g1[:, :768], jnp.where(me == i ^ 2, g2[:, :768], g3[:, :768]))
            ).astype(F32)
        )
    for t in range(12):
        u = t // 2
        for side in range(2):
            first = owned[side][:, u * LANES : (u + 1) * LANES]
            second = owned[side + 2][:, u * LANES : (u + 1) * LANES]
            if t % 2 == 0:
                part = jnp.where(low, first, lane_swap(second))
            else:
                part = jnp.where(low, lane_swap(first), second)
            chunk = (t // 4) * 8 + 2 * (t % 4) + side
            cols = slice(chunk * LANES, (chunk + 1) * LANES)
            dqkv_ref[0, :, cols] = part * column
            total = total + part * w_ref[0, :, cols].astype(F32)
    dgain_ref[0] = jnp.sum(total.T, axis=0, keepdims=True)
    for h in range(4):
        for c in range(4):
            dout_ref[0, h * 32 : (h + 1) * 32, c * 256 : (c + 1) * 256] = out_ref[
                h, c * 32 : (c + 1) * 32, :
            ].astype(F32)


def local_fast(
    tokens,
    pos_table,
    index_lo,
    index_hi,
    resolution,
    gain_attn,
    w_qkv,
    w_out,
    gain_mlp,
    w_up,
    w_down,
    cotangent,
):
    rows, width = tokens.shape
    layers = w_qkv.shape[0]
    square = Square()
    me = square.me
    me1 = me.reshape(1).astype(jnp.int32)
    shard = lax.axis_index("fsdp")
    core, deep = shard % 2, shard // 2
    deep1 = deep.reshape(1).astype(jnp.int32)
    len_low, len_high = index_lo.shape[0], index_hi.shape[0]
    lens = ((len_low, rows // len_low), (len_high, rows // len_high))
    block = (rows, width)
    blocks = range(4)

    def over_fsdp(x, k):
        return lax.ppermute(x, "fsdp", [(j, j ^ k) for j in range(8)])

    def layer_of(array, depth):
        return pl.BlockSpec((1,) + array.shape[1:], lambda *_: (depth,) + (0,) * (array.ndim - 1))

    pair_side, head_side = me & 1, me >> 1
    view = w_out.reshape(layers, 2, 2, 32, width)
    mine = jnp.where(head_side == 1, view[:, 1], view[:, 0])
    keep = jnp.where(core == 1, mine[:, 1], mine[:, 0])
    give = jnp.where(core == 1, mine[:, 0], mine[:, 1])
    out_pieces = jnp.where(core == pair_side, keep, over_fsdp(give, 1))
    gains_a = gain_attn.reshape(layers, 1, LANES)
    gains_m = gain_mlp.reshape(layers, 1, LANES)

    def part(top):
        return pl.BlockSpec((8, LANES, width), lambda *_: (0, top, 0))

    def fetch(body, args, specs, after=()):
        (packed,) = call(body, [((2 * LANES, width), BF16)], [me1] + args, [scalars()] + specs, after=after)
        return lax.all_gather(packed, "fsdp", axis=0, tiled=False)

    first_w = fetch(
        prepare_first,
        [w_qkv, gains_a, out_pieces[0], w_up, gains_m],
        [layer_of(w_qkv, 0), layer_of(gains_a, 0), None, layer_of(w_up, 0), layer_of(gains_m, 0)],
    )

    flag = resolution[me]
    flag1 = flag.reshape(1)
    flags = [resolution[owner].reshape(1) for owner in square.owners()]
    shard_count, group_count = 8, resolution.shape[0]
    high_groups = jnp.sum(resolution)
    tokens_low = ((group_count - high_groups) * shard_count * lens[0][1] * len_low).astype(F32)
    tokens_high = (high_groups * shard_count * lens[1][1] * len_high).astype(F32)
    token_share = 2.0 * jnp.where(flag == 1, tokens_high, tokens_low) / (tokens_low + tokens_high)
    live = jnp.where(flag == 1, lens[1][1] * len_high, lens[0][1] * len_low)
    weight = jnp.where(jnp.arange(rows, dtype=jnp.int32) < live, token_share, 0.0)
    gradient = cotangent.astype(F32) * weight[:, None]

    normed = [(block, F32), (block, BF16)]
    other = over_fsdp(pos_table, 1)
    pair = jnp.concatenate(
        [jnp.where(core == 0, pos_table, other), jnp.where(core == 0, other, pos_table)], axis=1
    )
    pieces = [pair] + [over_fsdp(pair, 2 * k) for k in range(1, 4)]
    (mixing,) = call(
        functools.partial(make_mixing, lens=lens),
        [((rows, len_high), BF16)],
        [flag1, index_lo, index_hi],
        [scalars(), None, None],
    )
    hidden, xhat = call(
        embed,
        normed,
        [deep1, tokens, mixing] + pieces,
        [scalars()] + [None] * 6,
        scratch=[VMEM((len_high, width), F32)],
        flops=2 * rows * len_high * width,
    )

    second_w = fetch(
        prepare_second,
        [w_qkv, gains_a, out_pieces[1], w_down],
        [layer_of(w_qkv, 1), layer_of(gains_a, 1), None, layer_of(w_down, 0)],
        [xhat],
    )
    third_w = fetch(
        prepare_third,
        [w_up, gains_m, w_down],
        [layer_of(w_up, 1), layer_of(gains_m, 1), layer_of(w_down, 1)],
        [xhat],
    )
    attn_w = [(first_w, part(0)), (second_w, part(1))]

    def tie(*values):
        return lax.optimization_barrier(values)

    def chain(kernel):
        done = []
        for k in blocks:
            done.append(kernel(k, [d[0] for d in done[-1:]]))
        return done

    def collect(parts):
        return [parts[0]] + [square.swap(parts[k], k) for k in range(1, 4)]

    d_top = square.spread(gradient.astype(BF16))
    saved = []
    for depth in range(layers):
        a_w, a_part = attn_w[depth]
        xs = square.spread(xhat)
        got = chain(
            lambda k, after: call(
                functools.partial(attention_forward, lens=lens),
                [(block, BF16)] * 2,
                [flags[k], xs[k], a_w],
                [scalars(), None, a_part],
                after=after,
            )
        )
        kept = [g[0] for g in got]
        es = collect([g[1] for g in got])
        if depth == 0:
            es, d_top = tie(es, d_top)
        before, (middle, xhat) = hidden, call(add_norm, normed, [hidden] + es)
        ms = square.spread(xhat)
        if depth < layers - 1:
            acts = chain(
                lambda k, after: call(
                    mlp_up, [((2,) + block, BF16)], [ms[k], first_w], [None, part(1)], after=after
                )
            )
            acts = [a[0] for a in acts]
            parts = [None] * 4
            last = acts
            for k in (1, 2, 3, 0):
                (parts[k],) = call(
                    mlp_down, [(block, BF16)], [acts[k], second_w], [None, part(0)], after=last
                )
                last = [parts[k]]
            saved.append((before, xs, kept, middle, ms, acts))
            hidden, xhat = call(add_norm, normed, [middle] + collect(parts))
        else:
            got = chain(
                lambda k, after: call(
                    mlp_both,
                    [(block, BF16)] * 4,
                    [ms[k], d_top[k], third_w, third_w],
                    [None, None, part(0), part(1)],
                    after=after,
                )
            )
            acts, dpres, output_parts, backs = ([g[t] for g in got] for t in range(4))
            saved.append((before, xs, kept, middle, ms, acts))

    def far_halves(x, y):
        half = x.shape[0] // 2
        return [square.swap(x[:half], 2), square.swap(y[half:], 1)]

    def home(term):
        return lax.psum_scatter(term, "fsdp", scatter_dimension=0, tiled=False)

    homes_m, homes_a = [None] * layers, [None] * layers
    for depth in reversed(range(layers)):
        top = depth == layers - 1
        a_w, a_part = attn_w[depth]
        before, xs, kept, middle, ms, acts = saved[depth]
        ds = d_top if top else square.spread(low)
        if not top:
            second_half = pl.BlockSpec((1,) + block, lambda *_: (1, 0, 0))
            got = chain(
                lambda k, after: call(
                    mlp_backward,
                    [(block, BF16)] * 2,
                    [ds[k], acts[k], first_w, second_w],
                    [None, second_half, part(1), part(0)],
                    after=after or late[1][1:],
                )
            )
            dpres, backs = ([g[t] for g in got] for t in range(2))
        es = collect(backs)
        first_half = pl.BlockSpec((1,) + block, lambda *_: (0, 0, 0))
        (term,) = call(
            grads_mlp,
            [((8, 2 * LANES, width), BF16)],
            list(ms) + list(dpres) + list(acts) + list(ds),
            [None] * 8 + [None if top else first_half] * 4 + [None] * 4,
        )
        es, term = tie(es, term)
        if not top:
            es, homes_m[depth + 1] = tie(es, homes_m[depth + 1])
        homes_m[depth] = home(term)
        d_middle, low = call(add_norm_backward, normed, [gradient] + es + [middle])
        ds = square.spread(low)
        got = chain(
            lambda k, after: call(
                functools.partial(attention_backward, lens=lens),
                [((rows, 768), BF16), (block, BF16)],
                [flags[k], ds[k], kept[k], a_w],
                [scalars(), None, None, a_part],
                after=after,
            )
        )
        dprojs = [g[0] for g in got]
        es = collect([g[1] for g in got])
        if top:
            outs = collect(output_parts)
        out_part = pl.BlockSpec((rows, 256), lambda *_: (0, 3))
        (term,) = call(
            grads_attention,
            [((8, LANES, width), BF16)],
            list(xs) + dprojs + list(kept) + list(ds),
            [None] * 8 + [out_part] * 4 + [None] * 4,
        )
        es, term = tie(es, term)
        homes_a[depth] = home(term)
        if top:
            late = (middle, outs)
        else:
            x, y = square.swap(homes_m[1], 1), square.swap(homes_m[1], 2)
            es, homes_a[1], x, y = tie(es, homes_a[1], x, y)
            homes_m[1] = [homes_m[1], x, y] + far_halves(x, y)
        gradient, low = call(add_norm_backward, normed, [d_middle] + es + [before])

    gradient, low, homes_m[0] = tie(gradient, low, homes_m[0])

    rest = (gradient - low.astype(F32)).astype(BF16)
    table_term = (dot_t(mixing, low) + dot_t(mixing, rest)).astype(BF16).reshape(len_high, 4, 256)
    table_term = table_term.transpose(1, 0, 2)
    mine = lax.dynamic_index_in_dim(table_term, deep, 0, keepdims=False).astype(F32)
    for k in range(1, 4):
        sent = lax.dynamic_index_in_dim(table_term, deep ^ k, 0, keepdims=False)
        mine = mine + over_fsdp(sent, 2 * k).astype(F32)
    mine = mine.astype(BF16)
    keep = jnp.where(core == 0, mine[:, :LANES], mine[:, LANES:])
    give = jnp.where(core == 0, mine[:, LANES:], mine[:, :LANES])
    d_table = square.total(keep.astype(F32) + over_fsdp(give, 1).astype(F32))

    homes_a[1] = square.spread(homes_a[1])
    x, y = square.swap(homes_m[0], 1), square.swap(homes_m[0], 2)
    homes_m[0] = [homes_m[0], x, y] + far_halves(x, y)
    big = [None] * 6
    (output,) = call(add_output, [(block, F32)], [late[0]] + late[1])
    for depth in reversed(range(layers)):
        pieces = homes_m[depth]
        prior = big[3:]
        names = [(w_up.shape, F32), (w_down.shape, F32), (gains_m.shape, F32)]
        args = [me1] + pieces + [w_up, gains_m]
        specs = [scalars()] + [None] * 5 + [layer_of(w_up, depth), layer_of(gains_m, depth)]
        extra = [] if prior[0] is None else prior
        big[3:] = call(
            finish_mlp,
            names,
            args + extra,
            specs + [pl.BlockSpec(memory_space=pl.ANY)] * len(extra),
            aliases={len(args) + t: t for t in range(len(extra))},
            out_specs=[layer_of(jax.ShapeDtypeStruct(s, d), depth) for s, d in names],
        )
        if depth == 0:
            homes_a[0], big, d_table, output = tie(homes_a[0], big, d_table, output)
            homes_a[0] = square.spread(homes_a[0])
        pieces = homes_a[depth]
        packed = [piece[:, 768:1024] for piece in pieces]
        odd_me = (me & 1) == 1
        even = [jnp.where(odd_me, packed[1], packed[0]), jnp.where(odd_me, packed[3], packed[2])]
        odd = [jnp.where(odd_me, packed[0], packed[1]), jnp.where(odd_me, packed[2], packed[3])]
        keep = [jnp.where(core == 0, a, b) for a, b in zip(even, odd)]
        give = jnp.stack([jnp.where(core == 0, b, a) for a, b in zip(even, odd)])
        got = over_fsdp(give, 1)
        high_me = head_side == 1
        keep = [jnp.where(high_me, keep[1], keep[0]), jnp.where(high_me, keep[0], keep[1])]
        got = [jnp.where(high_me, got[1], got[0]), jnp.where(high_me, got[0], got[1])]
        halves = []
        for h in range(2):
            halves.append(jnp.where(core == 0, keep[h], got[h]))
            halves.append(jnp.where(core == 0, got[h], keep[h]))
        outs = jnp.stack(halves)
        prior = big[:3]
        names = [(w_qkv.shape, F32), (w_out.shape, F32), (gains_a.shape, F32)]
        args = [me1] + pieces + [w_qkv, gains_a, outs]
        specs = [scalars()] + [None] * 4 + [layer_of(w_qkv, depth), layer_of(gains_a, depth), None]
        extra = [] if prior[0] is None else prior
        big[:3] = call(
            finish_attention,
            names,
            args + extra,
            specs + [pl.BlockSpec(memory_space=pl.ANY)] * len(extra),
            aliases={len(args) + t: t for t in range(len(extra))},
            out_specs=[layer_of(jax.ShapeDtypeStruct(s, d), depth) for s, d in names],
        )
    return (
        output,
        gradient,
        d_table,
        big[2].reshape(layers, LANES),
        big[0],
        big[1],
        big[5].reshape(layers, LANES),
        big[3],
        big[4],
    )


def solution(mesh):
    in_specs = (
        P(("dp", "fsdp"), None),
        P(None, "fsdp"),
        P(),
        P(),
        P(),
        P(None, "fsdp"),
        P(None, "fsdp", None),
        P(None, "fsdp", None),
        P(None, "fsdp"),
        P(None, "fsdp", None),
        P(None, "fsdp", None),
        P(("dp", "fsdp"), None),
    )
    out_specs = (
        P(("dp", "fsdp"), None),
        P(("dp", "fsdp"), None),
        P(None, "fsdp"),
        P(None, "fsdp"),
        P(None, "fsdp", None),
        P(None, "fsdp", None),
        P(None, "fsdp"),
        P(None, "fsdp", None),
        P(None, "fsdp", None),
    )
    fast = mesh.shape["dp"] == 4 and mesh.shape["fsdp"] == 8
    local = local_fast if fast else local_general
    return jax.shard_map(local, mesh=mesh, in_specs=in_specs, out_specs=out_specs, check_vma=False)
```

```python
import functools
import math

import jax
import jax.numpy as jnp
from jax import lax
from jax.experimental import pallas as pl
from jax.experimental.pallas import tpu as pltpu
from jax.sharding import PartitionSpec as P

HEADS = 16
EPS = 1e-06
NEG_FILL = -1e30
MIX_WEIGHTS = (0.5, 0.25, 0.125, 0.125)
BF16 = jnp.bfloat16
F32 = jnp.float32


def dot(a, b):
    return jnp.dot(a, b, preferred_element_type=F32)


def dot_t(a, b):
    return lax.dot_general(a, b, (((0,), (0,)), ((), ())), preferred_element_type=F32)


def dot_nt(a, b):
    return lax.dot_general(a, b, (((1,), (1,)), ((), ())), preferred_element_type=F32)


def normalize(hidden):
    center = hidden - jnp.mean(hidden, axis=-1, keepdims=True)
    rstd = lax.rsqrt(jnp.mean(center * center, axis=-1, keepdims=True) + EPS)
    return center * rstd, rstd


def norm_backward(e, xhat, rstd):
    return rstd * (
        e
        - jnp.mean(e, axis=-1, keepdims=True)
        - xhat * jnp.mean(e * xhat, axis=-1, keepdims=True)
    )


def gelu_exact(pre_act):
    return jax.nn.gelu(pre_act, approximate=False)


class Square:
    def __init__(self):
        self.count = lax.axis_size("dp")
        self.me = lax.axis_index("dp")
        self.pairs = self.count == 4

    def owners(self):
        if self.pairs:
            return [self.me ^ k for k in range(self.count)]
        return [jnp.int32(k) for k in range(self.count)]

    def swap(self, block, k):
        return lax.ppermute(block, "dp", [(i, i ^ k) for i in range(self.count)])

    def spread(self, block):
        if self.pairs:
            return [block] + [self.swap(block, k) for k in range(1, self.count)]
        full = lax.all_gather(block, "dp")
        return [full[k] for k in range(self.count)]

    def collect(self, parts):
        if self.pairs:
            total = parts[0].astype(F32)
            for k in range(1, self.count):
                total = total + self.swap(parts[k].astype(BF16), k).astype(F32)
            return total
        stacked = jnp.stack([part.astype(BF16) for part in parts])
        return lax.psum_scatter(stacked, "dp", scatter_dimension=0, tiled=False).astype(F32)

    def gather(self, piece):
        if not self.pairs:
            return lax.all_gather(piece, "dp")
        got = [piece] + [self.swap(piece, k) for k in range(1, self.count)]
        odd = (self.me & 1) == 1
        high = (self.me & 2) == 2
        low_pair = (jnp.where(odd, got[1], got[0]), jnp.where(odd, got[0], got[1]))
        far_pair = (jnp.where(odd, got[3], got[2]), jnp.where(odd, got[2], got[3]))
        return jnp.stack(
            [
                jnp.where(high, far_pair[0], low_pair[0]),
                jnp.where(high, far_pair[1], low_pair[1]),
                jnp.where(high, low_pair[0], far_pair[0]),
                jnp.where(high, low_pair[1], far_pair[1]),
            ]
        )

    def total(self, piece):
        if not self.pairs:
            return lax.psum(piece.astype(BF16), "dp").astype(F32)
        own = piece.astype(BF16)
        got = [own.astype(F32)] + [self.swap(own, k).astype(F32) for k in range(1, self.count)]
        return (got[0] + got[1]) + (got[2] + got[3])


def select(index, choices):
    out = choices[0]
    for k in range(1, len(choices)):
        out = jnp.where(index == k, choices[k], out)
    return out


def local_general(
    tokens,
    pos_table,
    index_lo,
    index_hi,
    resolution,
    gain_attn,
    w_qkv,
    w_out,
    gain_mlp,
    w_up,
    w_down,
    cotangent,
):
    row_count, width = tokens.shape
    layers, shard_rows, _ = w_qkv.shape
    hidden_units = w_up.shape[2]
    shard_count = lax.axis_size("fsdp")
    shard = lax.axis_index("fsdp")
    square = Square()
    group_count = square.count
    me = square.me
    head_size = width // HEADS
    my_heads = HEADS // group_count
    part = my_heads * head_size
    unit_part = hidden_units // group_count
    fine = square.pairs and shard_count * 2 == HEADS
    score_scale = 1.0 / math.sqrt(head_size)
    len_low = index_lo.shape[0]
    len_high = index_hi.shape[0]

    row_ids = jnp.arange(row_count, dtype=jnp.int32)

    def layout(flag):
        length = jnp.where(flag == 1, len_high, len_low).astype(jnp.int32)
        images = jnp.where(flag == 1, row_count // len_high, row_count // len_low).astype(jnp.int32)
        live = row_ids < images * length
        return live, jnp.where(live, row_ids // length, images)

    flag = resolution[me]
    live_rows, _ = layout(flag)
    block_ids = jnp.stack([layout(resolution[owner])[1] for owner in square.owners()])
    same_image = block_ids[:, :, None] == block_ids[:, None, :]
    picked = jnp.where(flag == 1, index_hi[row_ids % len_high], index_lo[row_ids % len_low])
    table_ids = jnp.arange(len_high, dtype=jnp.int32)
    mixing = jnp.zeros((row_count, len_high), F32)
    for slot in range(4):
        mixing = mixing + MIX_WEIGHTS[slot] * (
            picked[:, slot : slot + 1] == table_ids[None, :]
        ).astype(F32)
    mixing = (mixing * live_rows[:, None].astype(F32)).astype(BF16)
    high_groups = jnp.sum(resolution)
    tokens_low = (
        (group_count - high_groups) * shard_count * (row_count // len_low) * len_low
    ).astype(F32)
    tokens_high = (high_groups * shard_count * (row_count // len_high) * len_high).astype(F32)
    token_share = 2.0 * jnp.where(flag == 1, tokens_high, tokens_low) / (tokens_low + tokens_high)
    weight = jnp.where(live_rows, token_share, 0.0)

    half = shard_rows // 4
    core = shard % 2
    swap_core = [(j, j ^ 1) for j in range(shard_count)]
    pair_side, head_side = me & 1, (me >> 1) & 1

    def qkv_part(w):
        if fine:
            view = w.reshape(shard_rows, 3 * HEADS // 4, 2, 2, head_size)
            view = select(pair_side, [view[:, :, 0], view[:, :, 1]])
            view = select(head_side, [view[:, :, 0], view[:, :, 1]])
            return view.reshape(shard_rows, 3 * part)
        view = w.reshape(shard_rows, 3, group_count, part)
        return lax.dynamic_index_in_dim(view, me, 2, keepdims=False).reshape(shard_rows, 3 * part)

    def up_part(w):
        view = w.reshape(shard_rows, shard_count, group_count, unit_part // shard_count)
        return lax.dynamic_index_in_dim(view, me, 2, keepdims=False).reshape(shard_rows, unit_part)

    def down_part(w):
        rows = unit_part // shard_count
        return lax.dynamic_slice_in_dim(w, me * rows, rows, 0)

    def out_part(w):
        if fine:
            view = w.reshape(2, 2, half, width)
            mine = select(head_side, [view[0], view[1]])
            keep = select(core, [mine[0], mine[1]])
            give = select(core, [mine[1], mine[0]])
            got = lax.ppermute(give, "fsdp", swap_core)
            return jnp.where(core == pair_side, keep, got)
        return w

    def fetch(piece):
        return lax.all_gather(piece, "fsdp", axis=0, tiled=False)

    weights = []
    table = lax.all_gather(pos_table, "fsdp", axis=1, tiled=True)
    for depth in range(layers):
        gain_a = gain_attn[depth].astype(F32)[:, None]
        gain_m = gain_mlp[depth].astype(F32)[:, None]
        qkv = (qkv_part(w_qkv[depth]).astype(F32) * gain_a).astype(BF16)
        up = (up_part(w_up[depth]).astype(F32) * gain_m).astype(BF16)
        down = down_part(w_down[depth])
        out = out_part(w_out[depth])
        qkv_all = fetch(qkv).reshape(width, 3 * part)
        a = up.size // width
        b = a + down.shape[0]
        rest = fetch(jnp.concatenate([up.reshape(a, width), down, out], axis=0))
        up_all = rest[:, :a].reshape(width, unit_part)
        down_all = rest[:, a:b].reshape(unit_part, width)
        out_all = rest[:, b:].reshape(-1, width)
        if not fine:
            out_all = lax.dynamic_slice_in_dim(out_all, me * part, part, 0)
        weights.append((qkv_all, out_all, up_all, down_all))

    def split_heads(block):
        return block.reshape(group_count, row_count, my_heads, head_size)

    def scores_of(queries, key_rows):
        scores = (
            jnp.einsum("bqhd,bkhd->bhqk", queries, key_rows, preferred_element_type=F32)
            * score_scale
        )
        return jnp.where(same_image[:, None], scores, NEG_FILL)

    def spread(block):
        return jnp.concatenate(square.spread(block), axis=0)

    def collect(partial):
        return square.collect([partial[k * row_count : (k + 1) * row_count] for k in range(group_count)])

    hidden = tokens.astype(F32) + dot(mixing, table)
    saved = []
    for depth in range(layers):
        qkv_w, out_w, up_w, down_w = weights[depth]
        xhat_a, rstd_a = normalize(hidden)
        rows_a = spread(xhat_a.astype(BF16))
        projected = dot(rows_a, qkv_w).astype(BF16)
        queries = split_heads(projected[:, :part])
        key_rows = split_heads(projected[:, part : 2 * part])
        values = split_heads(projected[:, 2 * part :])
        scores = scores_of(queries, key_rows)
        row_max = jnp.max(scores, axis=-1, keepdims=True)
        powers = jnp.exp(scores - row_max)
        row_total = jnp.sum(powers, axis=-1, keepdims=True)
        log_total = row_max + jnp.log(row_total)
        probs = (powers / row_total).astype(BF16)
        attended = jnp.einsum("bhqk,bkhd->bqhd", probs, values, preferred_element_type=F32)
        attended = attended.reshape(group_count * row_count, part).astype(BF16)
        middle = hidden + collect(dot(attended, out_w).astype(BF16))
        xhat_m, rstd_m = normalize(middle)
        rows_m = spread(xhat_m.astype(BF16))
        pre_act = dot(rows_m, up_w)
        activated = gelu_exact(pre_act).astype(BF16)
        result = middle + collect(dot(activated, down_w).astype(BF16))
        saved.append(
            (xhat_a, rstd_a, rows_a, queries, key_rows, values, log_total, attended,
             xhat_m, rstd_m, rows_m, pre_act, activated)
        )
        hidden = result

    gradient = cotangent.astype(F32) * weight[:, None]
    shares = [None] * layers
    for depth in reversed(range(layers)):
        qkv_w, out_w, up_w, down_w = weights[depth]
        (xhat_a, rstd_a, rows_a, queries, key_rows, values, log_total, attended,
         xhat_m, rstd_m, rows_m, pre_act, activated) = saved[depth]
        d_result = spread(gradient.astype(BF16))
        grad_down = dot_t(activated, d_result).astype(BF16)
        d_activated = dot_nt(d_result, down_w)
        _, pullback = jax.vjp(gelu_exact, pre_act)
        d_pre = pullback(d_activated)[0].astype(BF16)
        grad_up = dot_t(rows_m, d_pre).astype(BF16)
        e = collect(dot_nt(d_pre, up_w).astype(BF16))
        d_middle = gradient + norm_backward(e, xhat_m, rstd_m)
        d_attn = spread(d_middle.astype(BF16))
        grad_out = dot_t(attended, d_attn).astype(BF16)
        d_attended = split_heads(dot_nt(d_attn, out_w).astype(BF16))
        probs = jnp.exp(scores_of(queries, key_rows) - log_total)
        d_values = jnp.einsum(
            "bhqk,bqhd->bkhd", probs.astype(BF16), d_attended, preferred_element_type=F32
        )
        d_probs = jnp.einsum("bqhd,bkhd->bhqk", d_attended, values, preferred_element_type=F32)
        centre = jnp.sum(probs * d_probs, axis=-1, keepdims=True)
        d_scores = (probs * (d_probs - centre)).astype(BF16)
        d_queries = (
            jnp.einsum("bhqk,bkhd->bqhd", d_scores, key_rows, preferred_element_type=F32)
            * score_scale
        )
        d_keys = (
            jnp.einsum("bhqk,bqhd->bkhd", d_scores, queries, preferred_element_type=F32)
            * score_scale
        )
        d_projected = jnp.concatenate(
            [x.astype(BF16).reshape(group_count * row_count, part) for x in (d_queries, d_keys, d_values)],
            axis=1,
        )
        grad_qkv = dot_t(rows_a, d_projected).astype(BF16)
        e = collect(dot_nt(d_projected, qkv_w).astype(BF16))
        gradient = d_middle + norm_backward(e, xhat_a, rstd_a)
        shares[depth] = (grad_qkv, grad_out, grad_up, grad_down)

    def home(term):
        return lax.psum_scatter(term, "fsdp", scatter_dimension=0, tiled=True)

    grads_qkv, grads_out, grads_up, grads_down, gains_a, gains_m = [], [], [], [], [], []
    for depth in reversed(range(layers)):
        grad_qkv, grad_out, grad_up, grad_down = shares[depth]
        rest = [
            grad_up.reshape(shard_count, -1, width),
            grad_down.reshape(shard_count, -1, width),
        ]
        if fine:
            rest.append(grad_out.reshape(shard_count, -1, width))
        else:
            full = jnp.zeros((width, width), BF16)
            full = lax.dynamic_update_slice_in_dim(full, grad_out, me * part, 0)
            rest.append(full.reshape(shard_count, -1, width))
        sizes = [x.shape[1] for x in rest]
        rest = home(jnp.concatenate(rest, axis=1))[0]
        qkv = square.gather(home(grad_qkv))
        if not fine:
            out = square.total(rest[sizes[0] + sizes[1] :])
            rest = rest[: sizes[0] + sizes[1]]
        rest = square.gather(rest)
        up = rest[:, : sizes[0]].reshape(group_count, shard_rows, shard_count, -1)
        up = up.transpose(1, 2, 0, 3).reshape(shard_rows, hidden_units).astype(F32)
        down = rest[:, sizes[0] : sizes[0] + sizes[1]].reshape(-1, width).astype(F32)
        if fine:
            pieces = rest[:, sizes[0] + sizes[1] :].reshape(2, 2, half, width)
            keep = select(core, [pieces[:, 0], pieces[:, 1]])
            give = select(core, [pieces[:, 1], pieces[:, 0]])
            got = lax.ppermute(give, "fsdp", swap_core)
            first = select(core, [keep, got])
            second = select(core, [got, keep])
            out = jnp.stack([first, second], axis=1).reshape(shard_rows, width).astype(F32)
            qkv = qkv.reshape(2, 2, shard_rows, 3 * my_heads, head_size).transpose(2, 3, 1, 0, 4)
        else:
            qkv = qkv.reshape(group_count, shard_rows, 3, part).transpose(1, 2, 0, 3)
        qkv = qkv.reshape(shard_rows, 3 * width).astype(F32)
        gains_a.append(jnp.sum(qkv * w_qkv[depth].astype(F32), axis=1))
        gains_m.append(jnp.sum(up * w_up[depth].astype(F32), axis=1))
        grads_qkv.append(qkv * gain_attn[depth].astype(F32)[:, None])
        grads_up.append(up * gain_mlp[depth].astype(F32)[:, None])
        grads_out.append(out)
        grads_down.append(down)

    high_part = gradient.astype(BF16)
    low_part = (gradient - high_part.astype(F32)).astype(BF16)
    table_term = dot_t(mixing, high_part) + dot_t(mixing, low_part)
    table_share = lax.psum_scatter(table_term.astype(BF16), "fsdp", scatter_dimension=1, tiled=True)
    d_table = square.total(table_share)
    return (
        hidden,
        gradient,
        d_table,
        jnp.stack(gains_a[::-1]),
        jnp.stack(grads_qkv[::-1]),
        jnp.stack(grads_out[::-1]),
        jnp.stack(gains_m[::-1]),
        jnp.stack(grads_up[::-1]),
        jnp.stack(grads_down[::-1]),
    )


VMEM = pltpu.VMEM
LANES = 128


def whole(shape):
    return pl.BlockSpec(tuple(shape), lambda *_: (0,) * len(shape))


def scalars():
    return pl.BlockSpec(memory_space=pltpu.SMEM)


def call(body, outs, args, specs=None, scratch=(), flops=0, reads=0, aliases=None, out_specs=None, limit=40, after=()):
    specs = [whole(a.shape) if s is None else s for a, s in zip(args, specs or [None] * len(args))]
    specs = specs + [pl.BlockSpec(memory_space=pl.ANY)] * len(after)
    count, extra = len(args), len(after)
    out_shape = [jax.ShapeDtypeStruct(shape, dtype) for shape, dtype in outs]
    moved = sum(math.prod(s) * jnp.dtype(d).itemsize for s, d in outs) + reads

    def run(*refs):
        body(*refs[:count], *refs[count + extra :])

    name = body.func.__name__ if isinstance(body, functools.partial) else body.__name__
    return pl.pallas_call(
        run,
        name=name,
        grid=(1,),
        in_specs=specs,
        out_specs=out_specs or [whole(shape) for shape, _ in outs],
        out_shape=out_shape,
        scratch_shapes=list(scratch),
        input_output_aliases=aliases or {},
        cost_estimate=pl.CostEstimate(flops=int(flops), bytes_accessed=int(moved), transcendentals=0),
        compiler_params=pltpu.CompilerParams(vmem_limit_bytes=limit << 20),
    )(*args, *after)


def diagonal(gain_row):
    r = lax.broadcasted_iota(jnp.int32, (LANES, LANES), 0)
    c = lax.broadcasted_iota(jnp.int32, (LANES, LANES), 1)
    return jnp.where(r == c, jnp.broadcast_to(gain_row.astype(F32), (LANES, LANES)), 0.0)


def lane_low(rows):
    return lax.broadcasted_iota(jnp.int32, (rows, LANES), 1) < LANES // 2


def lane_swap(block):
    return jnp.concatenate([block[:, LANES // 2 :], block[:, : LANES // 2]], axis=1)


def pack_attention(who_ref, w_ref, gain_row, keep, got, packed_ref, top):
    me, core = who_ref[0], who_ref[1]
    side, second = me & 1, me >> 1
    out = jnp.where(core == side, keep, got)
    diag = diagonal(gain_row).astype(BF16)
    low = lane_low(LANES)

    def head(t):
        chunk = pl.multiple_of(((t // 4) * 8 + 2 * (t % 4) + side) * LANES, LANES)
        got = dot(diag, w_ref[0, :, pl.ds(chunk, LANES)])
        turned = lane_swap(got)
        if t % 2 == 0:
            return jnp.where(second == 0, got, turned)
        return jnp.where(second == 0, turned, got)

    for u in range(6):
        pair = jnp.where(low, head(2 * u), head(2 * u + 1))
        packed_ref[top : top + LANES, u * LANES : (u + 1) * LANES] = pair.astype(BF16)
    for c in range(4):
        packed_ref[top + c * 32 : top + (c + 1) * 32, 768:1024] = out[:, c * 256 : (c + 1) * 256]


def pack_up(me, up_ref, gain_row, packed_ref, top):
    diag = diagonal(gain_row).astype(BF16)
    for j in range(8):
        chunk = pl.multiple_of((j * 4 + me) * LANES, LANES)
        packed_ref[top : top + LANES, j * LANES : (j + 1) * LANES] = dot(
            diag, up_ref[0, :, pl.ds(chunk, LANES)]
        ).astype(BF16)


def pack_down(me, down_ref, packed_ref, top):
    packed_ref[top : top + LANES, :] = down_ref[0, pl.ds(pl.multiple_of(me * LANES, LANES), LANES), :]


def prepare_first(who_ref, w_ref, gain_a, keep_ref, got_ref, up_ref, gain_m, packed_ref):
    pack_attention(who_ref, w_ref, gain_a[0:1, :], keep_ref[0], got_ref[0], packed_ref, 0)
    pack_up(who_ref[0], up_ref, gain_m[0:1, :], packed_ref, LANES)


def prepare_second(who_ref, w_ref, gain_a, keep_ref, got_ref, down_ref, packed_ref):
    pack_attention(who_ref, w_ref, gain_a[1:2, :], keep_ref[1], got_ref[1], packed_ref, LANES)
    pack_down(who_ref[0], down_ref, packed_ref, 0)


def prepare_third(who_ref, up_ref, gain_m, down_ref, packed_ref):
    pack_up(who_ref[0], up_ref, gain_m[1:2, :], packed_ref, 0)
    pack_down(who_ref[0], down_ref, packed_ref, LANES)


def image_numbers(rows, flag, lens):
    counts = [sum((rows >= t * n).astype(jnp.int32) for t in range(1, most + 1)) for n, most in lens]
    return jnp.where(flag == 1, counts[1], counts[0])


def make_mixing(flag_ref, low_ref, high_ref, mixing_ref, *, lens):
    rows = mixing_ref.shape[0]
    flag = flag_ref[0]

    def spread_rows(index_ref, length, most):
        count = index_ref.shape[0]
        columns = lax.broadcasted_iota(jnp.int32, (count, mixing_ref.shape[1]), 1)
        mix = jnp.zeros((count, mixing_ref.shape[1]), F32)
        for slot in range(4):
            mix = mix + MIX_WEIGHTS[slot] * (index_ref[:, slot : slot + 1] == columns).astype(F32)
        r = lax.broadcasted_iota(jnp.int32, (rows, count), 0)
        c = lax.broadcasted_iota(jnp.int32, (rows, count), 1)
        image = sum((r >= t * length).astype(jnp.int32) for t in range(1, most + 1))
        pick = ((r - image * length == c) & (r < most * length)).astype(BF16)
        return dot(pick, mix.astype(BF16))

    low = spread_rows(low_ref, *lens[0])
    high = spread_rows(high_ref, *lens[1])
    mixing_ref[...] = jnp.where(flag == 1, high, low).astype(BF16)


def write_norm(hidden, xhat_ref):
    xhat_ref[...] = normalize(hidden)[0].astype(BF16)


def join_table(z_ref, p0, p1, p2, p3, out_ref, table):
    for k, piece in enumerate((p0, p1, p2, p3)):
        table[:, pl.ds(pl.multiple_of((z_ref[0] ^ k) * 256, 256), 256)] = piece[...].astype(F32)
    out_ref[...] = table[...].astype(BF16)


def embed(who_ref, tokens_ref, mixing_ref, t0, t1, t2, t3, hidden_ref, xhat_ref, table):
    size = t0.shape[0]
    for k, piece in enumerate((t0, t1, t2, t3)):
        table[pl.ds(pl.multiple_of((who_ref[0] ^ k) * size, 8), size), :] = piece[...].astype(F32)
    rows = table[: mixing_ref.shape[1], :].astype(BF16)
    hidden = tokens_ref[...].astype(F32) + dot(mixing_ref[...], rows)
    hidden_ref[...] = hidden
    write_norm(hidden, xhat_ref)


def added(p0, r1, r2, r3):
    return (p0[...].astype(F32) + r1[...].astype(F32)) + (r2[...].astype(F32) + r3[...].astype(F32))


def add_norm(h_ref, p0, r1, r2, r3, middle_ref, xhat_ref):
    middle = h_ref[...] + added(p0, r1, r2, r3)
    middle_ref[...] = middle
    write_norm(middle, xhat_ref)


def add_output(h_ref, p0, r1, r2, r3, out_ref):
    out_ref[...] = h_ref[...] + added(p0, r1, r2, r3)


def add_norm_backward(g_ref, p0, r1, r2, r3, h_ref, d_ref, low_ref):
    d = g_ref[...] + norm_backward(added(p0, r1, r2, r3), *normalize(h_ref[...]))
    d_ref[...] = d
    low_ref[...] = d.astype(BF16)


def out_chunk(packed_ref, c):
    return packed_ref[:, c * 32 : (c + 1) * 32, 768:1024].reshape(256, 256)


def attention_forward(flag_ref, x_ref, w_ref, proj_ref, p_ref, *, lens):
    rows = x_ref.shape[0]
    flag = flag_ref[0]
    width = x_ref.shape[1]
    mask = image_numbers(lax.broadcasted_iota(jnp.int32, (rows, 1), 0), flag, lens) == image_numbers(
        lax.broadcasted_iota(jnp.int32, (1, rows), 1), flag, lens
    )
    for c in range(3):
        w = w_ref[:, :, c * 256 : (c + 1) * 256].reshape(width, 256)
        proj_ref[:, c * 256 : (c + 1) * 256] = dot(x_ref[...], w).astype(BF16)
    low = lane_low(rows)
    zero = jnp.zeros((), BF16)
    for u in range(2):
        q = proj_ref[:, u * LANES : (u + 1) * LANES] * jnp.asarray(0.125, BF16)
        k = proj_ref[:, 256 + u * LANES : 256 + (u + 1) * LANES]
        v = proj_ref[:, 512 + u * LANES : 512 + (u + 1) * LANES]
        total = None
        for keep in (low, ~low):
            s = dot_nt(jnp.where(keep, q, zero), k)
            s = jnp.where(mask, s, NEG_FILL)
            powers = jnp.exp(s - jnp.max(s, axis=-1, keepdims=True))
            probs = powers * (1.0 / jnp.sum(powers, axis=-1, keepdims=True))
            o = dot(probs.astype(BF16), jnp.where(keep, v, zero))
            total = o if total is None else total + o
        proj_ref[:, 768 + u * LANES : 768 + (u + 1) * LANES] = total.astype(BF16)
    for c in range(4):
        p_ref[:, c * 256 : (c + 1) * 256] = dot(proj_ref[:, 768:], out_chunk(w_ref, c)).astype(BF16)


def attention_backward(flag_ref, d_ref, proj_ref, w_ref, dproj_ref, p_ref, *, lens):
    rows, width = d_ref.shape
    flag = flag_ref[0]
    mask = image_numbers(lax.broadcasted_iota(jnp.int32, (rows, 1), 0), flag, lens) == image_numbers(
        lax.broadcasted_iota(jnp.int32, (1, rows), 1), flag, lens
    )
    d_o = sum(dot_nt(d_ref[:, c * 256 : (c + 1) * 256], out_chunk(w_ref, c)) for c in range(4))
    d_o = d_o.astype(BF16)
    low = lane_low(rows)
    zero = jnp.zeros((), BF16)
    scale = jnp.asarray(0.125, BF16)
    for u in range(2):
        q = proj_ref[:, u * LANES : (u + 1) * LANES] * scale
        k = proj_ref[:, 256 + u * LANES : 256 + (u + 1) * LANES]
        v = proj_ref[:, 512 + u * LANES : 512 + (u + 1) * LANES]
        g = d_o[:, u * LANES : (u + 1) * LANES]
        dq = dk = dv = None
        for keep in (low, ~low):
            k_own = jnp.where(keep, k, zero)
            s = jnp.where(mask, dot_nt(k_own, q), NEG_FILL)
            powers = jnp.exp(s - jnp.max(s, axis=0, keepdims=True))
            probs = powers * (1.0 / jnp.sum(powers, axis=0, keepdims=True))
            d_probs = dot_nt(jnp.where(keep, v, zero), g)
            centre = jnp.sum(probs * d_probs, axis=0, keepdims=True)
            d_scores = (probs * (d_probs - centre)).astype(BF16)
            terms = (
                dot_t(d_scores, k_own),
                dot(d_scores, jnp.where(keep, q, zero)),
                dot(probs.astype(BF16), jnp.where(keep, g, zero)),
            )
            dq, dk, dv = terms if dq is None else (dq + terms[0], dk + terms[1], dv + terms[2])
        dproj_ref[:, u * LANES : (u + 1) * LANES] = (dq * 0.125).astype(BF16)
        dproj_ref[:, 256 + u * LANES : 256 + (u + 1) * LANES] = dk.astype(BF16)
        dproj_ref[:, 512 + u * LANES : 512 + (u + 1) * LANES] = dv.astype(BF16)
    total = None
    for c in range(3):
        w = w_ref[:, :, c * 256 : (c + 1) * 256].reshape(width, 256)
        term = dot_nt(dproj_ref[:, c * 256 : (c + 1) * 256], w)
        total = term if total is None else total + term
    p_ref[...] = total.astype(BF16)


def gelu_parts(pre):
    upto = 0.5 * (1.0 + lax.erf(pre * math.sqrt(0.5)))
    density = jnp.exp(-0.5 * pre * pre) * (1.0 / math.sqrt(2.0 * math.pi))
    return pre * upto, upto + pre * density


def mlp_up(x_ref, up_ref, both_ref):
    width = x_ref.shape[1]
    for c in range(4):
        cols = slice(c * 256, (c + 1) * 256)
        act, slope = gelu_parts(dot(x_ref[...], up_ref[:, :, cols].reshape(width, 256)))
        both_ref[0, :, cols] = act.astype(BF16)
        both_ref[1, :, cols] = slope.astype(BF16)


def mlp_down(act_ref, down_ref, p_ref):
    width = p_ref.shape[1]
    p_ref[...] = dot(act_ref[0], down_ref[...].reshape(width, width)).astype(BF16)


def mlp_backward(d_ref, slope_ref, up_ref, down_ref, dpre_ref, p_ref):
    width = d_ref.shape[1]
    for c in range(4):
        cols = slice(c * 256, (c + 1) * 256)
        d_act = dot_nt(d_ref[...], down_ref[2 * c : 2 * c + 2].reshape(256, width))
        dpre_ref[:, cols] = (d_act * slope_ref[0, :, cols].astype(F32)).astype(BF16)
    p_ref[...] = dot_nt(dpre_ref[...], up_ref[...].reshape(width, width)).astype(BF16)


def mlp_both(x_ref, d_ref, up_ref, down_ref, act_ref, dpre_ref, p_ref, back_ref):
    width = x_ref.shape[1]
    for c in range(4):
        cols = slice(c * 256, (c + 1) * 256)
        act, slope = gelu_parts(dot(x_ref[...], up_ref[:, :, cols].reshape(width, 256)))
        act_ref[:, cols] = act.astype(BF16)
        d_act = dot_nt(d_ref[...], down_ref[2 * c : 2 * c + 2].reshape(256, width))
        dpre_ref[:, cols] = (d_act * slope).astype(BF16)
    back_ref[...] = dot_nt(dpre_ref[...], up_ref[...].reshape(width, width)).astype(BF16)
    p_ref[...] = dot(act_ref[...], down_ref[...].reshape(width, width)).astype(BF16)


def summed(left, right, rows, cols=slice(None)):
    total = None
    for a, b in zip(left, right):
        term = dot_t(a[:, rows], b[:, cols])
        total = term if total is None else total + term
    return total


def grads_mlp(*refs):
    x, dpre, act, d, out_ref = refs[:4], refs[4:8], refs[8:12], refs[12:16], refs[16]
    act = [a.at[0] if len(a.shape) == 3 else a for a in act]
    for half, (left, right) in enumerate(((x, dpre), (act, d))):
        for j in range(8):
            total = summed(left, right, slice(j * LANES, (j + 1) * LANES))
            out_ref[j, half * LANES : (half + 1) * LANES, :] = total.astype(BF16)


def grads_attention(*refs):
    x, dproj, kept, d, out_ref = refs[:4], refs[4:8], refs[8:12], refs[12:16], refs[16]
    for j in range(8):
        out_ref[j, :, :768] = summed(x, dproj, slice(j * LANES, (j + 1) * LANES)).astype(BF16)
    for c in range(4):
        total = summed(kept, d, slice(None), slice(c * 256, (c + 1) * 256))
        out_ref[:, c * 32 : (c + 1) * 32, 768:1024] = total.astype(BF16).reshape(8, 32, 256)


def rows_of(j):
    return pl.ds(pl.multiple_of(j * LANES, LANES), LANES)


def last_norm(z_ref, g_ref, p0, r1, r2, r3, h_ref, mixing_ref, d_ref, t0, t1, t2, t3, term_ref):
    d = g_ref[...] + norm_backward(added(p0, r1, r2, r3), *normalize(h_ref[...]))
    d_ref[...] = d
    high = d.astype(BF16)
    low = (d - high.astype(F32)).astype(BF16)
    term_ref[...] = dot_t(mixing_ref[...], high) + dot_t(mixing_ref[...], low)
    for k, out_ref in enumerate((t0, t1, t2, t3)):
        cols = pl.ds(pl.multiple_of((z_ref[0] ^ k) * 256, 256), 256)
        out_ref[...] = term_ref[:, cols].astype(BF16)


def table_halves(core_ref, t0, r1, r2, r3, keep_ref, give_ref):
    total = added(t0, r1, r2, r3).astype(BF16)
    first, second = total[:, :LANES], total[:, LANES:]
    keep_ref[...] = jnp.where(core_ref[0] == 0, first, second)
    give_ref[...] = jnp.where(core_ref[0] == 0, second, first)


def finish_mlp(me_ref, *refs, merged):
    g, up_ref, gain_ref, dup_ref, ddown_ref, dgain_ref = refs[:5], refs[5], refs[6], *refs[-3:]
    me = me_ref[0]
    low = 192 if merged else LANES
    column = jnp.sum(diagonal(gain_ref[0]), axis=1, keepdims=True)
    total = jnp.zeros((LANES, LANES), F32)
    downs = [piece[low : low + LANES, :] for piece in g[:3]] + [g[4][:LANES, :]]
    for k, piece in enumerate(downs):
        rows = pl.ds(pl.multiple_of((me ^ k) * LANES, LANES), LANES)
        ddown_ref[0, rows, :] = piece.astype(F32)
    ups = [piece[:LANES, :] for piece in g[:4]]
    for i in range(4):
        got = jnp.where(
            me == i, ups[0], jnp.where(me == i ^ 1, ups[1], jnp.where(me == i ^ 2, ups[2], ups[3]))
        ).astype(F32)
        for j in range(8):
            cols = slice((j * 4 + i) * LANES, (j * 4 + i + 1) * LANES)
            part = got[:, j * LANES : (j + 1) * LANES]
            dup_ref[0, :, cols] = part * column
            total = total + part * up_ref[0, :, cols].astype(F32)
    dgain_ref[0] = jnp.sum(total.T, axis=0, keepdims=True)


def attention_rows(refs):
    if len(refs) == 4:
        return [ref[...] for ref in refs]
    rows = [jnp.concatenate([ref[128:192, :], ref[320:384, :]], axis=0) for ref in refs[:3]]
    return rows + [jnp.concatenate([ref[128:192, :] for ref in refs[3:]], axis=0)]


def by_owner(me, pieces, i):
    g0, g1, g2, g3 = pieces
    return jnp.where(me == i, g0, jnp.where(me == i ^ 1, g1, jnp.where(me == i ^ 2, g2, g3)))


def split_out(who_ref, *refs):
    keep_ref, give_ref = refs[-2:]
    packed = [piece[:, 768:] for piece in attention_rows(refs[:-2])]
    me, core = who_ref[0], who_ref[1]
    for second in range(2):
        even, odd = by_owner(me, packed, 2 * second), by_owner(me, packed, 2 * second + 1)
        keep_ref[second] = jnp.where(core == 0, even, odd)
        give_ref[second] = jnp.where(core == 0, odd, even)


def finish_attention(who_ref, *refs, count):
    g, (w_ref, gain_ref, keep_ref, got_ref) = refs[:count], refs[count : count + 4]
    dqkv_ref, dout_ref, dgain_ref = refs[-3:]
    me, core = who_ref[0], who_ref[1]
    column = jnp.sum(diagonal(gain_ref[0]), axis=1, keepdims=True)
    total = jnp.zeros((LANES, LANES), F32)
    low = lane_low(LANES)
    rows = [piece[:, :768] for piece in attention_rows(g)]
    owned = [by_owner(me, rows, i).astype(F32) for i in range(4)]
    for t in range(12):
        u = t // 2
        for side in range(2):
            first = owned[side][:, u * LANES : (u + 1) * LANES]
            second = owned[side + 2][:, u * LANES : (u + 1) * LANES]
            if t % 2 == 0:
                part = jnp.where(low, first, lane_swap(second))
            else:
                part = jnp.where(low, lane_swap(first), second)
            chunk = (t // 4) * 8 + 2 * (t % 4) + side
            cols = slice(chunk * LANES, (chunk + 1) * LANES)
            dqkv_ref[0, :, cols] = part * column
            total = total + part * w_ref[0, :, cols].astype(F32)
    dgain_ref[0] = jnp.sum(total.T, axis=0, keepdims=True)
    for second in range(2):
        keep, got = keep_ref[second], got_ref[second]
        halves = (jnp.where(core == 0, keep, got), jnp.where(core == 0, got, keep))
        for h, part in enumerate(halves):
            for c in range(4):
                top = (2 * second + h) * 32
                dout_ref[0, top : top + 32, c * 256 : (c + 1) * 256] = part[c * 32 : (c + 1) * 32, :].astype(F32)


def local_fast(
    tokens,
    pos_table,
    index_lo,
    index_hi,
    resolution,
    gain_attn,
    w_qkv,
    w_out,
    gain_mlp,
    w_up,
    w_down,
    cotangent,
):
    rows, width = tokens.shape
    layers = w_qkv.shape[0]
    square = Square()
    me = square.me
    me1 = me.reshape(1).astype(jnp.int32)
    shard = lax.axis_index("fsdp")
    core, deep = shard % 2, shard // 2
    deep1 = deep.reshape(1).astype(jnp.int32)
    len_low, len_high = index_lo.shape[0], index_hi.shape[0]
    lens = ((len_low, rows // len_low), (len_high, rows // len_high))
    block = (rows, width)
    blocks = range(4)

    def over_fsdp(x, k):
        return lax.ppermute(x, "fsdp", [(j, j ^ k) for j in range(8)])

    def layer_of(array, depth):
        return pl.BlockSpec((1,) + array.shape[1:], lambda *_: (depth,) + (0,) * (array.ndim - 1))

    who = jnp.stack([me, core]).astype(jnp.int32)
    head_side = me >> 1

    def out_rows(half):
        return lax.dynamic_slice(w_out, (0, (head_side * 2 + half) * 32, 0), (layers, 32, width))

    keep, got = out_rows(core), over_fsdp(out_rows(1 - core), 1)
    gains_a = gain_attn.reshape(layers, 1, LANES)
    gains_m = gain_mlp.reshape(layers, 1, LANES)

    def part(top):
        return pl.BlockSpec((8, LANES, width), lambda *_: (0, top, 0))

    def fetch(body, args, specs, after=()):
        (packed,) = call(
            body, [((2 * LANES, width), BF16)], [who] + args, [scalars()] + specs, after=after, limit=60
        )
        return lax.all_gather(packed, "fsdp", axis=0, tiled=False)

    first_w = fetch(
        prepare_first,
        [w_qkv, gain_attn, keep, got, w_up, gain_mlp],
        [layer_of(w_qkv, 0), None, None, None, layer_of(w_up, 0), None],
    )

    flag = resolution[me]
    flag1 = flag.reshape(1)
    flags = [resolution[owner].reshape(1) for owner in square.owners()]
    shard_count, group_count = 8, resolution.shape[0]
    high_groups = jnp.sum(resolution)
    tokens_low = ((group_count - high_groups) * shard_count * lens[0][1] * len_low).astype(F32)
    tokens_high = (high_groups * shard_count * lens[1][1] * len_high).astype(F32)
    token_share = 2.0 * jnp.where(flag == 1, tokens_high, tokens_low) / (tokens_low + tokens_high)
    live = jnp.where(flag == 1, lens[1][1] * len_high, lens[0][1] * len_low)
    weight = jnp.where(jnp.arange(rows, dtype=jnp.int32) < live, token_share, 0.0)
    gradient = cotangent.astype(F32) * weight[:, None]

    normed = [(block, F32), (block, BF16)]
    size = -(-len_high // 32) * 8
    mine = lax.dynamic_slice(
        jnp.pad(pos_table, ((0, 4 * size - len_high), (0, 0))), (me * size, 0), (size, LANES)
    )
    other = over_fsdp(mine, 1)
    pair = jnp.concatenate([jnp.where(core == 0, mine, other), jnp.where(core == 0, other, mine)], axis=1)
    pieces = [pair] + [over_fsdp(pair, 2 * k) for k in range(1, 4)]
    (mine,) = call(
        join_table,
        [((size, width), BF16)],
        [deep1] + pieces,
        [scalars()] + [None] * 4,
        scratch=[VMEM((size, width), F32)],
    )
    (mixing,) = call(
        functools.partial(make_mixing, lens=lens),
        [((rows, len_high), BF16)],
        [flag1, index_lo, index_hi],
        [scalars(), None, None],
    )
    hidden, xhat = call(
        embed,
        normed,
        [who, tokens, mixing] + square.spread(mine),
        [scalars()] + [None] * 6,
        scratch=[VMEM((4 * size, width), F32)],
    )
    second_w = fetch(
        prepare_second,
        [w_qkv, gain_attn, keep, got, w_down],
        [layer_of(w_qkv, 1), None, None, None, layer_of(w_down, 0)],
        [xhat],
    )
    third_w = fetch(
        prepare_third,
        [w_up, gain_mlp, w_down],
        [layer_of(w_up, 1), None, layer_of(w_down, 1)],
        [xhat],
    )
    attn_w = [(first_w, part(0)), (second_w, part(1))]

    def tie(*values):
        return lax.optimization_barrier(values)

    def tie_last(es, term):
        near, term = tie(es[:3], term)
        far, near, term = tie(es[3], near, term)
        return near + [far], term

    def chain(kernel):
        done = []
        for k in blocks:
            done.append(kernel(k, [d[0] for d in done[-1:]]))
        return done

    def collect(parts):
        return [parts[0]] + [square.swap(parts[k], k) for k in range(1, 4)]

    d_top = square.spread(gradient.astype(BF16))
    saved = []
    for depth in range(layers):
        a_w, a_part = attn_w[depth]
        xs = square.spread(xhat)
        got = chain(
            lambda k, after: call(
                functools.partial(attention_forward, lens=lens),
                [(block, BF16)] * 2,
                [flags[k], xs[k], a_w],
                [scalars(), None, a_part],
                after=after,
            )
        )
        kept = [g[0] for g in got]
        es = collect([g[1] for g in got])
        if depth == 0:
            es, d_top = tie(es, d_top)
        before, (middle, xhat) = hidden, call(add_norm, normed, [hidden] + es)
        ms = square.spread(xhat)
        if depth < layers - 1:
            acts = chain(
                lambda k, after: call(
                    mlp_up, [((2,) + block, BF16)], [ms[k], first_w], [None, part(1)], after=after
                )
            )
            acts = [a[0] for a in acts]
            parts = [None] * 4
            last = acts
            for k in (1, 2, 3, 0):
                (parts[k],) = call(
                    mlp_down, [(block, BF16)], [acts[k], second_w], [None, part(0)], after=last
                )
                last = [parts[k]]
            saved.append((before, xs, kept, middle, ms, acts))
            hidden, xhat = call(add_norm, normed, [middle] + collect(parts))
        else:
            got = chain(
                lambda k, after: call(
                    mlp_both,
                    [(block, BF16)] * 4,
                    [ms[k], d_top[k], third_w, third_w],
                    [None, None, part(0), part(1)],
                    after=after,
                )
            )
            acts, dpres, output_parts, backs = ([g[t] for g in got] for t in range(4))
            saved.append((before, xs, kept, middle, ms, acts))

    def far_halves(x, y):
        half = x.shape[0] // 2
        return [square.swap(x[:half], 2), square.swap(y[half:], 1)]

    core1 = core.reshape(1).astype(jnp.int32)

    def home(term):
        return lax.psum_scatter(term, "fsdp", scatter_dimension=0, tiled=False)

    homes_m, homes_a = [None] * layers, [None] * layers
    for depth in reversed(range(layers)):
        top = depth == layers - 1
        a_w, a_part = attn_w[depth]
        before, xs, kept, middle, ms, acts = saved[depth]
        ds = d_top if top else square.spread(low)
        if not top:
            second_half = pl.BlockSpec((1,) + block, lambda *_: (1, 0, 0))
            got = chain(
                lambda k, after: call(
                    mlp_backward,
                    [(block, BF16)] * 2,
                    [ds[k], acts[k], first_w, second_w],
                    [None, second_half, part(1), part(0)],
                    after=after or late[1][1:] + [homes_m[1]],
                )
            )
            dpres, backs = ([g[t] for g in got] for t in range(2))
        es = collect(backs)
        first_half = pl.BlockSpec((1,) + block, lambda *_: (0, 0, 0))
        (term,) = call(
            grads_mlp,
            [((8, 2 * LANES, width), BF16)],
            list(ms) + list(dpres) + list(acts) + list(ds),
            [None] * 8 + [None if top else first_half] * 4 + [None] * 4,
        )
        es, term = tie_last(es, term)
        homes_m[depth] = home(term)
        d_middle, low = call(add_norm_backward, normed, [gradient] + es + [middle], limit=60)
        if not top:
            m, a = homes_m[1], homes_a[1]
            merged = jnp.concatenate([m[:LANES], a[:64], m[LANES:], a[64:]], axis=0)
        ds = square.spread(low)
        got = chain(
            lambda k, after: call(
                functools.partial(attention_backward, lens=lens),
                [((rows, 768), BF16), (block, BF16)],
                [flags[k], ds[k], kept[k], a_w],
                [scalars(), None, None, a_part],
                after=after or ([] if top else [merged]),
            )
        )
        dprojs = [g[0] for g in got]
        es = collect([g[1] for g in got])
        if top:
            outs = collect(output_parts)
        out_part = pl.BlockSpec((rows, 256), lambda *_: (0, 3))
        operands = list(xs) + dprojs + list(kept) + list(ds)
        specs = [None] * 8 + [out_part] * 4 + [None] * 4
        if top:
            (term,) = call(grads_attention, [((8, LANES, width), BF16)], operands, specs)
            es, term = tie_last(es, term)
            homes_a[depth] = home(term)
            late = (middle, outs)
            gradient, low = call(add_norm_backward, normed, [d_middle] + es + [before], limit=60)
        else:
            near = [square.swap(merged, 1), square.swap(merged, 2)]
            (term,) = call(grads_attention, [((8, LANES, width), BF16)], operands, specs, after=near)
            es, term = tie_last(es, term)
            homes_a[0] = home(term)
            gradient, *tables = call(
                last_norm,
                [(block, F32)] + [((len_high, 256), BF16)] * 4,
                [deep1, d_middle] + es + [before, mixing],
                [scalars()] + [None] * 7,
                scratch=[VMEM((len_high, width), F32)],
            )

    merged = [merged, *near] + far_halves(*near)

    tables = [tables[0]] + [over_fsdp(tables[k], 2 * k) for k in range(1, 4)]
    keep, give = call(table_halves, [((len_high, LANES), BF16)] * 2, [core1] + tables, [scalars()] + [None] * 4)
    d_table = square.total(keep.astype(F32) + over_fsdp(give, 1).astype(F32))

    (output,) = call(add_output, [(block, F32)], [late[0]] + late[1], after=tables[:1])
    homes_m[0], _ = tie(homes_m[0], tables[0])
    x, y = square.swap(homes_m[0], 1), square.swap(homes_m[0], 2)
    homes_m[0] = [homes_m[0], x, y] + far_halves(x, y)
    big = [None] * 6

    def finish(body, depth, args, shapes, prior):
        extra = [] if prior[0] is None else prior
        specs = [layer_of(a, depth) if a is w_up or a is w_qkv or a is gains_a or a is gains_m else None for a in args]
        return call(
            body,
            [(shape, F32) for shape in shapes],
            [who] + args + extra,
            [scalars()] + specs + [pl.BlockSpec(memory_space=pl.ANY)] * len(extra),
            aliases={1 + len(args) + t: t for t in range(len(extra))},
            out_specs=[layer_of(jax.ShapeDtypeStruct(shape, F32), depth) for shape in shapes],
        )

    def finish_m(depth, pieces):
        shapes = [w_up.shape, w_down.shape, gains_m.shape]
        body = functools.partial(finish_mlp, merged=depth > 0)
        big[3:] = finish(body, depth, pieces + [w_up, gains_m], shapes, big[3:])

    def finish_a(depth, pieces):
        keep, give = call(
            split_out, [((2, LANES, 256), BF16)] * 2, [who] + pieces, [scalars()] + [None] * len(pieces)
        )
        shapes = [w_qkv.shape, w_out.shape, gains_a.shape]
        body = functools.partial(finish_attention, count=len(pieces))
        args = pieces + [w_qkv, gains_a, keep, over_fsdp(give, 1)]
        big[:3] = finish(body, depth, args, shapes, big[:3])

    homes_a[0], homes_m[0], merged, d_table, output = tie(homes_a[0], homes_m[0], merged, d_table, output)
    pieces = square.spread(homes_a[0])
    finish_m(1, merged)
    finish_a(1, merged)
    finish_m(0, homes_m[0])
    pieces, big = tie(pieces, big)
    finish_a(0, pieces)
    return (
        output,
        gradient,
        d_table,
        big[2].reshape(layers, LANES),
        big[0],
        big[1],
        big[5].reshape(layers, LANES),
        big[3],
        big[4],
    )


def solution(mesh):
    in_specs = (
        P(("dp", "fsdp"), None),
        P(None, "fsdp"),
        P(),
        P(),
        P(),
        P(None, "fsdp"),
        P(None, "fsdp", None),
        P(None, "fsdp", None),
        P(None, "fsdp"),
        P(None, "fsdp", None),
        P(None, "fsdp", None),
        P(("dp", "fsdp"), None),
    )
    out_specs = (
        P(("dp", "fsdp"), None),
        P(("dp", "fsdp"), None),
        P(None, "fsdp"),
        P(None, "fsdp"),
        P(None, "fsdp", None),
        P(None, "fsdp", None),
        P(None, "fsdp"),
        P(None, "fsdp", None),
        P(None, "fsdp", None),
    )
    fast = mesh.shape["dp"] == 4 and mesh.shape["fsdp"] == 8
    local = local_fast if fast else local_general
    return jax.shard_map(local, mesh=mesh, in_specs=in_specs, out_specs=out_specs, check_vma=False)
```

```python
import functools
import math

import jax
import jax.numpy as jnp
from jax import lax
from jax.experimental import pallas as pl
from jax.experimental.pallas import tpu as pltpu
from jax.sharding import PartitionSpec as P

HEADS = 16
EPS = 1e-06
NEG_FILL = -1e30
MIX_WEIGHTS = (0.5, 0.25, 0.125, 0.125)
BF16 = jnp.bfloat16
F32 = jnp.float32


def dot(a, b):
    return jnp.dot(a, b, preferred_element_type=F32)


def dot_t(a, b):
    return lax.dot_general(a, b, (((0,), (0,)), ((), ())), preferred_element_type=F32)


def dot_nt(a, b):
    return lax.dot_general(a, b, (((1,), (1,)), ((), ())), preferred_element_type=F32)


def normalize(hidden):
    center = hidden - jnp.mean(hidden, axis=-1, keepdims=True)
    rstd = lax.rsqrt(jnp.mean(center * center, axis=-1, keepdims=True) + EPS)
    return center * rstd, rstd


def norm_backward(e, xhat, rstd):
    return rstd * (
        e
        - jnp.mean(e, axis=-1, keepdims=True)
        - xhat * jnp.mean(e * xhat, axis=-1, keepdims=True)
    )


def gelu_exact(pre_act):
    return jax.nn.gelu(pre_act, approximate=False)


class Square:
    def __init__(self):
        self.count = lax.axis_size("dp")
        self.me = lax.axis_index("dp")
        self.pairs = self.count == 4

    def owners(self):
        if self.pairs:
            return [self.me ^ k for k in range(self.count)]
        return [jnp.int32(k) for k in range(self.count)]

    def swap(self, block, k):
        return lax.ppermute(block, "dp", [(i, i ^ k) for i in range(self.count)])

    def spread(self, block):
        if self.pairs:
            return [block] + [self.swap(block, k) for k in range(1, self.count)]
        full = lax.all_gather(block, "dp")
        return [full[k] for k in range(self.count)]

    def collect(self, parts):
        if self.pairs:
            total = parts[0].astype(F32)
            for k in range(1, self.count):
                total = total + self.swap(parts[k].astype(BF16), k).astype(F32)
            return total
        stacked = jnp.stack([part.astype(BF16) for part in parts])
        return lax.psum_scatter(stacked, "dp", scatter_dimension=0, tiled=False).astype(F32)

    def gather(self, piece):
        if not self.pairs:
            return lax.all_gather(piece, "dp")
        got = [piece] + [self.swap(piece, k) for k in range(1, self.count)]
        odd = (self.me & 1) == 1
        high = (self.me & 2) == 2
        low_pair = (jnp.where(odd, got[1], got[0]), jnp.where(odd, got[0], got[1]))
        far_pair = (jnp.where(odd, got[3], got[2]), jnp.where(odd, got[2], got[3]))
        return jnp.stack(
            [
                jnp.where(high, far_pair[0], low_pair[0]),
                jnp.where(high, far_pair[1], low_pair[1]),
                jnp.where(high, low_pair[0], far_pair[0]),
                jnp.where(high, low_pair[1], far_pair[1]),
            ]
        )

    def total(self, piece):
        if not self.pairs:
            return lax.psum(piece.astype(BF16), "dp").astype(F32)
        own = piece.astype(BF16)
        got = [own.astype(F32)] + [self.swap(own, k).astype(F32) for k in range(1, self.count)]
        return (got[0] + got[1]) + (got[2] + got[3])


def select(index, choices):
    out = choices[0]
    for k in range(1, len(choices)):
        out = jnp.where(index == k, choices[k], out)
    return out


def local_general(
    tokens,
    pos_table,
    index_lo,
    index_hi,
    resolution,
    gain_attn,
    w_qkv,
    w_out,
    gain_mlp,
    w_up,
    w_down,
    cotangent,
):
    row_count, width = tokens.shape
    layers, shard_rows, _ = w_qkv.shape
    hidden_units = w_up.shape[2]
    shard_count = lax.axis_size("fsdp")
    shard = lax.axis_index("fsdp")
    square = Square()
    group_count = square.count
    me = square.me
    head_size = width // HEADS
    my_heads = HEADS // group_count
    part = my_heads * head_size
    unit_part = hidden_units // group_count
    fine = square.pairs and shard_count * 2 == HEADS
    score_scale = 1.0 / math.sqrt(head_size)
    len_low = index_lo.shape[0]
    len_high = index_hi.shape[0]

    row_ids = jnp.arange(row_count, dtype=jnp.int32)

    def layout(flag):
        length = jnp.where(flag == 1, len_high, len_low).astype(jnp.int32)
        images = jnp.where(flag == 1, row_count // len_high, row_count // len_low).astype(jnp.int32)
        live = row_ids < images * length
        return live, jnp.where(live, row_ids // length, images)

    flag = resolution[me]
    live_rows, _ = layout(flag)
    block_ids = jnp.stack([layout(resolution[owner])[1] for owner in square.owners()])
    same_image = block_ids[:, :, None] == block_ids[:, None, :]
    picked = jnp.where(flag == 1, index_hi[row_ids % len_high], index_lo[row_ids % len_low])
    table_ids = jnp.arange(len_high, dtype=jnp.int32)
    mixing = jnp.zeros((row_count, len_high), F32)
    for slot in range(4):
        mixing = mixing + MIX_WEIGHTS[slot] * (
            picked[:, slot : slot + 1] == table_ids[None, :]
        ).astype(F32)
    mixing = (mixing * live_rows[:, None].astype(F32)).astype(BF16)
    high_groups = jnp.sum(resolution)
    tokens_low = (
        (group_count - high_groups) * shard_count * (row_count // len_low) * len_low
    ).astype(F32)
    tokens_high = (high_groups * shard_count * (row_count // len_high) * len_high).astype(F32)
    token_share = 2.0 * jnp.where(flag == 1, tokens_high, tokens_low) / (tokens_low + tokens_high)
    weight = jnp.where(live_rows, token_share, 0.0)

    half = shard_rows // 4
    core = shard % 2
    swap_core = [(j, j ^ 1) for j in range(shard_count)]
    pair_side, head_side = me & 1, (me >> 1) & 1

    def qkv_part(w):
        if fine:
            view = w.reshape(shard_rows, 3 * HEADS // 4, 2, 2, head_size)
            view = select(pair_side, [view[:, :, 0], view[:, :, 1]])
            view = select(head_side, [view[:, :, 0], view[:, :, 1]])
            return view.reshape(shard_rows, 3 * part)
        view = w.reshape(shard_rows, 3, group_count, part)
        return lax.dynamic_index_in_dim(view, me, 2, keepdims=False).reshape(shard_rows, 3 * part)

    def up_part(w):
        view = w.reshape(shard_rows, shard_count, group_count, unit_part // shard_count)
        return lax.dynamic_index_in_dim(view, me, 2, keepdims=False).reshape(shard_rows, unit_part)

    def down_part(w):
        rows = unit_part // shard_count
        return lax.dynamic_slice_in_dim(w, me * rows, rows, 0)

    def out_part(w):
        if fine:
            view = w.reshape(2, 2, half, width)
            mine = select(head_side, [view[0], view[1]])
            keep = select(core, [mine[0], mine[1]])
            give = select(core, [mine[1], mine[0]])
            got = lax.ppermute(give, "fsdp", swap_core)
            return jnp.where(core == pair_side, keep, got)
        return w

    def fetch(piece):
        return lax.all_gather(piece, "fsdp", axis=0, tiled=False)

    weights = []
    table = lax.all_gather(pos_table, "fsdp", axis=1, tiled=True)
    for depth in range(layers):
        gain_a = gain_attn[depth].astype(F32)[:, None]
        gain_m = gain_mlp[depth].astype(F32)[:, None]
        qkv = (qkv_part(w_qkv[depth]).astype(F32) * gain_a).astype(BF16)
        up = (up_part(w_up[depth]).astype(F32) * gain_m).astype(BF16)
        down = down_part(w_down[depth])
        out = out_part(w_out[depth])
        qkv_all = fetch(qkv).reshape(width, 3 * part)
        a = up.size // width
        b = a + down.shape[0]
        rest = fetch(jnp.concatenate([up.reshape(a, width), down, out], axis=0))
        up_all = rest[:, :a].reshape(width, unit_part)
        down_all = rest[:, a:b].reshape(unit_part, width)
        out_all = rest[:, b:].reshape(-1, width)
        if not fine:
            out_all = lax.dynamic_slice_in_dim(out_all, me * part, part, 0)
        weights.append((qkv_all, out_all, up_all, down_all))

    def split_heads(block):
        return block.reshape(group_count, row_count, my_heads, head_size)

    def scores_of(queries, key_rows):
        scores = (
            jnp.einsum("bqhd,bkhd->bhqk", queries, key_rows, preferred_element_type=F32)
            * score_scale
        )
        return jnp.where(same_image[:, None], scores, NEG_FILL)

    def spread(block):
        return jnp.concatenate(square.spread(block), axis=0)

    def collect(partial):
        return square.collect([partial[k * row_count : (k + 1) * row_count] for k in range(group_count)])

    hidden = tokens.astype(F32) + dot(mixing, table)
    saved = []
    for depth in range(layers):
        qkv_w, out_w, up_w, down_w = weights[depth]
        xhat_a, rstd_a = normalize(hidden)
        rows_a = spread(xhat_a.astype(BF16))
        projected = dot(rows_a, qkv_w).astype(BF16)
        queries = split_heads(projected[:, :part])
        key_rows = split_heads(projected[:, part : 2 * part])
        values = split_heads(projected[:, 2 * part :])
        scores = scores_of(queries, key_rows)
        row_max = jnp.max(scores, axis=-1, keepdims=True)
        powers = jnp.exp(scores - row_max)
        row_total = jnp.sum(powers, axis=-1, keepdims=True)
        log_total = row_max + jnp.log(row_total)
        probs = (powers / row_total).astype(BF16)
        attended = jnp.einsum("bhqk,bkhd->bqhd", probs, values, preferred_element_type=F32)
        attended = attended.reshape(group_count * row_count, part).astype(BF16)
        middle = hidden + collect(dot(attended, out_w).astype(BF16))
        xhat_m, rstd_m = normalize(middle)
        rows_m = spread(xhat_m.astype(BF16))
        pre_act = dot(rows_m, up_w)
        activated = gelu_exact(pre_act).astype(BF16)
        result = middle + collect(dot(activated, down_w).astype(BF16))
        saved.append(
            (xhat_a, rstd_a, rows_a, queries, key_rows, values, log_total, attended,
             xhat_m, rstd_m, rows_m, pre_act, activated)
        )
        hidden = result

    gradient = cotangent.astype(F32) * weight[:, None]
    shares = [None] * layers
    for depth in reversed(range(layers)):
        qkv_w, out_w, up_w, down_w = weights[depth]
        (xhat_a, rstd_a, rows_a, queries, key_rows, values, log_total, attended,
         xhat_m, rstd_m, rows_m, pre_act, activated) = saved[depth]
        d_result = spread(gradient.astype(BF16))
        grad_down = dot_t(activated, d_result).astype(BF16)
        d_activated = dot_nt(d_result, down_w)
        _, pullback = jax.vjp(gelu_exact, pre_act)
        d_pre = pullback(d_activated)[0].astype(BF16)
        grad_up = dot_t(rows_m, d_pre).astype(BF16)
        e = collect(dot_nt(d_pre, up_w).astype(BF16))
        d_middle = gradient + norm_backward(e, xhat_m, rstd_m)
        d_attn = spread(d_middle.astype(BF16))
        grad_out = dot_t(attended, d_attn).astype(BF16)
        d_attended = split_heads(dot_nt(d_attn, out_w).astype(BF16))
        probs = jnp.exp(scores_of(queries, key_rows) - log_total)
        d_values = jnp.einsum(
            "bhqk,bqhd->bkhd", probs.astype(BF16), d_attended, preferred_element_type=F32
        )
        d_probs = jnp.einsum("bqhd,bkhd->bhqk", d_attended, values, preferred_element_type=F32)
        centre = jnp.sum(probs * d_probs, axis=-1, keepdims=True)
        d_scores = (probs * (d_probs - centre)).astype(BF16)
        d_queries = (
            jnp.einsum("bhqk,bkhd->bqhd", d_scores, key_rows, preferred_element_type=F32)
            * score_scale
        )
        d_keys = (
            jnp.einsum("bhqk,bqhd->bkhd", d_scores, queries, preferred_element_type=F32)
            * score_scale
        )
        d_projected = jnp.concatenate(
            [x.astype(BF16).reshape(group_count * row_count, part) for x in (d_queries, d_keys, d_values)],
            axis=1,
        )
        grad_qkv = dot_t(rows_a, d_projected).astype(BF16)
        e = collect(dot_nt(d_projected, qkv_w).astype(BF16))
        gradient = d_middle + norm_backward(e, xhat_a, rstd_a)
        shares[depth] = (grad_qkv, grad_out, grad_up, grad_down)

    def home(term):
        return lax.psum_scatter(term, "fsdp", scatter_dimension=0, tiled=True)

    grads_qkv, grads_out, grads_up, grads_down, gains_a, gains_m = [], [], [], [], [], []
    for depth in reversed(range(layers)):
        grad_qkv, grad_out, grad_up, grad_down = shares[depth]
        rest = [
            grad_up.reshape(shard_count, -1, width),
            grad_down.reshape(shard_count, -1, width),
        ]
        if fine:
            rest.append(grad_out.reshape(shard_count, -1, width))
        else:
            full = jnp.zeros((width, width), BF16)
            full = lax.dynamic_update_slice_in_dim(full, grad_out, me * part, 0)
            rest.append(full.reshape(shard_count, -1, width))
        sizes = [x.shape[1] for x in rest]
        rest = home(jnp.concatenate(rest, axis=1))[0]
        qkv = square.gather(home(grad_qkv))
        if not fine:
            out = square.total(rest[sizes[0] + sizes[1] :])
            rest = rest[: sizes[0] + sizes[1]]
        rest = square.gather(rest)
        up = rest[:, : sizes[0]].reshape(group_count, shard_rows, shard_count, -1)
        up = up.transpose(1, 2, 0, 3).reshape(shard_rows, hidden_units).astype(F32)
        down = rest[:, sizes[0] : sizes[0] + sizes[1]].reshape(-1, width).astype(F32)
        if fine:
            pieces = rest[:, sizes[0] + sizes[1] :].reshape(2, 2, half, width)
            keep = select(core, [pieces[:, 0], pieces[:, 1]])
            give = select(core, [pieces[:, 1], pieces[:, 0]])
            got = lax.ppermute(give, "fsdp", swap_core)
            first = select(core, [keep, got])
            second = select(core, [got, keep])
            out = jnp.stack([first, second], axis=1).reshape(shard_rows, width).astype(F32)
            qkv = qkv.reshape(2, 2, shard_rows, 3 * my_heads, head_size).transpose(2, 3, 1, 0, 4)
        else:
            qkv = qkv.reshape(group_count, shard_rows, 3, part).transpose(1, 2, 0, 3)
        qkv = qkv.reshape(shard_rows, 3 * width).astype(F32)
        gains_a.append(jnp.sum(qkv * w_qkv[depth].astype(F32), axis=1))
        gains_m.append(jnp.sum(up * w_up[depth].astype(F32), axis=1))
        grads_qkv.append(qkv * gain_attn[depth].astype(F32)[:, None])
        grads_up.append(up * gain_mlp[depth].astype(F32)[:, None])
        grads_out.append(out)
        grads_down.append(down)

    high_part = gradient.astype(BF16)
    low_part = (gradient - high_part.astype(F32)).astype(BF16)
    table_term = dot_t(mixing, high_part) + dot_t(mixing, low_part)
    table_share = lax.psum_scatter(table_term.astype(BF16), "fsdp", scatter_dimension=1, tiled=True)
    d_table = square.total(table_share)
    return (
        hidden,
        gradient,
        d_table,
        jnp.stack(gains_a[::-1]),
        jnp.stack(grads_qkv[::-1]),
        jnp.stack(grads_out[::-1]),
        jnp.stack(gains_m[::-1]),
        jnp.stack(grads_up[::-1]),
        jnp.stack(grads_down[::-1]),
    )


VMEM = pltpu.VMEM
LANES = 128


def whole(shape):
    return pl.BlockSpec(tuple(shape), lambda *_: (0,) * len(shape))


def scalars():
    return pl.BlockSpec(memory_space=pltpu.SMEM)


def call(body, outs, args, specs=None, scratch=(), flops=0, reads=0, aliases=None, out_specs=None, limit=40, after=()):
    specs = [whole(a.shape) if s is None else s for a, s in zip(args, specs or [None] * len(args))]
    specs = specs + [pl.BlockSpec(memory_space=pl.ANY)] * len(after)
    count, extra = len(args), len(after)
    out_shape = [jax.ShapeDtypeStruct(shape, dtype) for shape, dtype in outs]
    moved = sum(math.prod(s) * jnp.dtype(d).itemsize for s, d in outs) + reads

    def run(*refs):
        body(*refs[:count], *refs[count + extra :])

    name = body.func.__name__ if isinstance(body, functools.partial) else body.__name__
    return pl.pallas_call(
        run,
        name=name,
        grid=(1,),
        in_specs=specs,
        out_specs=out_specs or [whole(shape) for shape, _ in outs],
        out_shape=out_shape,
        scratch_shapes=list(scratch),
        input_output_aliases=aliases or {},
        cost_estimate=pl.CostEstimate(flops=int(flops), bytes_accessed=int(moved), transcendentals=0),
        compiler_params=pltpu.CompilerParams(vmem_limit_bytes=limit << 20),
    )(*args, *after)


def diagonal(gain_row):
    r = lax.broadcasted_iota(jnp.int32, (LANES, LANES), 0)
    c = lax.broadcasted_iota(jnp.int32, (LANES, LANES), 1)
    return jnp.where(r == c, jnp.broadcast_to(gain_row.astype(F32), (LANES, LANES)), 0.0)


def lane_low(rows):
    return lax.broadcasted_iota(jnp.int32, (rows, LANES), 1) < LANES // 2


def lane_swap(block):
    return jnp.concatenate([block[:, LANES // 2 :], block[:, : LANES // 2]], axis=1)


def pack_attention(who_ref, w_ref, gain_row, keep, got, packed_ref, top):
    me, core = who_ref[0], who_ref[1]
    side, second = me & 1, me >> 1
    out = jnp.where(core == side, keep, got)
    diag = diagonal(gain_row).astype(BF16)
    low = lane_low(LANES)

    def head(t):
        chunk = pl.multiple_of(((t // 4) * 8 + 2 * (t % 4) + side) * LANES, LANES)
        got = dot(diag, w_ref[0, :, pl.ds(chunk, LANES)])
        turned = lane_swap(got)
        if t % 2 == 0:
            return jnp.where(second == 0, got, turned)
        return jnp.where(second == 0, turned, got)

    for u in range(6):
        pair = jnp.where(low, head(2 * u), head(2 * u + 1))
        packed_ref[top : top + LANES, u * LANES : (u + 1) * LANES] = pair.astype(BF16)
    for c in range(4):
        packed_ref[top + c * 32 : top + (c + 1) * 32, 768:1024] = out[:, c * 256 : (c + 1) * 256]


def pack_up(me, up_ref, gain_row, packed_ref, top):
    diag = diagonal(gain_row).astype(BF16)
    for j in range(8):
        chunk = pl.multiple_of((j * 4 + me) * LANES, LANES)
        packed_ref[top : top + LANES, j * LANES : (j + 1) * LANES] = dot(
            diag, up_ref[0, :, pl.ds(chunk, LANES)]
        ).astype(BF16)


def pack_down(me, down_ref, packed_ref, top):
    packed_ref[top : top + LANES, :] = down_ref[0, pl.ds(pl.multiple_of(me * LANES, LANES), LANES), :]


def prepare_first(who_ref, w_ref, gain_a, keep_ref, got_ref, up_ref, gain_m, packed_ref):
    pack_attention(who_ref, w_ref, gain_a[0:1, :], keep_ref[0], got_ref[0], packed_ref, 0)
    pack_up(who_ref[0], up_ref, gain_m[0:1, :], packed_ref, LANES)


def prepare_second(who_ref, w_ref, gain_a, keep_ref, got_ref, down_ref, packed_ref):
    pack_attention(who_ref, w_ref, gain_a[1:2, :], keep_ref[1], got_ref[1], packed_ref, LANES)
    pack_down(who_ref[0], down_ref, packed_ref, 0)


def prepare_third(who_ref, up_ref, gain_m, down_ref, packed_ref):
    pack_up(who_ref[0], up_ref, gain_m[1:2, :], packed_ref, 0)
    pack_down(who_ref[0], down_ref, packed_ref, LANES)


def image_numbers(rows, flag, lens):
    counts = [sum((rows >= t * n).astype(jnp.int32) for t in range(1, most + 1)) for n, most in lens]
    return jnp.where(flag == 1, counts[1], counts[0])


def make_mixing(flag_ref, low_ref, high_ref, mixing_ref, *, lens):
    rows = mixing_ref.shape[0]
    flag = flag_ref[0]

    def spread_rows(index_ref, length, most):
        count = index_ref.shape[0]
        columns = lax.broadcasted_iota(jnp.int32, (count, mixing_ref.shape[1]), 1)
        mix = jnp.zeros((count, mixing_ref.shape[1]), F32)
        for slot in range(4):
            mix = mix + MIX_WEIGHTS[slot] * (index_ref[:, slot : slot + 1] == columns).astype(F32)
        r = lax.broadcasted_iota(jnp.int32, (rows, count), 0)
        c = lax.broadcasted_iota(jnp.int32, (rows, count), 1)
        image = sum((r >= t * length).astype(jnp.int32) for t in range(1, most + 1))
        pick = ((r - image * length == c) & (r < most * length)).astype(BF16)
        return dot(pick, mix.astype(BF16))

    low = spread_rows(low_ref, *lens[0])
    high = spread_rows(high_ref, *lens[1])
    mixing_ref[...] = jnp.where(flag == 1, high, low).astype(BF16)


def write_norm(hidden, xhat_ref):
    xhat_ref[...] = normalize(hidden)[0].astype(BF16)


def join_table(z_ref, p0, p1, p2, p3, out_ref, table):
    for k, piece in enumerate((p0, p1, p2, p3)):
        table[:, pl.ds(pl.multiple_of((z_ref[0] ^ k) * 256, 256), 256)] = piece[...].astype(F32)
    out_ref[...] = table[...].astype(BF16)


def embed(who_ref, tokens_ref, mixing_ref, t0, t1, t2, t3, hidden_ref, xhat_ref, table):
    size = t0.shape[0]
    for k, piece in enumerate((t0, t1, t2, t3)):
        table[pl.ds(pl.multiple_of((who_ref[0] ^ k) * size, 8), size), :] = piece[...].astype(F32)
    rows = table[: mixing_ref.shape[1], :].astype(BF16)
    hidden = tokens_ref[...].astype(F32) + dot(mixing_ref[...], rows)
    hidden_ref[...] = hidden
    write_norm(hidden, xhat_ref)


def added(p0, r1, r2, r3):
    return (p0[...].astype(F32) + r1[...].astype(F32)) + (r2[...].astype(F32) + r3[...].astype(F32))


def add_norm(h_ref, p0, r1, r2, r3, middle_ref, xhat_ref):
    middle = h_ref[...] + added(p0, r1, r2, r3)
    middle_ref[...] = middle
    write_norm(middle, xhat_ref)


def output_parts(a0, a1, a2, a3, down_ref, *outs):
    down = down_ref[...].reshape(-1, down_ref.shape[2])
    for act_ref, out_ref in zip((a0, a1, a2, a3), outs):
        out_ref[...] = dot(act_ref[...], down).astype(BF16)


def add_output(h_ref, p0, r1, r2, r3, out_ref):
    out_ref[...] = h_ref[...] + added(p0, r1, r2, r3)


def add_norm_backward(g_ref, p0, r1, r2, r3, h_ref, d_ref, low_ref):
    d = g_ref[...] + norm_backward(added(p0, r1, r2, r3), *normalize(h_ref[...]))
    d_ref[...] = d
    low_ref[...] = d.astype(BF16)


def out_chunk(packed_ref, c):
    return packed_ref[:, c * 32 : (c + 1) * 32, 768:1024].reshape(256, 256)


def attention_forward(flag_ref, x_ref, w_ref, proj_ref, p_ref, *, lens):
    rows = x_ref.shape[0]
    flag = flag_ref[0]
    width = x_ref.shape[1]
    mask = image_numbers(lax.broadcasted_iota(jnp.int32, (rows, 1), 0), flag, lens) == image_numbers(
        lax.broadcasted_iota(jnp.int32, (1, rows), 1), flag, lens
    )
    for c in range(3):
        w = w_ref[:, :, c * 256 : (c + 1) * 256].reshape(width, 256)
        proj_ref[:, c * 256 : (c + 1) * 256] = dot(x_ref[...], w).astype(BF16)
    low = lane_low(rows)
    zero = jnp.zeros((), BF16)
    for u in range(2):
        q = proj_ref[:, u * LANES : (u + 1) * LANES] * jnp.asarray(0.125, BF16)
        k = proj_ref[:, 256 + u * LANES : 256 + (u + 1) * LANES]
        v = proj_ref[:, 512 + u * LANES : 512 + (u + 1) * LANES]
        total = None
        for keep in (low, ~low):
            s = dot_nt(jnp.where(keep, q, zero), k)
            s = jnp.where(mask, s, NEG_FILL)
            powers = jnp.exp(s - jnp.max(s, axis=-1, keepdims=True))
            probs = powers * (1.0 / jnp.sum(powers, axis=-1, keepdims=True))
            o = dot(probs.astype(BF16), jnp.where(keep, v, zero))
            total = o if total is None else total + o
        proj_ref[:, 768 + u * LANES : 768 + (u + 1) * LANES] = total.astype(BF16)
    for c in range(4):
        p_ref[:, c * 256 : (c + 1) * 256] = dot(proj_ref[:, 768:], out_chunk(w_ref, c)).astype(BF16)


def attention_backward(flag_ref, d_ref, proj_ref, w_ref, dproj_ref, p_ref, *, lens):
    rows, width = d_ref.shape
    flag = flag_ref[0]
    mask = image_numbers(lax.broadcasted_iota(jnp.int32, (rows, 1), 0), flag, lens) == image_numbers(
        lax.broadcasted_iota(jnp.int32, (1, rows), 1), flag, lens
    )
    d_o = sum(dot_nt(d_ref[:, c * 256 : (c + 1) * 256], out_chunk(w_ref, c)) for c in range(4))
    d_o = d_o.astype(BF16)
    low = lane_low(rows)
    zero = jnp.zeros((), BF16)
    scale = jnp.asarray(0.125, BF16)
    for u in range(2):
        q = proj_ref[:, u * LANES : (u + 1) * LANES] * scale
        k = proj_ref[:, 256 + u * LANES : 256 + (u + 1) * LANES]
        v = proj_ref[:, 512 + u * LANES : 512 + (u + 1) * LANES]
        g = d_o[:, u * LANES : (u + 1) * LANES]
        dq = dk = dv = None
        for keep in (low, ~low):
            k_own = jnp.where(keep, k, zero)
            s = jnp.where(mask, dot_nt(k_own, q), NEG_FILL)
            powers = jnp.exp(s - jnp.max(s, axis=0, keepdims=True))
            probs = powers * (1.0 / jnp.sum(powers, axis=0, keepdims=True))
            d_probs = dot_nt(jnp.where(keep, v, zero), g)
            centre = jnp.sum(probs * d_probs, axis=0, keepdims=True)
            d_scores = (probs * (d_probs - centre)).astype(BF16)
            terms = (
                dot_t(d_scores, k_own),
                dot(d_scores, jnp.where(keep, q, zero)),
                dot(probs.astype(BF16), jnp.where(keep, g, zero)),
            )
            dq, dk, dv = terms if dq is None else (dq + terms[0], dk + terms[1], dv + terms[2])
        dproj_ref[:, u * LANES : (u + 1) * LANES] = (dq * 0.125).astype(BF16)
        dproj_ref[:, 256 + u * LANES : 256 + (u + 1) * LANES] = dk.astype(BF16)
        dproj_ref[:, 512 + u * LANES : 512 + (u + 1) * LANES] = dv.astype(BF16)
    total = None
    for c in range(3):
        w = w_ref[:, :, c * 256 : (c + 1) * 256].reshape(width, 256)
        term = dot_nt(dproj_ref[:, c * 256 : (c + 1) * 256], w)
        total = term if total is None else total + term
    p_ref[...] = total.astype(BF16)


def gelu_parts(pre):
    upto = 0.5 * (1.0 + lax.erf(pre * math.sqrt(0.5)))
    density = jnp.exp(-0.5 * pre * pre) * (1.0 / math.sqrt(2.0 * math.pi))
    return pre * upto, upto + pre * density


def mlp_up(x_ref, up_ref, both_ref):
    width = x_ref.shape[1]
    for c in range(4):
        cols = slice(c * 256, (c + 1) * 256)
        act, slope = gelu_parts(dot(x_ref[...], up_ref[:, :, cols].reshape(width, 256)))
        both_ref[0, :, cols] = act.astype(BF16)
        both_ref[1, :, cols] = slope.astype(BF16)


def mlp_down(*refs):
    count = len(refs) // 2
    down = refs[count][...].reshape(-1, refs[count].shape[2])
    for act_ref, out_ref in zip(refs[:count], refs[count + 1 :]):
        out_ref[...] = dot(act_ref[0], down).astype(BF16)


def mlp_backward(d_ref, slope_ref, up_ref, down_ref, dpre_ref, p_ref):
    width = d_ref.shape[1]
    for c in range(4):
        cols = slice(c * 256, (c + 1) * 256)
        d_act = dot_nt(d_ref[...], down_ref[2 * c : 2 * c + 2].reshape(256, width))
        dpre_ref[:, cols] = (d_act * slope_ref[0, :, cols].astype(F32)).astype(BF16)
    p_ref[...] = dot_nt(dpre_ref[...], up_ref[...].reshape(width, width)).astype(BF16)


def mlp_both(x_ref, d_ref, up_ref, down_ref, act_ref, dpre_ref, back_ref):
    width = x_ref.shape[1]
    for c in range(4):
        cols = slice(c * 256, (c + 1) * 256)
        act, slope = gelu_parts(dot(x_ref[...], up_ref[:, :, cols].reshape(width, 256)))
        act_ref[:, cols] = act.astype(BF16)
        d_act = dot_nt(d_ref[...], down_ref[2 * c : 2 * c + 2].reshape(256, width))
        dpre_ref[:, cols] = (d_act * slope).astype(BF16)
    back_ref[...] = dot_nt(dpre_ref[...], up_ref[...].reshape(width, width)).astype(BF16)


def summed(left, right, rows, cols=slice(None)):
    total = None
    for a, b in zip(left, right):
        term = dot_t(a[:, rows], b[:, cols])
        total = term if total is None else total + term
    return total


def stack_rows(blocks, out_ref):
    rows = blocks[0].shape[0]
    tall = -(-rows // 32) * 32
    for k, block in enumerate(blocks):
        out_ref[k * tall + rows // 16 * 16 : (k + 1) * tall, :] = jnp.zeros(
            (tall - rows // 16 * 16, out_ref.shape[1]), BF16
        )
        out_ref[k * tall : k * tall + rows, :] = block


def grads_mlp(*refs):
    x, dpre, act, d, out_ref, left, right = refs[:4], refs[4:8], refs[8:12], refs[12:16], *refs[16:]
    acts = [a[0] if len(a.shape) == 3 else a[...] for a in act]
    pairs = (([a[...] for a in x], dpre), (acts, d))
    for half, (first, second) in enumerate(pairs):
        stack_rows(first, left)
        stack_rows([b[...] for b in second], right)
        for t in range(4):
            total = dot_t(left[:, t * 256 : (t + 1) * 256], right[...]).astype(BF16)
            out_ref[2 * t : 2 * t + 2, half * LANES : (half + 1) * LANES, :] = total.reshape(2, LANES, -1)


def stack_attention(refs, left, right, narrow):
    x, dproj, kept, d = refs[:4], refs[4:8], refs[8:12], refs[12:16]
    stack_rows([a[...] for a in x], left)
    stack_rows([a[...] for a in dproj], right.at[:, :768])
    stack_rows([a[...] for a in kept], narrow)


def grads_attention(*refs):
    out_ref, left, right, narrow = refs[16:]
    stack_attention(refs, left, right, narrow)
    for t in range(4):
        total = dot_t(left[:, t * 256 : (t + 1) * 256], right[:, :768]).astype(BF16)
        out_ref[2 * t : 2 * t + 2, :LANES, :768] = total.reshape(2, LANES, -1)
    stack_rows([a[...] for a in refs[12:16]], right)
    for c in range(4):
        total = dot_t(narrow[...], right[:, c * 256 : (c + 1) * 256])
        out_ref[:, c * 32 : (c + 1) * 32, 768:1024] = total.astype(BF16).reshape(8, 32, 256)


def rows_of(j):
    return pl.ds(pl.multiple_of(j * LANES, LANES), LANES)


def grads_attention_sides(core_ref, *refs):
    theirs, mine, (left, right, narrow) = refs[16:20], refs[20], refs[21:]
    core = core_ref[0]
    stack_attention(refs, left, right, narrow)
    for z in range(4):
        theirs[z][:, :768] = dot_t(left[:, rows_of(z * 2 + 1 - core)], right[:, :768]).astype(BF16)
    for z in range(4):
        mine[z, :, :768] = dot_t(left[:, rows_of(z * 2 + core)], right[:, :768]).astype(BF16)
    stack_rows([a[...] for a in refs[12:16]], right)
    for c in range(4):
        total = dot_t(narrow[...], right[:, c * 256 : (c + 1) * 256]).astype(BF16).reshape(8, 32, 256)
        rows = slice(c * 32, (c + 1) * 32)
        for z in range(4):
            first, second = total[2 * z], total[2 * z + 1]
            theirs[z][rows, 768:1024] = jnp.where(core == 0, second, first)
            mine[z, rows, 768:1024] = jnp.where(core == 0, first, second)


def add_pair(mine_ref, *refs):
    for z in range(4):
        refs[4][z] = (mine_ref[z].astype(F32) + refs[z][...].astype(F32)).astype(BF16)


def last_norm(g_ref, p0, r1, r2, r3, h_ref, mixing_ref, term_ref, d_ref, out_ref, packed, sem):
    d = g_ref[...] + norm_backward(added(p0, r1, r2, r3), *normalize(h_ref[...]))
    d_ref[...] = d
    high = d.astype(BF16)
    low = (d - high.astype(F32)).astype(BF16)
    table = dot_t(mixing_ref[...], high) + dot_t(mixing_ref[...], low)
    packed[...] = jnp.zeros(packed.shape, BF16)
    for j in range(8):
        for c in range(-(-table.shape[0] // 32)):
            size = min(32, table.shape[0] - 32 * c)
            part = table[32 * c : 32 * c + size, j * LANES : (j + 1) * LANES]
            packed[j, :size, c * LANES : (c + 1) * LANES] = part.astype(BF16)
    copy = pltpu.make_async_copy(packed, out_ref.at[:, LANES : LANES + 32, :], sem.at[0])
    copy.start()
    copy.wait()


def unpack_table(refs, out_ref):
    g = [ref[LANES : LANES + 32, :].astype(F32) for ref in refs]
    total = (g[0] + g[1]) + (g[2] + g[3])
    for c in range(-(-out_ref.shape[0] // 32)):
        size = min(32, out_ref.shape[0] - 32 * c)
        out_ref[32 * c : 32 * c + size, :] = total[:size, c * LANES : (c + 1) * LANES]


def finish_mlp(me_ref, *refs, merged):
    g, up_ref, gain_ref, dup_ref, ddown_ref, dgain_ref = refs[:5], refs[5], refs[6], *refs[-3:]
    me = me_ref[0]
    low = 192 if merged else LANES
    column = jnp.sum(diagonal(gain_ref[0]), axis=1, keepdims=True)
    total = jnp.zeros((LANES, LANES), F32)
    downs = [piece[low : low + LANES, :] for piece in g[:3]] + [g[4][:LANES, :]]
    for k, piece in enumerate(downs):
        rows = pl.ds(pl.multiple_of((me ^ k) * LANES, LANES), LANES)
        ddown_ref[0, rows, :] = piece.astype(F32)
    ups = [piece[:LANES, :] for piece in g[:4]]
    for i in range(4):
        got = jnp.where(
            me == i, ups[0], jnp.where(me == i ^ 1, ups[1], jnp.where(me == i ^ 2, ups[2], ups[3]))
        ).astype(F32)
        for j in range(8):
            cols = slice((j * 4 + i) * LANES, (j * 4 + i + 1) * LANES)
            part = got[:, j * LANES : (j + 1) * LANES]
            dup_ref[0, :, cols] = part * column
            total = total + part * up_ref[0, :, cols].astype(F32)
    dgain_ref[0] = jnp.sum(total.T, axis=0, keepdims=True)


def attention_rows(refs):
    if len(refs) == 4:
        return [ref[:LANES, :] for ref in refs]
    rows = [jnp.concatenate([ref[128:192, :], ref[320:384, :]], axis=0) for ref in refs[:3]]
    return rows + [jnp.concatenate([ref[128:192, :] for ref in refs[3:]], axis=0)]


def by_owner(me, pieces, i):
    g0, g1, g2, g3 = pieces
    return jnp.where(me == i, g0, jnp.where(me == i ^ 1, g1, jnp.where(me == i ^ 2, g2, g3)))


def split_out(who_ref, *refs):
    keep_ref, give_ref = refs[-2:]
    packed = [piece[:, 768:] for piece in attention_rows(refs[:-2])]
    me, core = who_ref[0], who_ref[1]
    for second in range(2):
        even, odd = by_owner(me, packed, 2 * second), by_owner(me, packed, 2 * second + 1)
        keep_ref[second] = jnp.where(core == 0, even, odd)
        give_ref[second] = jnp.where(core == 0, odd, even)


def finish_attention(who_ref, *refs, count):
    g, (w_ref, gain_ref, keep_ref, got_ref) = refs[:count], refs[count : count + 4]
    if count == 4:
        unpack_table(g, refs[-1])
        refs = refs[:-1]
    dqkv_ref, dout_ref, dgain_ref = refs[-3:]
    me, core = who_ref[0], who_ref[1]
    column = jnp.sum(diagonal(gain_ref[0]), axis=1, keepdims=True)
    total = jnp.zeros((LANES, LANES), F32)
    low = lane_low(LANES)
    rows = [piece[:, :768] for piece in attention_rows(g)]
    owned = [by_owner(me, rows, i).astype(F32) for i in range(4)]
    for t in range(12):
        u = t // 2
        for side in range(2):
            first = owned[side][:, u * LANES : (u + 1) * LANES]
            second = owned[side + 2][:, u * LANES : (u + 1) * LANES]
            if t % 2 == 0:
                part = jnp.where(low, first, lane_swap(second))
            else:
                part = jnp.where(low, lane_swap(first), second)
            chunk = (t // 4) * 8 + 2 * (t % 4) + side
            cols = slice(chunk * LANES, (chunk + 1) * LANES)
            dqkv_ref[0, :, cols] = part * column
            total = total + part * w_ref[0, :, cols].astype(F32)
    dgain_ref[0] = jnp.sum(total.T, axis=0, keepdims=True)
    for second in range(2):
        keep, got = keep_ref[second], got_ref[second]
        halves = (jnp.where(core == 0, keep, got), jnp.where(core == 0, got, keep))
        for h, part in enumerate(halves):
            for c in range(4):
                top = (2 * second + h) * 32
                dout_ref[0, top : top + 32, c * 256 : (c + 1) * 256] = part[c * 32 : (c + 1) * 32, :].astype(F32)


def local_fast(
    tokens,
    pos_table,
    index_lo,
    index_hi,
    resolution,
    gain_attn,
    w_qkv,
    w_out,
    gain_mlp,
    w_up,
    w_down,
    cotangent,
):
    rows, width = tokens.shape
    layers = w_qkv.shape[0]
    square = Square()
    me = square.me
    me1 = me.reshape(1).astype(jnp.int32)
    shard = lax.axis_index("fsdp")
    core, deep = shard % 2, shard // 2
    deep1 = deep.reshape(1).astype(jnp.int32)
    len_low, len_high = index_lo.shape[0], index_hi.shape[0]
    lens = ((len_low, rows // len_low), (len_high, rows // len_high))
    block = (rows, width)
    blocks = range(4)

    def over_fsdp(x, k):
        return lax.ppermute(x, "fsdp", [(j, j ^ k) for j in range(8)])

    def layer_of(array, depth):
        return pl.BlockSpec((1,) + array.shape[1:], lambda *_: (depth,) + (0,) * (array.ndim - 1))

    who = jnp.stack([me, core]).astype(jnp.int32)
    head_side = me >> 1

    def out_rows(half):
        return lax.dynamic_slice(w_out, (0, (head_side * 2 + half) * 32, 0), (layers, 32, width))

    keep, got = out_rows(core), over_fsdp(out_rows(1 - core), 1)
    gains_a = gain_attn.reshape(layers, 1, LANES)
    gains_m = gain_mlp.reshape(layers, 1, LANES)

    def part(top):
        return pl.BlockSpec((8, LANES, width), lambda *_: (0, top, 0))

    def fetch(body, args, specs, after=()):
        (packed,) = call(
            body, [((2 * LANES, width), BF16)], [who] + args, [scalars()] + specs, after=after, limit=60
        )
        return lax.all_gather(packed, "fsdp", axis=0, tiled=False)

    first_w = fetch(
        prepare_first,
        [w_qkv, gain_attn, keep, got, w_up, gain_mlp],
        [layer_of(w_qkv, 0), None, None, None, layer_of(w_up, 0), None],
    )

    flag = resolution[me]
    flag1 = flag.reshape(1)
    flags = [resolution[owner].reshape(1) for owner in square.owners()]
    shard_count, group_count = 8, resolution.shape[0]
    high_groups = jnp.sum(resolution)
    tokens_low = ((group_count - high_groups) * shard_count * lens[0][1] * len_low).astype(F32)
    tokens_high = (high_groups * shard_count * lens[1][1] * len_high).astype(F32)
    token_share = 2.0 * jnp.where(flag == 1, tokens_high, tokens_low) / (tokens_low + tokens_high)
    live = jnp.where(flag == 1, lens[1][1] * len_high, lens[0][1] * len_low)
    weight = jnp.where(jnp.arange(rows, dtype=jnp.int32) < live, token_share, 0.0)
    gradient = cotangent.astype(F32) * weight[:, None]

    normed = [(block, F32), (block, BF16)]
    size = -(-len_high // 32) * 8
    mine = lax.dynamic_slice(
        jnp.pad(pos_table, ((0, 4 * size - len_high), (0, 0))), (me * size, 0), (size, LANES)
    )
    other = over_fsdp(mine, 1)
    pair = jnp.concatenate([jnp.where(core == 0, mine, other), jnp.where(core == 0, other, mine)], axis=1)
    pieces = [pair] + [over_fsdp(pair, 2 * k) for k in range(1, 4)]
    (mine,) = call(
        join_table,
        [((size, width), BF16)],
        [deep1] + pieces,
        [scalars()] + [None] * 4,
        scratch=[VMEM((size, width), F32)],
    )
    (mixing,) = call(
        functools.partial(make_mixing, lens=lens),
        [((rows, len_high), BF16)],
        [flag1, index_lo, index_hi],
        [scalars(), None, None],
    )
    hidden, xhat = call(
        embed,
        normed,
        [who, tokens, mixing] + square.spread(mine),
        [scalars()] + [None] * 6,
        scratch=[VMEM((4 * size, width), F32)],
    )
    second_w = fetch(
        prepare_second,
        [w_qkv, gain_attn, keep, got, w_down],
        [layer_of(w_qkv, 1), None, None, None, layer_of(w_down, 0)],
        [xhat],
    )
    third_w = fetch(
        prepare_third,
        [w_up, gain_mlp, w_down],
        [layer_of(w_up, 1), None, layer_of(w_down, 1)],
        [xhat],
    )
    attn_w = [(first_w, part(0)), (second_w, part(1))]

    def tie(*values):
        return lax.optimization_barrier(values)

    def tie_last(es, term):
        near, term = tie(es[:3], term)
        far, near, term = tie(es[3], near, term)
        return near + [far], term

    def chain(kernel):
        done = []
        for k in blocks:
            done.append(kernel(k, [d[0] for d in done[-1:]]))
        return done

    def collect(parts):
        return [parts[0]] + [square.swap(parts[k], k) for k in range(1, 4)]

    d_top = square.spread(gradient.astype(BF16))
    saved = []
    for depth in range(layers):
        a_w, a_part = attn_w[depth]
        xs = square.spread(xhat)
        got = chain(
            lambda k, after: call(
                functools.partial(attention_forward, lens=lens),
                [(block, BF16)] * 2,
                [flags[k], xs[k], a_w],
                [scalars(), None, a_part],
                after=after,
            )
        )
        kept = [g[0] for g in got]
        es = collect([g[1] for g in got])
        if depth == 0:
            es, d_top = tie(es, d_top)
        before, (middle, xhat) = hidden, call(add_norm, normed, [hidden] + es)
        ms = square.spread(xhat)
        if depth < layers - 1:
            acts = chain(
                lambda k, after: call(
                    mlp_up, [((2,) + block, BF16)], [ms[k], first_w], [None, part(1)], after=after
                )
            )
            acts = [a[0] for a in acts]
            first_half = pl.BlockSpec((1,) + block, lambda *_: (0, 0, 0))
            parts = call(
                mlp_down, [(block, BF16)] * 3, acts[1:] + [second_w], [first_half] * 3 + [part(0)], after=acts[:1]
            )
            (own,) = call(
                mlp_down, [(block, BF16)], [acts[0], second_w], [first_half, part(0)], after=parts[:1]
            )
            parts = [own] + list(parts)
            saved.append((before, xs, kept, middle, ms, acts))
            hidden, xhat = call(add_norm, normed, [middle] + collect(parts))
        else:
            got = chain(
                lambda k, after: call(
                    mlp_both,
                    [(block, BF16)] * 3,
                    [ms[k], d_top[k], third_w, third_w],
                    [None, None, part(0), part(1)],
                    after=after,
                )
            )
            acts, dpres, backs = ([g[t] for g in got] for t in range(3))
            top_acts = acts
            saved.append((before, xs, kept, middle, ms, acts))

    def far_halves(x, y):
        half = x.shape[0] // 2
        return [square.swap(x[:half], 2), square.swap(y[half:], 1)]

    core1 = core.reshape(1).astype(jnp.int32)
    tall = 4 * (-(-rows // 32) * 32)

    def home(term):
        return lax.psum_scatter(term, "fsdp", scatter_dimension=0, tiled=False)

    homes_m, homes_a = [None] * layers, [None] * layers
    for depth in reversed(range(layers)):
        top = depth == layers - 1
        a_w, a_part = attn_w[depth]
        before, xs, kept, middle, ms, acts = saved[depth]
        ds = d_top if top else square.spread(low)
        if not top:
            second_half = pl.BlockSpec((1,) + block, lambda *_: (1, 0, 0))
            got = chain(
                lambda k, after: call(
                    mlp_backward,
                    [(block, BF16)] * 2,
                    [ds[k], acts[k], first_w, second_w],
                    [None, second_half, part(1), part(0)],
                    after=after or [homes_m[1]],
                )
            )
            dpres, backs = ([g[t] for g in got] for t in range(2))
        es = collect(backs)
        first_half = pl.BlockSpec((1,) + block, lambda *_: (0, 0, 0))
        (term,) = call(
            grads_mlp,
            [((8, 2 * LANES, width), BF16)],
            list(ms) + list(dpres) + list(acts) + list(ds),
            [None] * 8 + [None if top else first_half] * 4 + [None] * 4,
            scratch=[VMEM((tall, width), BF16)] * 2,
        )
        es, term = tie_last(es, term)
        homes_m[depth] = home(term)
        d_middle, low = call(add_norm_backward, normed, [gradient] + es + [middle], limit=60)
        if not top:
            m, a = homes_m[1], homes_a[1]
            merged = jnp.concatenate([m[:LANES], a[:64], m[LANES:], a[64:]], axis=0)
        ds = square.spread(low)
        got = chain(
            lambda k, after: call(
                functools.partial(attention_backward, lens=lens),
                [((rows, 768), BF16), (block, BF16)],
                [flags[k], ds[k], kept[k], a_w],
                [scalars(), None, None, a_part],
                after=after or ([] if top else [merged]),
            )
        )
        dprojs = [g[0] for g in got]
        es = collect([g[1] for g in got])
        out_part = pl.BlockSpec((rows, 256), lambda *_: (0, 3))
        stacks = [VMEM((tall, width), BF16)] * 2 + [VMEM((tall, 256), BF16)]
        operands = list(xs) + dprojs + list(kept) + list(ds)
        specs = [None] * 8 + [out_part] * 4 + [None] * 4
        if top:
            *theirs, mine = call(
                grads_attention_sides,
                [((LANES, width), BF16)] * 4 + [((4, LANES, width), BF16)],
                [core1] + operands,
                [scalars()] + specs,
                scratch=stacks,
            )
            got = [over_fsdp(part, 1) for part in theirs]
            es, mine = tie_last(es, mine)
            (term,) = call(add_pair, [(mine.shape, BF16)], [mine] + got, after=[es[3]])
            es, term = tie(es, term)
            homes_a[depth] = lax.psum_scatter(
                term, "fsdp", scatter_dimension=0, tiled=False, axis_index_groups=[[0, 2, 4, 6], [1, 3, 5, 7]]
            )
            last_middle = middle
            gradient, low = call(add_norm_backward, normed, [d_middle] + es + [before], limit=60)
        else:
            near = [square.swap(merged, 1), square.swap(merged, 2)]
            (term,) = call(grads_attention, [((8, LANES + 32, width), BF16)], operands, specs, after=near, scratch=stacks)
            es, term = tie_last(es, term)
            anywhere = pl.BlockSpec(memory_space=pl.ANY)
            gradient, term = call(
                last_norm,
                [(block, F32), (term.shape, BF16)],
                [d_middle] + es + [before, mixing, term],
                [None] * 7 + [anywhere],
                out_specs=[whole(block), anywhere],
                aliases={7: 1},
                scratch=[VMEM((8, 32, width), BF16), pltpu.SemaphoreType.DMA((1,))],
            )
            homes_a[0] = home(term)

    merged = [merged, *near] + far_halves(*near)

    outs = call(
        output_parts, [(block, BF16)] * 4, top_acts + [third_w], [None] * 4 + [part(1)], after=[gradient]
    )
    (output,) = call(add_output, [(block, F32)], [last_middle] + collect(outs))
    homes_m[0], gradient = tie(homes_m[0], gradient)
    x, y = square.swap(homes_m[0], 1), square.swap(homes_m[0], 2)
    homes_m[0] = [homes_m[0], x, y] + far_halves(x, y)
    big = [None] * 6

    def finish(body, depth, args, shapes, prior):
        extra = [] if prior[0] is None else prior
        specs = [layer_of(a, depth) if a is w_up or a is w_qkv or a is gains_a or a is gains_m else None for a in args]
        return call(
            body,
            [(shape, F32) for shape in shapes],
            [who] + args + extra,
            [scalars()] + specs + [pl.BlockSpec(memory_space=pl.ANY)] * len(extra),
            aliases={1 + len(args) + t: t for t in range(len(extra))},
            out_specs=[
                layer_of(jax.ShapeDtypeStruct(shape, F32), depth) if len(shape) == 3 else whole(shape)
                for shape in shapes
            ],
        )

    def finish_m(depth, pieces):
        shapes = [w_up.shape, w_down.shape, gains_m.shape]
        body = functools.partial(finish_mlp, merged=depth > 0)
        big[3:] = finish(body, depth, pieces + [w_up, gains_m], shapes, big[3:])

    def finish_a(depth, pieces):
        keep, give = call(
            split_out, [((2, LANES, 256), BF16)] * 2, [who] + pieces, [scalars()] + [None] * len(pieces)
        )
        shapes = [w_qkv.shape, w_out.shape, gains_a.shape]
        body = functools.partial(finish_attention, count=len(pieces))
        args = pieces + [w_qkv, gains_a, keep, over_fsdp(give, 1)]
        if len(pieces) == 4:
            shapes = shapes + [(len_high, LANES)]
        big[:3] = finish(body, depth, args, shapes, big[:3])

    finish_m(1, merged)
    finish_a(1, merged)
    homes_a[0], homes_m[0], big, output = tie(homes_a[0], homes_m[0], big, output)
    pieces = square.spread(homes_a[0])
    finish_m(0, homes_m[0])
    pieces, big = tie(pieces, big)
    finish_a(0, pieces)
    d_table = big.pop(3)
    return (
        output,
        gradient,
        d_table,
        big[2].reshape(layers, LANES),
        big[0],
        big[1],
        big[5].reshape(layers, LANES),
        big[3],
        big[4],
    )


def solution(mesh):
    in_specs = (
        P(("dp", "fsdp"), None),
        P(None, "fsdp"),
        P(),
        P(),
        P(),
        P(None, "fsdp"),
        P(None, "fsdp", None),
        P(None, "fsdp", None),
        P(None, "fsdp"),
        P(None, "fsdp", None),
        P(None, "fsdp", None),
        P(("dp", "fsdp"), None),
    )
    out_specs = (
        P(("dp", "fsdp"), None),
        P(("dp", "fsdp"), None),
        P(None, "fsdp"),
        P(None, "fsdp"),
        P(None, "fsdp", None),
        P(None, "fsdp", None),
        P(None, "fsdp"),
        P(None, "fsdp", None),
        P(None, "fsdp", None),
    )
    fast = mesh.shape["dp"] == 4 and mesh.shape["fsdp"] == 8
    local = local_fast if fast else local_general
    return jax.shard_map(local, mesh=mesh, in_specs=in_specs, out_specs=out_specs, check_vma=False)
```

```python
import functools
import math

import jax
import jax.numpy as jnp
from jax import lax
from jax.experimental import pallas as pl
from jax.experimental.pallas import tpu as pltpu
from jax.sharding import PartitionSpec as P

HEADS = 16
EPS = 1e-06
NEG_FILL = -1e30
MIX_WEIGHTS = (0.5, 0.25, 0.125, 0.125)
BF16 = jnp.bfloat16
F32 = jnp.float32


def dot(a, b):
    return jnp.dot(a, b, preferred_element_type=F32)


def dot_t(a, b):
    return lax.dot_general(a, b, (((0,), (0,)), ((), ())), preferred_element_type=F32)


def dot_nt(a, b):
    return lax.dot_general(a, b, (((1,), (1,)), ((), ())), preferred_element_type=F32)


def normalize(hidden):
    center = hidden - jnp.mean(hidden, axis=-1, keepdims=True)
    rstd = lax.rsqrt(jnp.mean(center * center, axis=-1, keepdims=True) + EPS)
    return center * rstd, rstd


def norm_backward(e, xhat, rstd):
    return rstd * (
        e
        - jnp.mean(e, axis=-1, keepdims=True)
        - xhat * jnp.mean(e * xhat, axis=-1, keepdims=True)
    )


def gelu_exact(pre_act):
    return jax.nn.gelu(pre_act, approximate=False)


class Square:
    def __init__(self):
        self.count = lax.axis_size("dp")
        self.me = lax.axis_index("dp")
        self.pairs = self.count == 4

    def owners(self):
        if self.pairs:
            return [self.me ^ k for k in range(self.count)]
        return [jnp.int32(k) for k in range(self.count)]

    def swap(self, block, k):
        return lax.ppermute(block, "dp", [(i, i ^ k) for i in range(self.count)])

    def spread(self, block):
        if self.pairs:
            return [block] + [self.swap(block, k) for k in range(1, self.count)]
        full = lax.all_gather(block, "dp")
        return [full[k] for k in range(self.count)]

    def collect(self, parts):
        if self.pairs:
            total = parts[0].astype(F32)
            for k in range(1, self.count):
                total = total + self.swap(parts[k].astype(BF16), k).astype(F32)
            return total
        stacked = jnp.stack([part.astype(BF16) for part in parts])
        return lax.psum_scatter(stacked, "dp", scatter_dimension=0, tiled=False).astype(F32)

    def gather(self, piece):
        if not self.pairs:
            return lax.all_gather(piece, "dp")
        got = [piece] + [self.swap(piece, k) for k in range(1, self.count)]
        odd = (self.me & 1) == 1
        high = (self.me & 2) == 2
        low_pair = (jnp.where(odd, got[1], got[0]), jnp.where(odd, got[0], got[1]))
        far_pair = (jnp.where(odd, got[3], got[2]), jnp.where(odd, got[2], got[3]))
        return jnp.stack(
            [
                jnp.where(high, far_pair[0], low_pair[0]),
                jnp.where(high, far_pair[1], low_pair[1]),
                jnp.where(high, low_pair[0], far_pair[0]),
                jnp.where(high, low_pair[1], far_pair[1]),
            ]
        )

    def total(self, piece):
        if not self.pairs:
            return lax.psum(piece.astype(BF16), "dp").astype(F32)
        own = piece.astype(BF16)
        got = [own.astype(F32)] + [self.swap(own, k).astype(F32) for k in range(1, self.count)]
        return (got[0] + got[1]) + (got[2] + got[3])


def select(index, choices):
    out = choices[0]
    for k in range(1, len(choices)):
        out = jnp.where(index == k, choices[k], out)
    return out


def local_general(
    tokens,
    pos_table,
    index_lo,
    index_hi,
    resolution,
    gain_attn,
    w_qkv,
    w_out,
    gain_mlp,
    w_up,
    w_down,
    cotangent,
):
    row_count, width = tokens.shape
    layers, shard_rows, _ = w_qkv.shape
    hidden_units = w_up.shape[2]
    shard_count = lax.axis_size("fsdp")
    shard = lax.axis_index("fsdp")
    square = Square()
    group_count = square.count
    me = square.me
    head_size = width // HEADS
    my_heads = HEADS // group_count
    part = my_heads * head_size
    unit_part = hidden_units // group_count
    fine = square.pairs and shard_count * 2 == HEADS
    score_scale = 1.0 / math.sqrt(head_size)
    len_low = index_lo.shape[0]
    len_high = index_hi.shape[0]

    row_ids = jnp.arange(row_count, dtype=jnp.int32)

    def layout(flag):
        length = jnp.where(flag == 1, len_high, len_low).astype(jnp.int32)
        images = jnp.where(flag == 1, row_count // len_high, row_count // len_low).astype(jnp.int32)
        live = row_ids < images * length
        return live, jnp.where(live, row_ids // length, images)

    flag = resolution[me]
    live_rows, _ = layout(flag)
    block_ids = jnp.stack([layout(resolution[owner])[1] for owner in square.owners()])
    same_image = block_ids[:, :, None] == block_ids[:, None, :]
    picked = jnp.where(flag == 1, index_hi[row_ids % len_high], index_lo[row_ids % len_low])
    table_ids = jnp.arange(len_high, dtype=jnp.int32)
    mixing = jnp.zeros((row_count, len_high), F32)
    for slot in range(4):
        mixing = mixing + MIX_WEIGHTS[slot] * (
            picked[:, slot : slot + 1] == table_ids[None, :]
        ).astype(F32)
    mixing = (mixing * live_rows[:, None].astype(F32)).astype(BF16)
    high_groups = jnp.sum(resolution)
    tokens_low = (
        (group_count - high_groups) * shard_count * (row_count // len_low) * len_low
    ).astype(F32)
    tokens_high = (high_groups * shard_count * (row_count // len_high) * len_high).astype(F32)
    token_share = 2.0 * jnp.where(flag == 1, tokens_high, tokens_low) / (tokens_low + tokens_high)
    weight = jnp.where(live_rows, token_share, 0.0)

    half = shard_rows // 4
    core = shard % 2
    swap_core = [(j, j ^ 1) for j in range(shard_count)]
    pair_side, head_side = me & 1, (me >> 1) & 1

    def qkv_part(w):
        if fine:
            view = w.reshape(shard_rows, 3 * HEADS // 4, 2, 2, head_size)
            view = select(pair_side, [view[:, :, 0], view[:, :, 1]])
            view = select(head_side, [view[:, :, 0], view[:, :, 1]])
            return view.reshape(shard_rows, 3 * part)
        view = w.reshape(shard_rows, 3, group_count, part)
        return lax.dynamic_index_in_dim(view, me, 2, keepdims=False).reshape(shard_rows, 3 * part)

    def up_part(w):
        view = w.reshape(shard_rows, shard_count, group_count, unit_part // shard_count)
        return lax.dynamic_index_in_dim(view, me, 2, keepdims=False).reshape(shard_rows, unit_part)

    def down_part(w):
        rows = unit_part // shard_count
        return lax.dynamic_slice_in_dim(w, me * rows, rows, 0)

    def out_part(w):
        if fine:
            view = w.reshape(2, 2, half, width)
            mine = select(head_side, [view[0], view[1]])
            keep = select(core, [mine[0], mine[1]])
            give = select(core, [mine[1], mine[0]])
            got = lax.ppermute(give, "fsdp", swap_core)
            return jnp.where(core == pair_side, keep, got)
        return w

    def fetch(piece):
        return lax.all_gather(piece, "fsdp", axis=0, tiled=False)

    weights = []
    table = lax.all_gather(pos_table, "fsdp", axis=1, tiled=True)
    for depth in range(layers):
        gain_a = gain_attn[depth].astype(F32)[:, None]
        gain_m = gain_mlp[depth].astype(F32)[:, None]
        qkv = (qkv_part(w_qkv[depth]).astype(F32) * gain_a).astype(BF16)
        up = (up_part(w_up[depth]).astype(F32) * gain_m).astype(BF16)
        down = down_part(w_down[depth])
        out = out_part(w_out[depth])
        qkv_all = fetch(qkv).reshape(width, 3 * part)
        a = up.size // width
        b = a + down.shape[0]
        rest = fetch(jnp.concatenate([up.reshape(a, width), down, out], axis=0))
        up_all = rest[:, :a].reshape(width, unit_part)
        down_all = rest[:, a:b].reshape(unit_part, width)
        out_all = rest[:, b:].reshape(-1, width)
        if not fine:
            out_all = lax.dynamic_slice_in_dim(out_all, me * part, part, 0)
        weights.append((qkv_all, out_all, up_all, down_all))

    def split_heads(block):
        return block.reshape(group_count, row_count, my_heads, head_size)

    def scores_of(queries, key_rows):
        scores = (
            jnp.einsum("bqhd,bkhd->bhqk", queries, key_rows, preferred_element_type=F32)
            * score_scale
        )
        return jnp.where(same_image[:, None], scores, NEG_FILL)

    def spread(block):
        return jnp.concatenate(square.spread(block), axis=0)

    def collect(partial):
        return square.collect([partial[k * row_count : (k + 1) * row_count] for k in range(group_count)])

    hidden = tokens.astype(F32) + dot(mixing, table)
    saved = []
    for depth in range(layers):
        qkv_w, out_w, up_w, down_w = weights[depth]
        xhat_a, rstd_a = normalize(hidden)
        rows_a = spread(xhat_a.astype(BF16))
        projected = dot(rows_a, qkv_w).astype(BF16)
        queries = split_heads(projected[:, :part])
        key_rows = split_heads(projected[:, part : 2 * part])
        values = split_heads(projected[:, 2 * part :])
        scores = scores_of(queries, key_rows)
        row_max = jnp.max(scores, axis=-1, keepdims=True)
        powers = jnp.exp(scores - row_max)
        row_total = jnp.sum(powers, axis=-1, keepdims=True)
        log_total = row_max + jnp.log(row_total)
        probs = (powers / row_total).astype(BF16)
        attended = jnp.einsum("bhqk,bkhd->bqhd", probs, values, preferred_element_type=F32)
        attended = attended.reshape(group_count * row_count, part).astype(BF16)
        middle = hidden + collect(dot(attended, out_w).astype(BF16))
        xhat_m, rstd_m = normalize(middle)
        rows_m = spread(xhat_m.astype(BF16))
        pre_act = dot(rows_m, up_w)
        activated = gelu_exact(pre_act).astype(BF16)
        result = middle + collect(dot(activated, down_w).astype(BF16))
        saved.append(
            (xhat_a, rstd_a, rows_a, queries, key_rows, values, log_total, attended,
             xhat_m, rstd_m, rows_m, pre_act, activated)
        )
        hidden = result

    gradient = cotangent.astype(F32) * weight[:, None]
    shares = [None] * layers
    for depth in reversed(range(layers)):
        qkv_w, out_w, up_w, down_w = weights[depth]
        (xhat_a, rstd_a, rows_a, queries, key_rows, values, log_total, attended,
         xhat_m, rstd_m, rows_m, pre_act, activated) = saved[depth]
        d_result = spread(gradient.astype(BF16))
        grad_down = dot_t(activated, d_result).astype(BF16)
        d_activated = dot_nt(d_result, down_w)
        _, pullback = jax.vjp(gelu_exact, pre_act)
        d_pre = pullback(d_activated)[0].astype(BF16)
        grad_up = dot_t(rows_m, d_pre).astype(BF16)
        e = collect(dot_nt(d_pre, up_w).astype(BF16))
        d_middle = gradient + norm_backward(e, xhat_m, rstd_m)
        d_attn = spread(d_middle.astype(BF16))
        grad_out = dot_t(attended, d_attn).astype(BF16)
        d_attended = split_heads(dot_nt(d_attn, out_w).astype(BF16))
        probs = jnp.exp(scores_of(queries, key_rows) - log_total)
        d_values = jnp.einsum(
            "bhqk,bqhd->bkhd", probs.astype(BF16), d_attended, preferred_element_type=F32
        )
        d_probs = jnp.einsum("bqhd,bkhd->bhqk", d_attended, values, preferred_element_type=F32)
        centre = jnp.sum(probs * d_probs, axis=-1, keepdims=True)
        d_scores = (probs * (d_probs - centre)).astype(BF16)
        d_queries = (
            jnp.einsum("bhqk,bkhd->bqhd", d_scores, key_rows, preferred_element_type=F32)
            * score_scale
        )
        d_keys = (
            jnp.einsum("bhqk,bqhd->bkhd", d_scores, queries, preferred_element_type=F32)
            * score_scale
        )
        d_projected = jnp.concatenate(
            [x.astype(BF16).reshape(group_count * row_count, part) for x in (d_queries, d_keys, d_values)],
            axis=1,
        )
        grad_qkv = dot_t(rows_a, d_projected).astype(BF16)
        e = collect(dot_nt(d_projected, qkv_w).astype(BF16))
        gradient = d_middle + norm_backward(e, xhat_a, rstd_a)
        shares[depth] = (grad_qkv, grad_out, grad_up, grad_down)

    def home(term):
        return lax.psum_scatter(term, "fsdp", scatter_dimension=0, tiled=True)

    grads_qkv, grads_out, grads_up, grads_down, gains_a, gains_m = [], [], [], [], [], []
    for depth in reversed(range(layers)):
        grad_qkv, grad_out, grad_up, grad_down = shares[depth]
        rest = [
            grad_up.reshape(shard_count, -1, width),
            grad_down.reshape(shard_count, -1, width),
        ]
        if fine:
            rest.append(grad_out.reshape(shard_count, -1, width))
        else:
            full = jnp.zeros((width, width), BF16)
            full = lax.dynamic_update_slice_in_dim(full, grad_out, me * part, 0)
            rest.append(full.reshape(shard_count, -1, width))
        sizes = [x.shape[1] for x in rest]
        rest = home(jnp.concatenate(rest, axis=1))[0]
        qkv = square.gather(home(grad_qkv))
        if not fine:
            out = square.total(rest[sizes[0] + sizes[1] :])
            rest = rest[: sizes[0] + sizes[1]]
        rest = square.gather(rest)
        up = rest[:, : sizes[0]].reshape(group_count, shard_rows, shard_count, -1)
        up = up.transpose(1, 2, 0, 3).reshape(shard_rows, hidden_units).astype(F32)
        down = rest[:, sizes[0] : sizes[0] + sizes[1]].reshape(-1, width).astype(F32)
        if fine:
            pieces = rest[:, sizes[0] + sizes[1] :].reshape(2, 2, half, width)
            keep = select(core, [pieces[:, 0], pieces[:, 1]])
            give = select(core, [pieces[:, 1], pieces[:, 0]])
            got = lax.ppermute(give, "fsdp", swap_core)
            first = select(core, [keep, got])
            second = select(core, [got, keep])
            out = jnp.stack([first, second], axis=1).reshape(shard_rows, width).astype(F32)
            qkv = qkv.reshape(2, 2, shard_rows, 3 * my_heads, head_size).transpose(2, 3, 1, 0, 4)
        else:
            qkv = qkv.reshape(group_count, shard_rows, 3, part).transpose(1, 2, 0, 3)
        qkv = qkv.reshape(shard_rows, 3 * width).astype(F32)
        gains_a.append(jnp.sum(qkv * w_qkv[depth].astype(F32), axis=1))
        gains_m.append(jnp.sum(up * w_up[depth].astype(F32), axis=1))
        grads_qkv.append(qkv * gain_attn[depth].astype(F32)[:, None])
        grads_up.append(up * gain_mlp[depth].astype(F32)[:, None])
        grads_out.append(out)
        grads_down.append(down)

    high_part = gradient.astype(BF16)
    low_part = (gradient - high_part.astype(F32)).astype(BF16)
    table_term = dot_t(mixing, high_part) + dot_t(mixing, low_part)
    table_share = lax.psum_scatter(table_term.astype(BF16), "fsdp", scatter_dimension=1, tiled=True)
    d_table = square.total(table_share)
    return (
        hidden,
        gradient,
        d_table,
        jnp.stack(gains_a[::-1]),
        jnp.stack(grads_qkv[::-1]),
        jnp.stack(grads_out[::-1]),
        jnp.stack(gains_m[::-1]),
        jnp.stack(grads_up[::-1]),
        jnp.stack(grads_down[::-1]),
    )


VMEM = pltpu.VMEM
LANES = 128


def whole(shape):
    return pl.BlockSpec(tuple(shape), lambda *_: (0,) * len(shape))


def scalars():
    return pl.BlockSpec(memory_space=pltpu.SMEM)


def call(body, outs, args, specs=None, scratch=(), flops=0, reads=0, aliases=None, out_specs=None, limit=40, after=()):
    specs = [whole(a.shape) if s is None else s for a, s in zip(args, specs or [None] * len(args))]
    specs = specs + [pl.BlockSpec(memory_space=pl.ANY)] * len(after)
    count, extra = len(args), len(after)
    out_shape = [jax.ShapeDtypeStruct(shape, dtype) for shape, dtype in outs]
    moved = sum(math.prod(s) * jnp.dtype(d).itemsize for s, d in outs) + reads

    def run(*refs):
        body(*refs[:count], *refs[count + extra :])

    name = body.func.__name__ if isinstance(body, functools.partial) else body.__name__
    return pl.pallas_call(
        run,
        name=name,
        grid=(1,),
        in_specs=specs,
        out_specs=out_specs or [whole(shape) for shape, _ in outs],
        out_shape=out_shape,
        scratch_shapes=list(scratch),
        input_output_aliases=aliases or {},
        cost_estimate=pl.CostEstimate(flops=int(flops), bytes_accessed=int(moved), transcendentals=0),
        compiler_params=pltpu.CompilerParams(vmem_limit_bytes=limit << 20),
    )(*args, *after)


def diagonal(gain_row):
    r = lax.broadcasted_iota(jnp.int32, (LANES, LANES), 0)
    c = lax.broadcasted_iota(jnp.int32, (LANES, LANES), 1)
    return jnp.where(r == c, jnp.broadcast_to(gain_row.astype(F32), (LANES, LANES)), 0.0)


def lane_low(rows):
    return lax.broadcasted_iota(jnp.int32, (rows, LANES), 1) < LANES // 2


def lane_swap(block):
    return jnp.concatenate([block[:, LANES // 2 :], block[:, : LANES // 2]], axis=1)


def pack_attention(who_ref, w_ref, gain_row, keep, got, packed_ref, top):
    me, core = who_ref[0], who_ref[1]
    side, second = me & 1, me >> 1
    out = jnp.where(core == side, keep, got)
    diag = diagonal(gain_row).astype(BF16)
    low = lane_low(LANES)

    def head(t):
        chunk = pl.multiple_of(((t // 4) * 8 + 2 * (t % 4) + side) * LANES, LANES)
        got = dot(diag, w_ref[0, :, pl.ds(chunk, LANES)])
        turned = lane_swap(got)
        if t % 2 == 0:
            return jnp.where(second == 0, got, turned)
        return jnp.where(second == 0, turned, got)

    for u in range(6):
        pair = jnp.where(low, head(2 * u), head(2 * u + 1))
        packed_ref[top : top + LANES, u * LANES : (u + 1) * LANES] = pair.astype(BF16)
    for c in range(4):
        packed_ref[top + c * 32 : top + (c + 1) * 32, 768:1024] = out[:, c * 256 : (c + 1) * 256]


def pack_up(me, up_ref, gain_row, packed_ref, top):
    diag = diagonal(gain_row).astype(BF16)
    for j in range(8):
        chunk = pl.multiple_of((j * 4 + me) * LANES, LANES)
        packed_ref[top : top + LANES, j * LANES : (j + 1) * LANES] = dot(
            diag, up_ref[0, :, pl.ds(chunk, LANES)]
        ).astype(BF16)


def pack_down(me, down_ref, packed_ref, top):
    packed_ref[top : top + LANES, :] = down_ref[0, pl.ds(pl.multiple_of(me * LANES, LANES), LANES), :]


def prepare_first(who_ref, w_ref, gain_a, keep_ref, got_ref, up_ref, gain_m, packed_ref):
    pack_attention(who_ref, w_ref, gain_a[0:1, :], keep_ref[0], got_ref[0], packed_ref, 0)
    pack_up(who_ref[0], up_ref, gain_m[0:1, :], packed_ref, LANES)


def prepare_second(who_ref, w_ref, gain_a, keep_ref, got_ref, down_ref, packed_ref):
    pack_attention(who_ref, w_ref, gain_a[1:2, :], keep_ref[1], got_ref[1], packed_ref, LANES)
    pack_down(who_ref[0], down_ref, packed_ref, 0)


def prepare_third(who_ref, up_ref, gain_m, down_ref, packed_ref):
    pack_up(who_ref[0], up_ref, gain_m[1:2, :], packed_ref, 0)
    pack_down(who_ref[0], down_ref, packed_ref, LANES)


def image_numbers(rows, flag, lens):
    counts = [sum((rows >= t * n).astype(jnp.int32) for t in range(1, most + 1)) for n, most in lens]
    return jnp.where(flag == 1, counts[1], counts[0])


def make_mixing(flag_ref, low_ref, high_ref, mixing_ref, *, lens):
    rows = mixing_ref.shape[0]
    flag = flag_ref[0]

    def spread_rows(index_ref, length, most):
        count = index_ref.shape[0]
        columns = lax.broadcasted_iota(jnp.int32, (count, mixing_ref.shape[1]), 1)
        mix = jnp.zeros((count, mixing_ref.shape[1]), F32)
        for slot in range(4):
            mix = mix + MIX_WEIGHTS[slot] * (index_ref[:, slot : slot + 1] == columns).astype(F32)
        r = lax.broadcasted_iota(jnp.int32, (rows, count), 0)
        c = lax.broadcasted_iota(jnp.int32, (rows, count), 1)
        image = sum((r >= t * length).astype(jnp.int32) for t in range(1, most + 1))
        pick = ((r - image * length == c) & (r < most * length)).astype(BF16)
        return dot(pick, mix.astype(BF16))

    low = spread_rows(low_ref, *lens[0])
    high = spread_rows(high_ref, *lens[1])
    mixing_ref[...] = jnp.where(flag == 1, high, low).astype(BF16)


def write_norm(hidden, xhat_ref):
    xhat_ref[...] = normalize(hidden)[0].astype(BF16)


def join_table(z_ref, p0, p1, p2, p3, out_ref, table):
    for k, piece in enumerate((p0, p1, p2, p3)):
        table[:, pl.ds(pl.multiple_of((z_ref[0] ^ k) * 256, 256), 256)] = piece[...].astype(F32)
    out_ref[...] = table[...].astype(BF16)


def embed(who_ref, tokens_ref, mixing_ref, t0, t1, t2, t3, hidden_ref, xhat_ref, table):
    size = t0.shape[0]
    for k, piece in enumerate((t0, t1, t2, t3)):
        table[pl.ds(pl.multiple_of((who_ref[0] ^ k) * size, 8), size), :] = piece[...].astype(F32)
    rows = table[: mixing_ref.shape[1], :].astype(BF16)
    hidden = tokens_ref[...].astype(F32) + dot(mixing_ref[...], rows)
    hidden_ref[...] = hidden
    write_norm(hidden, xhat_ref)


def added(p0, r1, r2, r3):
    return (p0[...].astype(F32) + r1[...].astype(F32)) + (r2[...].astype(F32) + r3[...].astype(F32))


def add_norm(h_ref, p0, r1, r2, r3, middle_ref, xhat_ref):
    middle = h_ref[...] + added(p0, r1, r2, r3)
    middle_ref[...] = middle
    write_norm(middle, xhat_ref)


def output_parts(a0, a1, a2, a3, down_ref, *outs):
    down = down_ref[...].reshape(-1, down_ref.shape[2])
    for act_ref, out_ref in zip((a0, a1, a2, a3), outs):
        out_ref[...] = dot(act_ref[...], down).astype(BF16)


def add_output(h_ref, p0, r1, r2, r3, out_ref):
    out_ref[...] = h_ref[...] + added(p0, r1, r2, r3)


def add_norm_backward(g_ref, p0, r1, r2, r3, h_ref, d_ref, low_ref):
    d = g_ref[...] + norm_backward(added(p0, r1, r2, r3), *normalize(h_ref[...]))
    d_ref[...] = d
    low_ref[...] = d.astype(BF16)


def out_chunk(packed_ref, c):
    return packed_ref[:, c * 32 : (c + 1) * 32, 768:1024].reshape(256, 256)


def attention_forward(flag_ref, x_ref, w_ref, proj_ref, p_ref, *, lens):
    rows = x_ref.shape[0]
    flag = flag_ref[0]
    width = x_ref.shape[1]
    mask = image_numbers(lax.broadcasted_iota(jnp.int32, (rows, 1), 0), flag, lens) == image_numbers(
        lax.broadcasted_iota(jnp.int32, (1, rows), 1), flag, lens
    )
    for c in range(3):
        w = w_ref[:, :, c * 256 : (c + 1) * 256].reshape(width, 256)
        proj_ref[:, c * 256 : (c + 1) * 256] = dot(x_ref[...], w).astype(BF16)
    low = lane_low(rows)
    zero = jnp.zeros((), BF16)
    for u in range(2):
        q = proj_ref[:, u * LANES : (u + 1) * LANES] * jnp.asarray(0.125, BF16)
        k = proj_ref[:, 256 + u * LANES : 256 + (u + 1) * LANES]
        v = proj_ref[:, 512 + u * LANES : 512 + (u + 1) * LANES]
        total = None
        for keep in (low, ~low):
            s = dot_nt(jnp.where(keep, q, zero), k)
            s = jnp.where(mask, s, NEG_FILL)
            powers = jnp.exp(s - jnp.max(s, axis=-1, keepdims=True))
            probs = powers * (1.0 / jnp.sum(powers, axis=-1, keepdims=True))
            o = dot(probs.astype(BF16), jnp.where(keep, v, zero))
            total = o if total is None else total + o
        proj_ref[:, 768 + u * LANES : 768 + (u + 1) * LANES] = total.astype(BF16)
    for c in range(4):
        p_ref[:, c * 256 : (c + 1) * 256] = dot(proj_ref[:, 768:], out_chunk(w_ref, c)).astype(BF16)


def attention_backward(flag_ref, d_ref, proj_ref, w_ref, dproj_ref, p_ref, *, lens):
    rows, width = d_ref.shape
    flag = flag_ref[0]
    mask = image_numbers(lax.broadcasted_iota(jnp.int32, (rows, 1), 0), flag, lens) == image_numbers(
        lax.broadcasted_iota(jnp.int32, (1, rows), 1), flag, lens
    )
    d_o = sum(dot_nt(d_ref[:, c * 256 : (c + 1) * 256], out_chunk(w_ref, c)) for c in range(4))
    d_o = d_o.astype(BF16)
    low = lane_low(rows)
    zero = jnp.zeros((), BF16)
    scale = jnp.asarray(0.125, BF16)
    for u in range(2):
        q = proj_ref[:, u * LANES : (u + 1) * LANES] * scale
        k = proj_ref[:, 256 + u * LANES : 256 + (u + 1) * LANES]
        v = proj_ref[:, 512 + u * LANES : 512 + (u + 1) * LANES]
        g = d_o[:, u * LANES : (u + 1) * LANES]
        dq = dk = dv = None
        for keep in (low, ~low):
            k_own = jnp.where(keep, k, zero)
            s = jnp.where(mask, dot_nt(k_own, q), NEG_FILL)
            powers = jnp.exp(s - jnp.max(s, axis=0, keepdims=True))
            probs = powers * (1.0 / jnp.sum(powers, axis=0, keepdims=True))
            d_probs = dot_nt(jnp.where(keep, v, zero), g)
            centre = jnp.sum(probs * d_probs, axis=0, keepdims=True)
            d_scores = (probs * (d_probs - centre)).astype(BF16)
            terms = (
                dot_t(d_scores, k_own),
                dot(d_scores, jnp.where(keep, q, zero)),
                dot(probs.astype(BF16), jnp.where(keep, g, zero)),
            )
            dq, dk, dv = terms if dq is None else (dq + terms[0], dk + terms[1], dv + terms[2])
        dproj_ref[:, u * LANES : (u + 1) * LANES] = (dq * 0.125).astype(BF16)
        dproj_ref[:, 256 + u * LANES : 256 + (u + 1) * LANES] = dk.astype(BF16)
        dproj_ref[:, 512 + u * LANES : 512 + (u + 1) * LANES] = dv.astype(BF16)
    total = None
    for c in range(3):
        w = w_ref[:, :, c * 256 : (c + 1) * 256].reshape(width, 256)
        term = dot_nt(dproj_ref[:, c * 256 : (c + 1) * 256], w)
        total = term if total is None else total + term
    p_ref[...] = total.astype(BF16)


def gelu_parts(pre):
    upto = 0.5 * (1.0 + lax.erf(pre * math.sqrt(0.5)))
    density = jnp.exp(-0.5 * pre * pre) * (1.0 / math.sqrt(2.0 * math.pi))
    return pre * upto, upto + pre * density


def mlp_up(x_ref, up_ref, both_ref):
    width = x_ref.shape[1]
    for c in range(4):
        cols = slice(c * 256, (c + 1) * 256)
        act, slope = gelu_parts(dot(x_ref[...], up_ref[:, :, cols].reshape(width, 256)))
        both_ref[0, :, cols] = act.astype(BF16)
        both_ref[1, :, cols] = slope.astype(BF16)


def mlp_down(*refs):
    count = len(refs) // 2
    down = refs[count][...].reshape(-1, refs[count].shape[2])
    for act_ref, out_ref in zip(refs[:count], refs[count + 1 :]):
        out_ref[...] = dot(act_ref[0], down).astype(BF16)


def mlp_backward(d_ref, slope_ref, up_ref, down_ref, dpre_ref, p_ref):
    width = d_ref.shape[1]
    for c in range(4):
        cols = slice(c * 256, (c + 1) * 256)
        d_act = dot_nt(d_ref[...], down_ref[2 * c : 2 * c + 2].reshape(256, width))
        dpre_ref[:, cols] = (d_act * slope_ref[0, :, cols].astype(F32)).astype(BF16)
    p_ref[...] = dot_nt(dpre_ref[...], up_ref[...].reshape(width, width)).astype(BF16)


def mlp_both(x_ref, d_ref, up_ref, down_ref, act_ref, dpre_ref, back_ref):
    width = x_ref.shape[1]
    for c in range(4):
        cols = slice(c * 256, (c + 1) * 256)
        act, slope = gelu_parts(dot(x_ref[...], up_ref[:, :, cols].reshape(width, 256)))
        act_ref[:, cols] = act.astype(BF16)
        d_act = dot_nt(d_ref[...], down_ref[2 * c : 2 * c + 2].reshape(256, width))
        dpre_ref[:, cols] = (d_act * slope).astype(BF16)
    back_ref[...] = dot_nt(dpre_ref[...], up_ref[...].reshape(width, width)).astype(BF16)


def summed(left, right, rows, cols=slice(None)):
    total = None
    for a, b in zip(left, right):
        term = dot_t(a[:, rows], b[:, cols])
        total = term if total is None else total + term
    return total


def stack_rows(blocks, out_ref):
    rows = blocks[0].shape[0]
    tall = -(-rows // 32) * 32
    for k, block in enumerate(blocks):
        out_ref[k * tall + rows // 16 * 16 : (k + 1) * tall, :] = jnp.zeros(
            (tall - rows // 16 * 16, out_ref.shape[1]), BF16
        )
        out_ref[k * tall : k * tall + rows, :] = block


def grads_mlp(*refs):
    x, dpre, act, d, out_ref, left, right = refs[:4], refs[4:8], refs[8:12], refs[12:16], *refs[16:]
    acts = [a[0] if len(a.shape) == 3 else a[...] for a in act]
    pairs = (([a[...] for a in x], dpre), (acts, d))
    for half, (first, second) in enumerate(pairs):
        stack_rows(first, left)
        stack_rows([b[...] for b in second], right)
        for t in range(4):
            total = dot_t(left[:, t * 256 : (t + 1) * 256], right[...]).astype(BF16)
            out_ref[2 * t : 2 * t + 2, half * LANES : (half + 1) * LANES, :] = total.reshape(2, LANES, -1)


def stack_attention(refs, left, right, narrow):
    x, dproj, kept, d = refs[:4], refs[4:8], refs[8:12], refs[12:16]
    stack_rows([a[...] for a in x], left)
    stack_rows([a[...] for a in dproj], right.at[:, :768])
    stack_rows([a[...] for a in kept], narrow)


def grads_attention(*refs):
    out_ref, left, right, narrow = refs[16:]
    stack_attention(refs, left, right, narrow)
    for t in range(4):
        total = dot_t(left[:, t * 256 : (t + 1) * 256], right[:, :768]).astype(BF16)
        out_ref[2 * t : 2 * t + 2, :LANES, :768] = total.reshape(2, LANES, -1)
    stack_rows([a[...] for a in refs[12:16]], right)
    for c in range(4):
        total = dot_t(narrow[...], right[:, c * 256 : (c + 1) * 256])
        out_ref[:, c * 32 : (c + 1) * 32, 768:1024] = total.astype(BF16).reshape(8, 32, 256)


def rows_of(j):
    return pl.ds(pl.multiple_of(j * LANES, LANES), LANES)


def grads_attention_sides(core_ref, *refs):
    theirs, mine, (left, right, narrow) = refs[16:20], refs[20], refs[21:]
    core = core_ref[0]
    stack_attention(refs, left, right, narrow)
    for z in range(4):
        theirs[z][:, :768] = dot_t(left[:, rows_of(z * 2 + 1 - core)], right[:, :768]).astype(BF16)
    for z in range(4):
        mine[z, :, :768] = dot_t(left[:, rows_of(z * 2 + core)], right[:, :768]).astype(BF16)
    stack_rows([a[...] for a in refs[12:16]], right)
    for c in range(4):
        total = dot_t(narrow[...], right[:, c * 256 : (c + 1) * 256]).astype(BF16).reshape(8, 32, 256)
        rows = slice(c * 32, (c + 1) * 32)
        for z in range(4):
            first, second = total[2 * z], total[2 * z + 1]
            theirs[z][rows, 768:1024] = jnp.where(core == 0, second, first)
            mine[z, rows, 768:1024] = jnp.where(core == 0, first, second)


def add_pair(mine_ref, *refs):
    for z in range(4):
        refs[4][z] = (mine_ref[z].astype(F32) + refs[z][...].astype(F32)).astype(BF16)


def last_norm(g_ref, p0, r1, r2, r3, h_ref, mixing_ref, term_ref, d_ref, out_ref, packed, sem):
    d = g_ref[...] + norm_backward(added(p0, r1, r2, r3), *normalize(h_ref[...]))
    d_ref[...] = d
    high = d.astype(BF16)
    low = (d - high.astype(F32)).astype(BF16)
    table = dot_t(mixing_ref[...], high) + dot_t(mixing_ref[...], low)
    packed[...] = jnp.zeros(packed.shape, BF16)
    for j in range(8):
        for c in range(-(-table.shape[0] // 32)):
            size = min(32, table.shape[0] - 32 * c)
            part = table[32 * c : 32 * c + size, j * LANES : (j + 1) * LANES]
            packed[j, :size, c * LANES : (c + 1) * LANES] = part.astype(BF16)
    copy = pltpu.make_async_copy(packed, out_ref.at[:, LANES : LANES + 32, :], sem.at[0])
    copy.start()
    copy.wait()


def unpack_table(refs, out_ref):
    g = [ref[LANES : LANES + 32, :].astype(F32) for ref in refs]
    total = (g[0] + g[1]) + (g[2] + g[3])
    for c in range(-(-out_ref.shape[0] // 32)):
        size = min(32, out_ref.shape[0] - 32 * c)
        out_ref[32 * c : 32 * c + size, :] = total[:size, c * LANES : (c + 1) * LANES]


def finish_mlp(me_ref, *refs, merged):
    g, up_ref, gain_ref, dup_ref, ddown_ref, dgain_ref = refs[:5], refs[5], refs[6], *refs[-3:]
    me = me_ref[0]
    low = 192 if merged else LANES
    column = jnp.sum(diagonal(gain_ref[0]), axis=1, keepdims=True)
    total = jnp.zeros((LANES, LANES), F32)
    downs = [piece[low : low + LANES, :] for piece in g[:3]] + [g[4][:LANES, :]]
    for k, piece in enumerate(downs):
        rows = pl.ds(pl.multiple_of((me ^ k) * LANES, LANES), LANES)
        ddown_ref[0, rows, :] = piece.astype(F32)
    ups = [piece[:LANES, :] for piece in g[:4]]
    for i in range(4):
        got = jnp.where(
            me == i, ups[0], jnp.where(me == i ^ 1, ups[1], jnp.where(me == i ^ 2, ups[2], ups[3]))
        ).astype(F32)
        for j in range(8):
            cols = slice((j * 4 + i) * LANES, (j * 4 + i + 1) * LANES)
            part = got[:, j * LANES : (j + 1) * LANES]
            dup_ref[0, :, cols] = part * column
            total = total + part * up_ref[0, :, cols].astype(F32)
    dgain_ref[0] = jnp.sum(total.T, axis=0, keepdims=True)


def attention_rows(refs):
    if len(refs) == 4:
        return [ref[:LANES, :] for ref in refs]
    rows = [jnp.concatenate([ref[128:192, :], ref[320:384, :]], axis=0) for ref in refs[:3]]
    return rows + [jnp.concatenate([ref[128:192, :] for ref in refs[3:]], axis=0)]


def by_owner(me, pieces, i):
    g0, g1, g2, g3 = pieces
    return jnp.where(me == i, g0, jnp.where(me == i ^ 1, g1, jnp.where(me == i ^ 2, g2, g3)))


def split_out(who_ref, *refs):
    keep_ref, give_ref = refs[-2:]
    packed = [piece[:, 768:] for piece in attention_rows(refs[:-2])]
    me, core = who_ref[0], who_ref[1]
    for second in range(2):
        even, odd = by_owner(me, packed, 2 * second), by_owner(me, packed, 2 * second + 1)
        keep_ref[second] = jnp.where(core == 0, even, odd)
        give_ref[second] = jnp.where(core == 0, odd, even)


def finish_attention(who_ref, *refs, count):
    g, (w_ref, gain_ref, keep_ref, got_ref) = refs[:count], refs[count : count + 4]
    if count == 4:
        unpack_table(g, refs[-1])
        refs = refs[:-1]
    dqkv_ref, dout_ref, dgain_ref = refs[-3:]
    me, core = who_ref[0], who_ref[1]
    column = jnp.sum(diagonal(gain_ref[0]), axis=1, keepdims=True)
    total = jnp.zeros((LANES, LANES), F32)
    low = lane_low(LANES)
    rows = [piece[:, :768] for piece in attention_rows(g)]
    owned = [by_owner(me, rows, i).astype(F32) for i in range(4)]
    for t in range(12):
        u = t // 2
        for side in range(2):
            first = owned[side][:, u * LANES : (u + 1) * LANES]
            second = owned[side + 2][:, u * LANES : (u + 1) * LANES]
            if t % 2 == 0:
                part = jnp.where(low, first, lane_swap(second))
            else:
                part = jnp.where(low, lane_swap(first), second)
            chunk = (t // 4) * 8 + 2 * (t % 4) + side
            cols = slice(chunk * LANES, (chunk + 1) * LANES)
            dqkv_ref[0, :, cols] = part * column
            total = total + part * w_ref[0, :, cols].astype(F32)
    dgain_ref[0] = jnp.sum(total.T, axis=0, keepdims=True)
    for second in range(2):
        keep, got = keep_ref[second], got_ref[second]
        halves = (jnp.where(core == 0, keep, got), jnp.where(core == 0, got, keep))
        for h, part in enumerate(halves):
            for c in range(4):
                top = (2 * second + h) * 32
                dout_ref[0, top : top + 32, c * 256 : (c + 1) * 256] = part[c * 32 : (c + 1) * 32, :].astype(F32)


def local_fast(
    tokens,
    pos_table,
    index_lo,
    index_hi,
    resolution,
    gain_attn,
    w_qkv,
    w_out,
    gain_mlp,
    w_up,
    w_down,
    cotangent,
):
    rows, width = tokens.shape
    layers = w_qkv.shape[0]
    square = Square()
    me = square.me
    me1 = me.reshape(1).astype(jnp.int32)
    shard = lax.axis_index("fsdp")
    core, deep = shard % 2, shard // 2
    deep1 = deep.reshape(1).astype(jnp.int32)
    len_low, len_high = index_lo.shape[0], index_hi.shape[0]
    lens = ((len_low, rows // len_low), (len_high, rows // len_high))
    block = (rows, width)
    blocks = range(4)

    def over_fsdp(x, k):
        return lax.ppermute(x, "fsdp", [(j, j ^ k) for j in range(8)])

    def layer_of(array, depth):
        return pl.BlockSpec((1,) + array.shape[1:], lambda *_: (depth,) + (0,) * (array.ndim - 1))

    who = jnp.stack([me, core]).astype(jnp.int32)
    head_side = me >> 1

    def out_rows(half):
        return lax.dynamic_slice(w_out, (0, (head_side * 2 + half) * 32, 0), (layers, 32, width))

    keep, got = out_rows(core), over_fsdp(out_rows(1 - core), 1)
    gains_a = gain_attn.reshape(layers, 1, LANES)
    gains_m = gain_mlp.reshape(layers, 1, LANES)

    def part(top):
        return pl.BlockSpec((8, LANES, width), lambda *_: (0, top, 0))

    def fetch(body, args, specs, after=()):
        (packed,) = call(
            body, [((2 * LANES, width), BF16)], [who] + args, [scalars()] + specs, after=after, limit=60
        )
        return lax.all_gather(packed, "fsdp", axis=0, tiled=False)

    first_w = fetch(
        prepare_first,
        [w_qkv, gain_attn, keep, got, w_up, gain_mlp],
        [layer_of(w_qkv, 0), None, None, None, layer_of(w_up, 0), None],
    )

    flag = resolution[me]
    flag1 = flag.reshape(1)
    flags = [resolution[owner].reshape(1) for owner in square.owners()]
    shard_count, group_count = 8, resolution.shape[0]
    high_groups = jnp.sum(resolution)
    tokens_low = ((group_count - high_groups) * shard_count * lens[0][1] * len_low).astype(F32)
    tokens_high = (high_groups * shard_count * lens[1][1] * len_high).astype(F32)
    token_share = 2.0 * jnp.where(flag == 1, tokens_high, tokens_low) / (tokens_low + tokens_high)
    live = jnp.where(flag == 1, lens[1][1] * len_high, lens[0][1] * len_low)
    weight = jnp.where(jnp.arange(rows, dtype=jnp.int32) < live, token_share, 0.0)
    gradient = cotangent.astype(F32) * weight[:, None]

    normed = [(block, F32), (block, BF16)]
    size = -(-len_high // 32) * 8
    mine = lax.dynamic_slice(
        jnp.pad(pos_table, ((0, 4 * size - len_high), (0, 0))), (me * size, 0), (size, LANES)
    )
    other = over_fsdp(mine, 1)
    pair = jnp.concatenate([jnp.where(core == 0, mine, other), jnp.where(core == 0, other, mine)], axis=1)
    pieces = [pair] + [over_fsdp(pair, 2 * k) for k in range(1, 4)]
    (mine,) = call(
        join_table,
        [((size, width), BF16)],
        [deep1] + pieces,
        [scalars()] + [None] * 4,
        scratch=[VMEM((size, width), F32)],
    )
    (mixing,) = call(
        functools.partial(make_mixing, lens=lens),
        [((rows, len_high), BF16)],
        [flag1, index_lo, index_hi],
        [scalars(), None, None],
    )
    hidden, xhat = call(
        embed,
        normed,
        [who, tokens, mixing] + square.spread(mine),
        [scalars()] + [None] * 6,
        scratch=[VMEM((4 * size, width), F32)],
    )
    second_w = fetch(
        prepare_second,
        [w_qkv, gain_attn, keep, got, w_down],
        [layer_of(w_qkv, 1), None, None, None, layer_of(w_down, 0)],
        [xhat],
    )
    third_w = fetch(
        prepare_third,
        [w_up, gain_mlp, w_down],
        [layer_of(w_up, 1), None, layer_of(w_down, 1)],
        [xhat],
    )
    attn_w = [(first_w, part(0)), (second_w, part(1))]

    def tie(*values):
        return lax.optimization_barrier(values)

    def tie_last(es, term):
        near, term = tie(es[:3], term)
        far, near, term = tie(es[3], near, term)
        return near + [far], term

    def chain(kernel):
        done = []
        for k in blocks:
            done.append(kernel(k, [d[0] for d in done[-1:]]))
        return done

    def collect(parts):
        return [parts[0]] + [square.swap(parts[k], k) for k in range(1, 4)]

    d_top = square.spread(gradient.astype(BF16))
    saved = []
    for depth in range(layers):
        a_w, a_part = attn_w[depth]
        xs = square.spread(xhat)
        got = chain(
            lambda k, after: call(
                functools.partial(attention_forward, lens=lens),
                [(block, BF16)] * 2,
                [flags[k], xs[k], a_w],
                [scalars(), None, a_part],
                after=after,
            )
        )
        kept = [g[0] for g in got]
        es = collect([g[1] for g in got])
        if depth == 0:
            es, d_top = tie(es, d_top)
        before, (middle, xhat) = hidden, call(add_norm, normed, [hidden] + es)
        if depth > 0:
            xhat, third_w = tie(xhat, third_w)
        ms = square.spread(xhat)
        if depth < layers - 1:
            acts = chain(
                lambda k, after: call(
                    mlp_up, [((2,) + block, BF16)], [ms[k], first_w], [None, part(1)], after=after
                )
            )
            acts = [a[0] for a in acts]
            first_half = pl.BlockSpec((1,) + block, lambda *_: (0, 0, 0))
            parts = call(
                mlp_down, [(block, BF16)] * 3, acts[1:] + [second_w], [first_half] * 3 + [part(0)], after=acts[:1]
            )
            (own,) = call(
                mlp_down, [(block, BF16)], [acts[0], second_w], [first_half, part(0)], after=parts[:1]
            )
            parts = [own] + list(parts)
            saved.append((before, xs, kept, middle, ms, acts))
            hidden, xhat = call(add_norm, normed, [middle] + collect(parts))
        else:
            got = chain(
                lambda k, after: call(
                    mlp_both,
                    [(block, BF16)] * 3,
                    [ms[k], d_top[k], third_w, third_w],
                    [None, None, part(0), part(1)],
                    after=after,
                )
            )
            acts, dpres, backs = ([g[t] for g in got] for t in range(3))
            top_acts = acts
            saved.append((before, xs, kept, middle, ms, acts))

    def far_halves(x, y):
        half = x.shape[0] // 2
        return [square.swap(x[:half], 2), square.swap(y[half:], 1)]

    core1 = core.reshape(1).astype(jnp.int32)
    tall = 4 * (-(-rows // 32) * 32)

    def home(term):
        return lax.psum_scatter(term, "fsdp", scatter_dimension=0, tiled=False)

    homes_m, homes_a = [None] * layers, [None] * layers
    for depth in reversed(range(layers)):
        top = depth == layers - 1
        a_w, a_part = attn_w[depth]
        before, xs, kept, middle, ms, acts = saved[depth]
        ds = d_top if top else square.spread(low)
        if not top:
            second_half = pl.BlockSpec((1,) + block, lambda *_: (1, 0, 0))
            got = chain(
                lambda k, after: call(
                    mlp_backward,
                    [(block, BF16)] * 2,
                    [ds[k], acts[k], first_w, second_w],
                    [None, second_half, part(1), part(0)],
                    after=after or [homes_m[1]],
                )
            )
            dpres, backs = ([g[t] for g in got] for t in range(2))
        es = collect(backs)
        first_half = pl.BlockSpec((1,) + block, lambda *_: (0, 0, 0))
        (term,) = call(
            grads_mlp,
            [((8, 2 * LANES, width), BF16)],
            list(ms) + list(dpres) + list(acts) + list(ds),
            [None] * 8 + [None if top else first_half] * 4 + [None] * 4,
            scratch=[VMEM((tall, width), BF16)] * 2,
        )
        es, term = tie_last(es, term)
        homes_m[depth] = home(term)
        d_middle, low = call(add_norm_backward, normed, [gradient] + es + [middle], limit=60)
        if not top:
            m, a = homes_m[1], homes_a[1]
            merged = jnp.concatenate([m[:LANES], a[:64], m[LANES:], a[64:]], axis=0)
        ds = square.spread(low)
        got = chain(
            lambda k, after: call(
                functools.partial(attention_backward, lens=lens),
                [((rows, 768), BF16), (block, BF16)],
                [flags[k], ds[k], kept[k], a_w],
                [scalars(), None, None, a_part],
                after=after or ([] if top else [merged]),
            )
        )
        dprojs = [g[0] for g in got]
        es = collect([g[1] for g in got])
        out_part = pl.BlockSpec((rows, 256), lambda *_: (0, 3))
        stacks = [VMEM((tall, width), BF16)] * 2 + [VMEM((tall, 256), BF16)]
        operands = list(xs) + dprojs + list(kept) + list(ds)
        specs = [None] * 8 + [out_part] * 4 + [None] * 4
        if top:
            *theirs, mine = call(
                grads_attention_sides,
                [((LANES, width), BF16)] * 4 + [((4, LANES, width), BF16)],
                [core1] + operands,
                [scalars()] + specs,
                scratch=stacks,
            )
            got = [over_fsdp(part, 1) for part in theirs]
            es, mine = tie_last(es, mine)
            (term,) = call(add_pair, [(mine.shape, BF16)], [mine] + got, after=[es[3]])
            es, term = tie(es, term)
            homes_a[depth] = lax.psum_scatter(
                term, "fsdp", scatter_dimension=0, tiled=False, axis_index_groups=[[0, 2, 4, 6], [1, 3, 5, 7]]
            )
            last_middle = middle
            gradient, low = call(add_norm_backward, normed, [d_middle] + es + [before], limit=60)
        else:
            near = [square.swap(merged, 1), square.swap(merged, 2)]
            (term,) = call(grads_attention, [((8, LANES + 32, width), BF16)], operands, specs, after=near, scratch=stacks)
            es, term = tie_last(es, term)
            anywhere = pl.BlockSpec(memory_space=pl.ANY)
            gradient, term = call(
                last_norm,
                [(block, F32), (term.shape, BF16)],
                [d_middle] + es + [before, mixing, term],
                [None] * 7 + [anywhere],
                out_specs=[whole(block), anywhere],
                aliases={7: 1},
                scratch=[VMEM((8, 32, width), BF16), pltpu.SemaphoreType.DMA((1,))],
            )
            homes_a[0] = home(term)

    merged = [merged, *near] + far_halves(*near)

    outs = call(
        output_parts, [(block, BF16)] * 4, top_acts + [third_w], [None] * 4 + [part(1)], after=[gradient]
    )
    (output,) = call(add_output, [(block, F32)], [last_middle] + collect(outs))
    homes_m[0], gradient = tie(homes_m[0], gradient)
    x, y = square.swap(homes_m[0], 1), square.swap(homes_m[0], 2)
    homes_m[0] = [homes_m[0], x, y] + far_halves(x, y)
    big = [None] * 6

    def finish(body, depth, args, shapes, prior):
        extra = [] if prior[0] is None else prior
        specs = [layer_of(a, depth) if a is w_up or a is w_qkv or a is gains_a or a is gains_m else None for a in args]
        return call(
            body,
            [(shape, F32) for shape in shapes],
            [who] + args + extra,
            [scalars()] + specs + [pl.BlockSpec(memory_space=pl.ANY)] * len(extra),
            aliases={1 + len(args) + t: t for t in range(len(extra))},
            out_specs=[
                layer_of(jax.ShapeDtypeStruct(shape, F32), depth) if len(shape) == 3 else whole(shape)
                for shape in shapes
            ],
        )

    def finish_m(depth, pieces):
        shapes = [w_up.shape, w_down.shape, gains_m.shape]
        body = functools.partial(finish_mlp, merged=depth > 0)
        big[3:] = finish(body, depth, pieces + [w_up, gains_m], shapes, big[3:])

    def finish_a(depth, pieces):
        keep, give = call(
            split_out, [((2, LANES, 256), BF16)] * 2, [who] + pieces, [scalars()] + [None] * len(pieces)
        )
        shapes = [w_qkv.shape, w_out.shape, gains_a.shape]
        body = functools.partial(finish_attention, count=len(pieces))
        args = pieces + [w_qkv, gains_a, keep, over_fsdp(give, 1)]
        if len(pieces) == 4:
            shapes = shapes + [(len_high, LANES)]
        big[:3] = finish(body, depth, args, shapes, big[:3])

    finish_m(1, merged)
    finish_a(1, merged)
    homes_a[0], homes_m[0], big, output = tie(homes_a[0], homes_m[0], big, output)
    pieces = square.spread(homes_a[0])
    finish_m(0, homes_m[0])
    pieces, big = tie(pieces, big)
    finish_a(0, pieces)
    d_table = big.pop(3)
    return (
        output,
        gradient,
        d_table,
        big[2].reshape(layers, LANES),
        big[0],
        big[1],
        big[5].reshape(layers, LANES),
        big[3],
        big[4],
    )


def solution(mesh):
    in_specs = (
        P(("dp", "fsdp"), None),
        P(None, "fsdp"),
        P(),
        P(),
        P(),
        P(None, "fsdp"),
        P(None, "fsdp", None),
        P(None, "fsdp", None),
        P(None, "fsdp"),
        P(None, "fsdp", None),
        P(None, "fsdp", None),
        P(("dp", "fsdp"), None),
    )
    out_specs = (
        P(("dp", "fsdp"), None),
        P(("dp", "fsdp"), None),
        P(None, "fsdp"),
        P(None, "fsdp"),
        P(None, "fsdp", None),
        P(None, "fsdp", None),
        P(None, "fsdp"),
        P(None, "fsdp", None),
        P(None, "fsdp", None),
    )
    fast = mesh.shape["dp"] == 4 and mesh.shape["fsdp"] == 8
    local = local_fast if fast else local_general
    return jax.shard_map(local, mesh=mesh, in_specs=in_specs, out_specs=out_specs, check_vma=False)
```

```python
import functools
import math

import jax
import jax.numpy as jnp
from jax import lax
from jax.experimental import pallas as pl
from jax.experimental.pallas import tpu as pltpu
from jax.sharding import PartitionSpec as P

HEADS = 16
EPS = 1e-06
NEG_FILL = -1e30
MIX_WEIGHTS = (0.5, 0.25, 0.125, 0.125)
BF16 = jnp.bfloat16
F32 = jnp.float32


def dot(a, b):
    return jnp.dot(a, b, preferred_element_type=F32)


def dot_t(a, b):
    return lax.dot_general(a, b, (((0,), (0,)), ((), ())), preferred_element_type=F32)


def dot_nt(a, b):
    return lax.dot_general(a, b, (((1,), (1,)), ((), ())), preferred_element_type=F32)


def normalize(hidden):
    center = hidden - jnp.mean(hidden, axis=-1, keepdims=True)
    rstd = lax.rsqrt(jnp.mean(center * center, axis=-1, keepdims=True) + EPS)
    return center * rstd, rstd


def norm_backward(e, xhat, rstd):
    return rstd * (
        e
        - jnp.mean(e, axis=-1, keepdims=True)
        - xhat * jnp.mean(e * xhat, axis=-1, keepdims=True)
    )


def gelu_exact(pre_act):
    return jax.nn.gelu(pre_act, approximate=False)


class Square:
    def __init__(self):
        self.count = lax.axis_size("dp")
        self.me = lax.axis_index("dp")
        self.pairs = self.count == 4

    def owners(self):
        if self.pairs:
            return [self.me ^ k for k in range(self.count)]
        return [jnp.int32(k) for k in range(self.count)]

    def swap(self, block, k):
        return lax.ppermute(block, "dp", [(i, i ^ k) for i in range(self.count)])

    def spread(self, block):
        if self.pairs:
            return [block] + [self.swap(block, k) for k in range(1, self.count)]
        full = lax.all_gather(block, "dp")
        return [full[k] for k in range(self.count)]

    def collect(self, parts):
        if self.pairs:
            total = parts[0].astype(F32)
            for k in range(1, self.count):
                total = total + self.swap(parts[k].astype(BF16), k).astype(F32)
            return total
        stacked = jnp.stack([part.astype(BF16) for part in parts])
        return lax.psum_scatter(stacked, "dp", scatter_dimension=0, tiled=False).astype(F32)

    def gather(self, piece):
        if not self.pairs:
            return lax.all_gather(piece, "dp")
        got = [piece] + [self.swap(piece, k) for k in range(1, self.count)]
        odd = (self.me & 1) == 1
        high = (self.me & 2) == 2
        low_pair = (jnp.where(odd, got[1], got[0]), jnp.where(odd, got[0], got[1]))
        far_pair = (jnp.where(odd, got[3], got[2]), jnp.where(odd, got[2], got[3]))
        return jnp.stack(
            [
                jnp.where(high, far_pair[0], low_pair[0]),
                jnp.where(high, far_pair[1], low_pair[1]),
                jnp.where(high, low_pair[0], far_pair[0]),
                jnp.where(high, low_pair[1], far_pair[1]),
            ]
        )

    def total(self, piece):
        if not self.pairs:
            return lax.psum(piece.astype(BF16), "dp").astype(F32)
        own = piece.astype(BF16)
        got = [own.astype(F32)] + [self.swap(own, k).astype(F32) for k in range(1, self.count)]
        return (got[0] + got[1]) + (got[2] + got[3])


def select(index, choices):
    out = choices[0]
    for k in range(1, len(choices)):
        out = jnp.where(index == k, choices[k], out)
    return out


def local_general(
    tokens,
    pos_table,
    index_lo,
    index_hi,
    resolution,
    gain_attn,
    w_qkv,
    w_out,
    gain_mlp,
    w_up,
    w_down,
    cotangent,
):
    row_count, width = tokens.shape
    layers, shard_rows, _ = w_qkv.shape
    hidden_units = w_up.shape[2]
    shard_count = lax.axis_size("fsdp")
    shard = lax.axis_index("fsdp")
    square = Square()
    group_count = square.count
    me = square.me
    head_size = width // HEADS
    my_heads = HEADS // group_count
    part = my_heads * head_size
    unit_part = hidden_units // group_count
    fine = square.pairs and shard_count * 2 == HEADS
    score_scale = 1.0 / math.sqrt(head_size)
    len_low = index_lo.shape[0]
    len_high = index_hi.shape[0]

    row_ids = jnp.arange(row_count, dtype=jnp.int32)

    def layout(flag):
        length = jnp.where(flag == 1, len_high, len_low).astype(jnp.int32)
        images = jnp.where(flag == 1, row_count // len_high, row_count // len_low).astype(jnp.int32)
        live = row_ids < images * length
        return live, jnp.where(live, row_ids // length, images)

    flag = resolution[me]
    live_rows, _ = layout(flag)
    block_ids = jnp.stack([layout(resolution[owner])[1] for owner in square.owners()])
    same_image = block_ids[:, :, None] == block_ids[:, None, :]
    picked = jnp.where(flag == 1, index_hi[row_ids % len_high], index_lo[row_ids % len_low])
    table_ids = jnp.arange(len_high, dtype=jnp.int32)
    mixing = jnp.zeros((row_count, len_high), F32)
    for slot in range(4):
        mixing = mixing + MIX_WEIGHTS[slot] * (
            picked[:, slot : slot + 1] == table_ids[None, :]
        ).astype(F32)
    mixing = (mixing * live_rows[:, None].astype(F32)).astype(BF16)
    high_groups = jnp.sum(resolution)
    tokens_low = (
        (group_count - high_groups) * shard_count * (row_count // len_low) * len_low
    ).astype(F32)
    tokens_high = (high_groups * shard_count * (row_count // len_high) * len_high).astype(F32)
    token_share = 2.0 * jnp.where(flag == 1, tokens_high, tokens_low) / (tokens_low + tokens_high)
    weight = jnp.where(live_rows, token_share, 0.0)

    half = shard_rows // 4
    core = shard % 2
    swap_core = [(j, j ^ 1) for j in range(shard_count)]
    pair_side, head_side = me & 1, (me >> 1) & 1

    def qkv_part(w):
        if fine:
            view = w.reshape(shard_rows, 3 * HEADS // 4, 2, 2, head_size)
            view = select(pair_side, [view[:, :, 0], view[:, :, 1]])
            view = select(head_side, [view[:, :, 0], view[:, :, 1]])
            return view.reshape(shard_rows, 3 * part)
        view = w.reshape(shard_rows, 3, group_count, part)
        return lax.dynamic_index_in_dim(view, me, 2, keepdims=False).reshape(shard_rows, 3 * part)

    def up_part(w):
        view = w.reshape(shard_rows, shard_count, group_count, unit_part // shard_count)
        return lax.dynamic_index_in_dim(view, me, 2, keepdims=False).reshape(shard_rows, unit_part)

    def down_part(w):
        rows = unit_part // shard_count
        return lax.dynamic_slice_in_dim(w, me * rows, rows, 0)

    def out_part(w):
        if fine:
            view = w.reshape(2, 2, half, width)
            mine = select(head_side, [view[0], view[1]])
            keep = select(core, [mine[0], mine[1]])
            give = select(core, [mine[1], mine[0]])
            got = lax.ppermute(give, "fsdp", swap_core)
            return jnp.where(core == pair_side, keep, got)
        return w

    def fetch(piece):
        return lax.all_gather(piece, "fsdp", axis=0, tiled=False)

    weights = []
    table = lax.all_gather(pos_table, "fsdp", axis=1, tiled=True)
    for depth in range(layers):
        gain_a = gain_attn[depth].astype(F32)[:, None]
        gain_m = gain_mlp[depth].astype(F32)[:, None]
        qkv = (qkv_part(w_qkv[depth]).astype(F32) * gain_a).astype(BF16)
        up = (up_part(w_up[depth]).astype(F32) * gain_m).astype(BF16)
        down = down_part(w_down[depth])
        out = out_part(w_out[depth])
        qkv_all = fetch(qkv).reshape(width, 3 * part)
        a = up.size // width
        b = a + down.shape[0]
        rest = fetch(jnp.concatenate([up.reshape(a, width), down, out], axis=0))
        up_all = rest[:, :a].reshape(width, unit_part)
        down_all = rest[:, a:b].reshape(unit_part, width)
        out_all = rest[:, b:].reshape(-1, width)
        if not fine:
            out_all = lax.dynamic_slice_in_dim(out_all, me * part, part, 0)
        weights.append((qkv_all, out_all, up_all, down_all))

    def split_heads(block):
        return block.reshape(group_count, row_count, my_heads, head_size)

    def scores_of(queries, key_rows):
        scores = (
            jnp.einsum("bqhd,bkhd->bhqk", queries, key_rows, preferred_element_type=F32)
            * score_scale
        )
        return jnp.where(same_image[:, None], scores, NEG_FILL)

    def spread(block):
        return jnp.concatenate(square.spread(block), axis=0)

    def collect(partial):
        return square.collect([partial[k * row_count : (k + 1) * row_count] for k in range(group_count)])

    hidden = tokens.astype(F32) + dot(mixing, table)
    saved = []
    for depth in range(layers):
        qkv_w, out_w, up_w, down_w = weights[depth]
        xhat_a, rstd_a = normalize(hidden)
        rows_a = spread(xhat_a.astype(BF16))
        projected = dot(rows_a, qkv_w).astype(BF16)
        queries = split_heads(projected[:, :part])
        key_rows = split_heads(projected[:, part : 2 * part])
        values = split_heads(projected[:, 2 * part :])
        scores = scores_of(queries, key_rows)
        row_max = jnp.max(scores, axis=-1, keepdims=True)
        powers = jnp.exp(scores - row_max)
        row_total = jnp.sum(powers, axis=-1, keepdims=True)
        log_total = row_max + jnp.log(row_total)
        probs = (powers / row_total).astype(BF16)
        attended = jnp.einsum("bhqk,bkhd->bqhd", probs, values, preferred_element_type=F32)
        attended = attended.reshape(group_count * row_count, part).astype(BF16)
        middle = hidden + collect(dot(attended, out_w).astype(BF16))
        xhat_m, rstd_m = normalize(middle)
        rows_m = spread(xhat_m.astype(BF16))
        pre_act = dot(rows_m, up_w)
        activated = gelu_exact(pre_act).astype(BF16)
        result = middle + collect(dot(activated, down_w).astype(BF16))
        saved.append(
            (xhat_a, rstd_a, rows_a, queries, key_rows, values, log_total, attended,
             xhat_m, rstd_m, rows_m, pre_act, activated)
        )
        hidden = result

    gradient = cotangent.astype(F32) * weight[:, None]
    shares = [None] * layers
    for depth in reversed(range(layers)):
        qkv_w, out_w, up_w, down_w = weights[depth]
        (xhat_a, rstd_a, rows_a, queries, key_rows, values, log_total, attended,
         xhat_m, rstd_m, rows_m, pre_act, activated) = saved[depth]
        d_result = spread(gradient.astype(BF16))
        grad_down = dot_t(activated, d_result).astype(BF16)
        d_activated = dot_nt(d_result, down_w)
        _, pullback = jax.vjp(gelu_exact, pre_act)
        d_pre = pullback(d_activated)[0].astype(BF16)
        grad_up = dot_t(rows_m, d_pre).astype(BF16)
        e = collect(dot_nt(d_pre, up_w).astype(BF16))
        d_middle = gradient + norm_backward(e, xhat_m, rstd_m)
        d_attn = spread(d_middle.astype(BF16))
        grad_out = dot_t(attended, d_attn).astype(BF16)
        d_attended = split_heads(dot_nt(d_attn, out_w).astype(BF16))
        probs = jnp.exp(scores_of(queries, key_rows) - log_total)
        d_values = jnp.einsum(
            "bhqk,bqhd->bkhd", probs.astype(BF16), d_attended, preferred_element_type=F32
        )
        d_probs = jnp.einsum("bqhd,bkhd->bhqk", d_attended, values, preferred_element_type=F32)
        centre = jnp.sum(probs * d_probs, axis=-1, keepdims=True)
        d_scores = (probs * (d_probs - centre)).astype(BF16)
        d_queries = (
            jnp.einsum("bhqk,bkhd->bqhd", d_scores, key_rows, preferred_element_type=F32)
            * score_scale
        )
        d_keys = (
            jnp.einsum("bhqk,bqhd->bkhd", d_scores, queries, preferred_element_type=F32)
            * score_scale
        )
        d_projected = jnp.concatenate(
            [x.astype(BF16).reshape(group_count * row_count, part) for x in (d_queries, d_keys, d_values)],
            axis=1,
        )
        grad_qkv = dot_t(rows_a, d_projected).astype(BF16)
        e = collect(dot_nt(d_projected, qkv_w).astype(BF16))
        gradient = d_middle + norm_backward(e, xhat_a, rstd_a)
        shares[depth] = (grad_qkv, grad_out, grad_up, grad_down)

    def home(term):
        return lax.psum_scatter(term, "fsdp", scatter_dimension=0, tiled=True)

    grads_qkv, grads_out, grads_up, grads_down, gains_a, gains_m = [], [], [], [], [], []
    for depth in reversed(range(layers)):
        grad_qkv, grad_out, grad_up, grad_down = shares[depth]
        rest = [
            grad_up.reshape(shard_count, -1, width),
            grad_down.reshape(shard_count, -1, width),
        ]
        if fine:
            rest.append(grad_out.reshape(shard_count, -1, width))
        else:
            full = jnp.zeros((width, width), BF16)
            full = lax.dynamic_update_slice_in_dim(full, grad_out, me * part, 0)
            rest.append(full.reshape(shard_count, -1, width))
        sizes = [x.shape[1] for x in rest]
        rest = home(jnp.concatenate(rest, axis=1))[0]
        qkv = square.gather(home(grad_qkv))
        if not fine:
            out = square.total(rest[sizes[0] + sizes[1] :])
            rest = rest[: sizes[0] + sizes[1]]
        rest = square.gather(rest)
        up = rest[:, : sizes[0]].reshape(group_count, shard_rows, shard_count, -1)
        up = up.transpose(1, 2, 0, 3).reshape(shard_rows, hidden_units).astype(F32)
        down = rest[:, sizes[0] : sizes[0] + sizes[1]].reshape(-1, width).astype(F32)
        if fine:
            pieces = rest[:, sizes[0] + sizes[1] :].reshape(2, 2, half, width)
            keep = select(core, [pieces[:, 0], pieces[:, 1]])
            give = select(core, [pieces[:, 1], pieces[:, 0]])
            got = lax.ppermute(give, "fsdp", swap_core)
            first = select(core, [keep, got])
            second = select(core, [got, keep])
            out = jnp.stack([first, second], axis=1).reshape(shard_rows, width).astype(F32)
            qkv = qkv.reshape(2, 2, shard_rows, 3 * my_heads, head_size).transpose(2, 3, 1, 0, 4)
        else:
            qkv = qkv.reshape(group_count, shard_rows, 3, part).transpose(1, 2, 0, 3)
        qkv = qkv.reshape(shard_rows, 3 * width).astype(F32)
        gains_a.append(jnp.sum(qkv * w_qkv[depth].astype(F32), axis=1))
        gains_m.append(jnp.sum(up * w_up[depth].astype(F32), axis=1))
        grads_qkv.append(qkv * gain_attn[depth].astype(F32)[:, None])
        grads_up.append(up * gain_mlp[depth].astype(F32)[:, None])
        grads_out.append(out)
        grads_down.append(down)

    high_part = gradient.astype(BF16)
    low_part = (gradient - high_part.astype(F32)).astype(BF16)
    table_term = dot_t(mixing, high_part) + dot_t(mixing, low_part)
    table_share = lax.psum_scatter(table_term.astype(BF16), "fsdp", scatter_dimension=1, tiled=True)
    d_table = square.total(table_share)
    return (
        hidden,
        gradient,
        d_table,
        jnp.stack(gains_a[::-1]),
        jnp.stack(grads_qkv[::-1]),
        jnp.stack(grads_out[::-1]),
        jnp.stack(gains_m[::-1]),
        jnp.stack(grads_up[::-1]),
        jnp.stack(grads_down[::-1]),
    )


VMEM = pltpu.VMEM
LANES = 128


def whole(shape):
    return pl.BlockSpec(tuple(shape), lambda *_: (0,) * len(shape))


def scalars():
    return pl.BlockSpec(memory_space=pltpu.SMEM)


def call(body, outs, args, specs=None, scratch=(), flops=0, reads=0, aliases=None, out_specs=None, limit=40, after=()):
    specs = [whole(a.shape) if s is None else s for a, s in zip(args, specs or [None] * len(args))]
    specs = specs + [pl.BlockSpec(memory_space=pl.ANY)] * len(after)
    count, extra = len(args), len(after)
    out_shape = [jax.ShapeDtypeStruct(shape, dtype) for shape, dtype in outs]
    moved = sum(math.prod(s) * jnp.dtype(d).itemsize for s, d in outs) + reads

    def run(*refs):
        body(*refs[:count], *refs[count + extra :])

    name = body.func.__name__ if isinstance(body, functools.partial) else body.__name__
    return pl.pallas_call(
        run,
        name=name,
        grid=(1,),
        in_specs=specs,
        out_specs=out_specs or [whole(shape) for shape, _ in outs],
        out_shape=out_shape,
        scratch_shapes=list(scratch),
        input_output_aliases=aliases or {},
        cost_estimate=pl.CostEstimate(flops=int(flops), bytes_accessed=int(moved), transcendentals=0),
        compiler_params=pltpu.CompilerParams(vmem_limit_bytes=limit << 20),
    )(*args, *after)


def diagonal(gain_row):
    r = lax.broadcasted_iota(jnp.int32, (LANES, LANES), 0)
    c = lax.broadcasted_iota(jnp.int32, (LANES, LANES), 1)
    return jnp.where(r == c, jnp.broadcast_to(gain_row.astype(F32), (LANES, LANES)), 0.0)


def lane_low(rows):
    return lax.broadcasted_iota(jnp.int32, (rows, LANES), 1) < LANES // 2


def lane_swap(block):
    return jnp.concatenate([block[:, LANES // 2 :], block[:, : LANES // 2]], axis=1)


def pack_attention(who_ref, w_ref, gain_row, keep, got, packed_ref, top):
    me, core = who_ref[0], who_ref[1]
    side, second = me & 1, me >> 1
    out = jnp.where(core == side, keep, got)
    diag = diagonal(gain_row).astype(BF16)
    low = lane_low(LANES)

    def head(t):
        chunk = pl.multiple_of(((t // 4) * 8 + 2 * (t % 4) + side) * LANES, LANES)
        got = dot(diag, w_ref[0, :, pl.ds(chunk, LANES)])
        turned = lane_swap(got)
        if t % 2 == 0:
            return jnp.where(second == 0, got, turned)
        return jnp.where(second == 0, turned, got)

    for u in range(6):
        pair = jnp.where(low, head(2 * u), head(2 * u + 1))
        packed_ref[top : top + LANES, u * LANES : (u + 1) * LANES] = pair.astype(BF16)
    for c in range(4):
        packed_ref[top + c * 32 : top + (c + 1) * 32, 768:1024] = out[:, c * 256 : (c + 1) * 256]


def pack_up(me, up_ref, gain_row, packed_ref, top):
    diag = diagonal(gain_row).astype(BF16)
    for j in range(8):
        chunk = pl.multiple_of((j * 4 + me) * LANES, LANES)
        packed_ref[top : top + LANES, j * LANES : (j + 1) * LANES] = dot(
            diag, up_ref[0, :, pl.ds(chunk, LANES)]
        ).astype(BF16)


def pack_down(me, down_ref, packed_ref, top):
    packed_ref[top : top + LANES, :] = down_ref[0, pl.ds(pl.multiple_of(me * LANES, LANES), LANES), :]


def prepare_first(who_ref, w_ref, gain_a, keep_ref, got_ref, up_ref, gain_m, packed_ref):
    pack_attention(who_ref, w_ref, gain_a[0:1, :], keep_ref[0], got_ref[0], packed_ref, 0)
    pack_up(who_ref[0], up_ref, gain_m[0:1, :], packed_ref, LANES)


def prepare_second(who_ref, w_ref, gain_a, keep_ref, got_ref, down_ref, packed_ref):
    pack_attention(who_ref, w_ref, gain_a[1:2, :], keep_ref[1], got_ref[1], packed_ref, LANES)
    pack_down(who_ref[0], down_ref, packed_ref, 0)


def prepare_third(who_ref, up_ref, gain_m, down_ref, packed_ref):
    pack_up(who_ref[0], up_ref, gain_m[1:2, :], packed_ref, 0)
    pack_down(who_ref[0], down_ref, packed_ref, LANES)


def image_numbers(rows, flag, lens):
    counts = [sum((rows >= t * n).astype(jnp.int32) for t in range(1, most + 1)) for n, most in lens]
    return jnp.where(flag == 1, counts[1], counts[0])


def make_mixing(flag_ref, low_ref, high_ref, mixing_ref, *, lens):
    rows = mixing_ref.shape[0]
    flag = flag_ref[0]

    def spread_rows(index_ref, length, most):
        count = index_ref.shape[0]
        columns = lax.broadcasted_iota(jnp.int32, (count, mixing_ref.shape[1]), 1)
        mix = jnp.zeros((count, mixing_ref.shape[1]), F32)
        for slot in range(4):
            mix = mix + MIX_WEIGHTS[slot] * (index_ref[:, slot : slot + 1] == columns).astype(F32)
        r = lax.broadcasted_iota(jnp.int32, (rows, count), 0)
        c = lax.broadcasted_iota(jnp.int32, (rows, count), 1)
        image = sum((r >= t * length).astype(jnp.int32) for t in range(1, most + 1))
        pick = ((r - image * length == c) & (r < most * length)).astype(BF16)
        return dot(pick, mix.astype(BF16))

    low = spread_rows(low_ref, *lens[0])
    high = spread_rows(high_ref, *lens[1])
    mixing_ref[...] = jnp.where(flag == 1, high, low).astype(BF16)


def write_norm(hidden, xhat_ref):
    xhat_ref[...] = normalize(hidden)[0].astype(BF16)


def join_table(z_ref, p0, p1, p2, p3, out_ref, table):
    for k, piece in enumerate((p0, p1, p2, p3)):
        table[:, pl.ds(pl.multiple_of((z_ref[0] ^ k) * 256, 256), 256)] = piece[...].astype(F32)
    out_ref[...] = table[...].astype(BF16)


def embed(who_ref, tokens_ref, mixing_ref, t0, t1, t2, t3, hidden_ref, xhat_ref, table):
    size = t0.shape[0]
    for k, piece in enumerate((t0, t1, t2, t3)):
        table[pl.ds(pl.multiple_of((who_ref[0] ^ k) * size, 8), size), :] = piece[...].astype(F32)
    rows = table[: mixing_ref.shape[1], :].astype(BF16)
    hidden = tokens_ref[...].astype(F32) + dot(mixing_ref[...], rows)
    hidden_ref[...] = hidden
    write_norm(hidden, xhat_ref)


def added(p0, r1, r2, r3):
    return (p0[...].astype(F32) + r1[...].astype(F32)) + (r2[...].astype(F32) + r3[...].astype(F32))


def add_norm(h_ref, p0, r1, r2, r3, middle_ref, xhat_ref):
    middle = h_ref[...] + added(p0, r1, r2, r3)
    middle_ref[...] = middle
    write_norm(middle, xhat_ref)


def output_parts(a0, a1, a2, a3, down_ref, *outs):
    down = down_ref[...].reshape(-1, down_ref.shape[2])
    for act_ref, out_ref in zip((a0, a1, a2, a3), outs):
        out_ref[...] = dot(act_ref[...], down).astype(BF16)


def add_output(h_ref, p0, r1, r2, r3, out_ref):
    out_ref[...] = h_ref[...] + added(p0, r1, r2, r3)


def add_norm_backward(g_ref, p0, r1, r2, r3, h_ref, d_ref, low_ref):
    d = g_ref[...] + norm_backward(added(p0, r1, r2, r3), *normalize(h_ref[...]))
    d_ref[...] = d
    low_ref[...] = d.astype(BF16)


def out_chunk(packed_ref, c):
    return packed_ref[:, c * 32 : (c + 1) * 32, 768:1024].reshape(256, 256)


def attention_forward(flag_ref, x_ref, w_ref, proj_ref, p_ref, *, lens):
    rows = x_ref.shape[0]
    flag = flag_ref[0]
    width = x_ref.shape[1]
    mask = image_numbers(lax.broadcasted_iota(jnp.int32, (rows, 1), 0), flag, lens) == image_numbers(
        lax.broadcasted_iota(jnp.int32, (1, rows), 1), flag, lens
    )
    for c in range(3):
        w = w_ref[:, :, c * 256 : (c + 1) * 256].reshape(width, 256)
        proj_ref[:, c * 256 : (c + 1) * 256] = dot(x_ref[...], w).astype(BF16)
    low = lane_low(rows)
    zero = jnp.zeros((), BF16)
    for u in range(2):
        q = proj_ref[:, u * LANES : (u + 1) * LANES] * jnp.asarray(0.125, BF16)
        k = proj_ref[:, 256 + u * LANES : 256 + (u + 1) * LANES]
        v = proj_ref[:, 512 + u * LANES : 512 + (u + 1) * LANES]
        total = None
        for keep in (low, ~low):
            s = dot_nt(jnp.where(keep, q, zero), k)
            s = jnp.where(mask, s, NEG_FILL)
            powers = jnp.exp(s - jnp.max(s, axis=-1, keepdims=True))
            probs = powers * (1.0 / jnp.sum(powers, axis=-1, keepdims=True))
            o = dot(probs.astype(BF16), jnp.where(keep, v, zero))
            total = o if total is None else total + o
        proj_ref[:, 768 + u * LANES : 768 + (u + 1) * LANES] = total.astype(BF16)
    for c in range(4):
        p_ref[:, c * 256 : (c + 1) * 256] = dot(proj_ref[:, 768:], out_chunk(w_ref, c)).astype(BF16)


def attention_backward(flag_ref, d_ref, proj_ref, w_ref, dproj_ref, p_ref, *, lens):
    rows, width = d_ref.shape
    flag = flag_ref[0]
    mask = image_numbers(lax.broadcasted_iota(jnp.int32, (rows, 1), 0), flag, lens) == image_numbers(
        lax.broadcasted_iota(jnp.int32, (1, rows), 1), flag, lens
    )
    d_o = sum(dot_nt(d_ref[:, c * 256 : (c + 1) * 256], out_chunk(w_ref, c)) for c in range(4))
    d_o = d_o.astype(BF16)
    low = lane_low(rows)
    zero = jnp.zeros((), BF16)
    scale = jnp.asarray(0.125, BF16)
    for u in range(2):
        q = proj_ref[:, u * LANES : (u + 1) * LANES] * scale
        k = proj_ref[:, 256 + u * LANES : 256 + (u + 1) * LANES]
        v = proj_ref[:, 512 + u * LANES : 512 + (u + 1) * LANES]
        g = d_o[:, u * LANES : (u + 1) * LANES]
        dq = dk = dv = None
        for keep in (low, ~low):
            k_own = jnp.where(keep, k, zero)
            s = jnp.where(mask, dot_nt(k_own, q), NEG_FILL)
            powers = jnp.exp(s - jnp.max(s, axis=0, keepdims=True))
            probs = powers * (1.0 / jnp.sum(powers, axis=0, keepdims=True))
            d_probs = dot_nt(jnp.where(keep, v, zero), g)
            centre = jnp.sum(probs * d_probs, axis=0, keepdims=True)
            d_scores = (probs * (d_probs - centre)).astype(BF16)
            terms = (
                dot_t(d_scores, k_own),
                dot(d_scores, jnp.where(keep, q, zero)),
                dot(probs.astype(BF16), jnp.where(keep, g, zero)),
            )
            dq, dk, dv = terms if dq is None else (dq + terms[0], dk + terms[1], dv + terms[2])
        dproj_ref[:, u * LANES : (u + 1) * LANES] = (dq * 0.125).astype(BF16)
        dproj_ref[:, 256 + u * LANES : 256 + (u + 1) * LANES] = dk.astype(BF16)
        dproj_ref[:, 512 + u * LANES : 512 + (u + 1) * LANES] = dv.astype(BF16)
    total = None
    for c in range(3):
        w = w_ref[:, :, c * 256 : (c + 1) * 256].reshape(width, 256)
        term = dot_nt(dproj_ref[:, c * 256 : (c + 1) * 256], w)
        total = term if total is None else total + term
    p_ref[...] = total.astype(BF16)


def gelu_parts(pre):
    upto = 0.5 * (1.0 + lax.erf(pre * math.sqrt(0.5)))
    density = jnp.exp(-0.5 * pre * pre) * (1.0 / math.sqrt(2.0 * math.pi))
    return pre * upto, upto + pre * density


def mlp_up(x_ref, up_ref, both_ref):
    width = x_ref.shape[1]
    for c in range(4):
        cols = slice(c * 256, (c + 1) * 256)
        act, slope = gelu_parts(dot(x_ref[...], up_ref[:, :, cols].reshape(width, 256)))
        both_ref[0, :, cols] = act.astype(BF16)
        both_ref[1, :, cols] = slope.astype(BF16)


def mlp_down(*refs):
    count = len(refs) // 2
    down = refs[count][...].reshape(-1, refs[count].shape[2])
    for act_ref, out_ref in zip(refs[:count], refs[count + 1 :]):
        out_ref[...] = dot(act_ref[0], down).astype(BF16)


def mlp_backward(d_ref, slope_ref, up_ref, down_ref, dpre_ref, p_ref):
    width = d_ref.shape[1]
    for c in range(4):
        cols = slice(c * 256, (c + 1) * 256)
        d_act = dot_nt(d_ref[...], down_ref[2 * c : 2 * c + 2].reshape(256, width))
        dpre_ref[:, cols] = (d_act * slope_ref[0, :, cols].astype(F32)).astype(BF16)
    p_ref[...] = dot_nt(dpre_ref[...], up_ref[...].reshape(width, width)).astype(BF16)


def mlp_both(x_ref, d_ref, up_ref, down_ref, act_ref, dpre_ref, back_ref):
    width = x_ref.shape[1]
    for c in range(4):
        cols = slice(c * 256, (c + 1) * 256)
        act, slope = gelu_parts(dot(x_ref[...], up_ref[:, :, cols].reshape(width, 256)))
        act_ref[:, cols] = act.astype(BF16)
        d_act = dot_nt(d_ref[...], down_ref[2 * c : 2 * c + 2].reshape(256, width))
        dpre_ref[:, cols] = (d_act * slope).astype(BF16)
    back_ref[...] = dot_nt(dpre_ref[...], up_ref[...].reshape(width, width)).astype(BF16)


def summed(left, right, rows, cols=slice(None)):
    total = None
    for a, b in zip(left, right):
        term = dot_t(a[:, rows], b[:, cols])
        total = term if total is None else total + term
    return total


def stack_rows(blocks, out_ref):
    rows = blocks[0].shape[0]
    tall = -(-rows // 32) * 32
    for k, block in enumerate(blocks):
        out_ref[k * tall + rows // 16 * 16 : (k + 1) * tall, :] = jnp.zeros(
            (tall - rows // 16 * 16, out_ref.shape[1]), BF16
        )
        out_ref[k * tall : k * tall + rows, :] = block


def grads_mlp(*refs):
    x, dpre, act, d, out_ref, left, right = refs[:4], refs[4:8], refs[8:12], refs[12:16], *refs[16:]
    acts = [a[0] if len(a.shape) == 3 else a[...] for a in act]
    pairs = (([a[...] for a in x], dpre), (acts, d))
    for half, (first, second) in enumerate(pairs):
        stack_rows(first, left)
        stack_rows([b[...] for b in second], right)
        for t in range(4):
            total = dot_t(left[:, t * 256 : (t + 1) * 256], right[...]).astype(BF16)
            out_ref[2 * t : 2 * t + 2, half * LANES : (half + 1) * LANES, :] = total.reshape(2, LANES, -1)


def stack_attention(refs, left, right, narrow):
    x, dproj, kept, d = refs[:4], refs[4:8], refs[8:12], refs[12:16]
    stack_rows([a[...] for a in x], left)
    stack_rows([a[...] for a in dproj], right.at[:, :768])
    stack_rows([a[...] for a in kept], narrow)


def grads_attention(*refs):
    out_ref, left, right, narrow = refs[16:]
    stack_attention(refs, left, right, narrow)
    for t in range(4):
        total = dot_t(left[:, t * 256 : (t + 1) * 256], right[:, :768]).astype(BF16)
        out_ref[2 * t : 2 * t + 2, :LANES, :768] = total.reshape(2, LANES, -1)
    stack_rows([a[...] for a in refs[12:16]], right)
    for c in range(4):
        total = dot_t(narrow[...], right[:, c * 256 : (c + 1) * 256])
        out_ref[:, c * 32 : (c + 1) * 32, 768:1024] = total.astype(BF16).reshape(8, 32, 256)


def rows_of(j):
    return pl.ds(pl.multiple_of(j * LANES, LANES), LANES)


def grads_attention_sides(core_ref, *refs):
    theirs, mine, (left, right, narrow) = refs[16:20], refs[20], refs[21:]
    core = core_ref[0]
    stack_attention(refs, left, right, narrow)
    for z in range(4):
        theirs[z][:, :768] = dot_t(left[:, rows_of(z * 2 + 1 - core)], right[:, :768]).astype(BF16)
    for z in range(4):
        mine[z, :, :768] = dot_t(left[:, rows_of(z * 2 + core)], right[:, :768]).astype(BF16)
    stack_rows([a[...] for a in refs[12:16]], right)
    for c in range(4):
        total = dot_t(narrow[...], right[:, c * 256 : (c + 1) * 256]).astype(BF16).reshape(8, 32, 256)
        rows = slice(c * 32, (c + 1) * 32)
        for z in range(4):
            first, second = total[2 * z], total[2 * z + 1]
            theirs[z][rows, 768:1024] = jnp.where(core == 0, second, first)
            mine[z, rows, 768:1024] = jnp.where(core == 0, first, second)


def add_pair(mine_ref, *refs):
    for z in range(4):
        refs[4][z] = (mine_ref[z].astype(F32) + refs[z][...].astype(F32)).astype(BF16)


def last_norm(g_ref, p0, r1, r2, r3, h_ref, mixing_ref, term_ref, d_ref, out_ref, packed, sem):
    d = g_ref[...] + norm_backward(added(p0, r1, r2, r3), *normalize(h_ref[...]))
    d_ref[...] = d
    high = d.astype(BF16)
    low = (d - high.astype(F32)).astype(BF16)
    table = dot_t(mixing_ref[...], high) + dot_t(mixing_ref[...], low)
    packed[...] = jnp.zeros(packed.shape, BF16)
    for j in range(8):
        for c in range(-(-table.shape[0] // 32)):
            size = min(32, table.shape[0] - 32 * c)
            part = table[32 * c : 32 * c + size, j * LANES : (j + 1) * LANES]
            packed[j, :size, c * LANES : (c + 1) * LANES] = part.astype(BF16)
    copy = pltpu.make_async_copy(packed, out_ref.at[:, LANES : LANES + 32, :], sem.at[0])
    copy.start()
    copy.wait()


def unpack_table(refs, out_ref):
    g = [ref[LANES : LANES + 32, :].astype(F32) for ref in refs]
    total = (g[0] + g[1]) + (g[2] + g[3])
    for c in range(-(-out_ref.shape[0] // 32)):
        size = min(32, out_ref.shape[0] - 32 * c)
        out_ref[32 * c : 32 * c + size, :] = total[:size, c * LANES : (c + 1) * LANES]


def finish_mlp(me_ref, *refs, merged):
    g, up_ref, gain_ref, dup_ref, ddown_ref, dgain_ref = refs[:5], refs[5], refs[6], *refs[-3:]
    me = me_ref[0]
    low = 192 if merged else LANES
    column = jnp.sum(diagonal(gain_ref[0]), axis=1, keepdims=True)
    total = jnp.zeros((LANES, LANES), F32)
    downs = [piece[low : low + LANES, :] for piece in g[:3]] + [g[4][:LANES, :]]
    for k, piece in enumerate(downs):
        rows = pl.ds(pl.multiple_of((me ^ k) * LANES, LANES), LANES)
        ddown_ref[0, rows, :] = piece.astype(F32)
    ups = [piece[:LANES, :] for piece in g[:4]]
    for i in range(4):
        got = jnp.where(
            me == i, ups[0], jnp.where(me == i ^ 1, ups[1], jnp.where(me == i ^ 2, ups[2], ups[3]))
        ).astype(F32)
        for j in range(8):
            cols = slice((j * 4 + i) * LANES, (j * 4 + i + 1) * LANES)
            part = got[:, j * LANES : (j + 1) * LANES]
            dup_ref[0, :, cols] = part * column
            total = total + part * up_ref[0, :, cols].astype(F32)
    dgain_ref[0] = jnp.sum(total.T, axis=0, keepdims=True)


def attention_rows(refs):
    if len(refs) == 4:
        return [ref[:LANES, :] for ref in refs]
    rows = [jnp.concatenate([ref[128:192, :], ref[320:384, :]], axis=0) for ref in refs[:3]]
    return rows + [jnp.concatenate([ref[128:192, :] for ref in refs[3:]], axis=0)]


def by_owner(me, pieces, i):
    g0, g1, g2, g3 = pieces
    return jnp.where(me == i, g0, jnp.where(me == i ^ 1, g1, jnp.where(me == i ^ 2, g2, g3)))


def split_out(who_ref, *refs):
    keep_ref, give_ref = refs[-2:]
    packed = [piece[:, 768:] for piece in attention_rows(refs[:-2])]
    me, core = who_ref[0], who_ref[1]
    for second in range(2):
        even, odd = by_owner(me, packed, 2 * second), by_owner(me, packed, 2 * second + 1)
        keep_ref[second] = jnp.where(core == 0, even, odd)
        give_ref[second] = jnp.where(core == 0, odd, even)


def finish_attention(who_ref, *refs, count):
    g, (w_ref, gain_ref, keep_ref, got_ref) = refs[:count], refs[count : count + 4]
    if count == 4:
        unpack_table(g, refs[-1])
        refs = refs[:-1]
    dqkv_ref, dout_ref, dgain_ref = refs[-3:]
    me, core = who_ref[0], who_ref[1]
    column = jnp.sum(diagonal(gain_ref[0]), axis=1, keepdims=True)
    total = jnp.zeros((LANES, LANES), F32)
    low = lane_low(LANES)
    rows = [piece[:, :768] for piece in attention_rows(g)]
    owned = [by_owner(me, rows, i).astype(F32) for i in range(4)]
    for t in range(12):
        u = t // 2
        for side in range(2):
            first = owned[side][:, u * LANES : (u + 1) * LANES]
            second = owned[side + 2][:, u * LANES : (u + 1) * LANES]
            if t % 2 == 0:
                part = jnp.where(low, first, lane_swap(second))
            else:
                part = jnp.where(low, lane_swap(first), second)
            chunk = (t // 4) * 8 + 2 * (t % 4) + side
            cols = slice(chunk * LANES, (chunk + 1) * LANES)
            dqkv_ref[0, :, cols] = part * column
            total = total + part * w_ref[0, :, cols].astype(F32)
    dgain_ref[0] = jnp.sum(total.T, axis=0, keepdims=True)
    for second in range(2):
        keep, got = keep_ref[second], got_ref[second]
        halves = (jnp.where(core == 0, keep, got), jnp.where(core == 0, got, keep))
        for h, part in enumerate(halves):
            for c in range(4):
                top = (2 * second + h) * 32
                dout_ref[0, top : top + 32, c * 256 : (c + 1) * 256] = part[c * 32 : (c + 1) * 32, :].astype(F32)


def local_fast(
    tokens,
    pos_table,
    index_lo,
    index_hi,
    resolution,
    gain_attn,
    w_qkv,
    w_out,
    gain_mlp,
    w_up,
    w_down,
    cotangent,
):
    rows, width = tokens.shape
    layers = w_qkv.shape[0]
    square = Square()
    me = square.me
    me1 = me.reshape(1).astype(jnp.int32)
    shard = lax.axis_index("fsdp")
    core, deep = shard % 2, shard // 2
    deep1 = deep.reshape(1).astype(jnp.int32)
    len_low, len_high = index_lo.shape[0], index_hi.shape[0]
    lens = ((len_low, rows // len_low), (len_high, rows // len_high))
    block = (rows, width)
    blocks = range(4)

    def over_fsdp(x, k):
        return lax.ppermute(x, "fsdp", [(j, j ^ k) for j in range(8)])

    def layer_of(array, depth):
        return pl.BlockSpec((1,) + array.shape[1:], lambda *_: (depth,) + (0,) * (array.ndim - 1))

    who = jnp.stack([me, core]).astype(jnp.int32)
    head_side = me >> 1

    def out_rows(half):
        return lax.dynamic_slice(w_out, (0, (head_side * 2 + half) * 32, 0), (layers, 32, width))

    keep, got = out_rows(core), over_fsdp(out_rows(1 - core), 1)
    gains_a = gain_attn.reshape(layers, 1, LANES)
    gains_m = gain_mlp.reshape(layers, 1, LANES)

    def part(top):
        return pl.BlockSpec((8, LANES, width), lambda *_: (0, top, 0))

    def fetch(body, args, specs, after=()):
        (packed,) = call(
            body, [((2 * LANES, width), BF16)], [who] + args, [scalars()] + specs, after=after, limit=60
        )
        return lax.all_gather(packed, "fsdp", axis=0, tiled=False)

    first_w = fetch(
        prepare_first,
        [w_qkv, gain_attn, keep, got, w_up, gain_mlp],
        [layer_of(w_qkv, 0), None, None, None, layer_of(w_up, 0), None],
    )

    flag = resolution[me]
    flag1 = flag.reshape(1)
    flags = [resolution[owner].reshape(1) for owner in square.owners()]
    shard_count, group_count = 8, resolution.shape[0]
    high_groups = jnp.sum(resolution)
    tokens_low = ((group_count - high_groups) * shard_count * lens[0][1] * len_low).astype(F32)
    tokens_high = (high_groups * shard_count * lens[1][1] * len_high).astype(F32)
    token_share = 2.0 * jnp.where(flag == 1, tokens_high, tokens_low) / (tokens_low + tokens_high)
    live = jnp.where(flag == 1, lens[1][1] * len_high, lens[0][1] * len_low)
    weight = jnp.where(jnp.arange(rows, dtype=jnp.int32) < live, token_share, 0.0)
    gradient = cotangent.astype(F32) * weight[:, None]

    normed = [(block, F32), (block, BF16)]
    size = -(-len_high // 32) * 8
    mine = lax.dynamic_slice(
        jnp.pad(pos_table, ((0, 4 * size - len_high), (0, 0))), (me * size, 0), (size, LANES)
    )
    other = over_fsdp(mine, 1)
    pair = jnp.concatenate([jnp.where(core == 0, mine, other), jnp.where(core == 0, other, mine)], axis=1)
    pieces = [pair] + [over_fsdp(pair, 2 * k) for k in range(1, 4)]
    (mine,) = call(
        join_table,
        [((size, width), BF16)],
        [deep1] + pieces,
        [scalars()] + [None] * 4,
        scratch=[VMEM((size, width), F32)],
    )
    (mixing,) = call(
        functools.partial(make_mixing, lens=lens),
        [((rows, len_high), BF16)],
        [flag1, index_lo, index_hi],
        [scalars(), None, None],
    )
    hidden, xhat = call(
        embed,
        normed,
        [who, tokens, mixing] + square.spread(mine),
        [scalars()] + [None] * 6,
        scratch=[VMEM((4 * size, width), F32)],
    )
    second_w = fetch(
        prepare_second,
        [w_qkv, gain_attn, keep, got, w_down],
        [layer_of(w_qkv, 1), None, None, None, layer_of(w_down, 0)],
        [xhat],
    )
    third_w = fetch(
        prepare_third,
        [w_up, gain_mlp, w_down],
        [layer_of(w_up, 1), None, layer_of(w_down, 1)],
        [xhat],
    )
    attn_w = [(first_w, part(0)), (second_w, part(1))]

    def tie(*values):
        return lax.optimization_barrier(values)

    def tie_last(es, term):
        near, term = tie(es[:3], term)
        far, near, term = tie(es[3], near, term)
        return near + [far], term

    def chain(kernel):
        done = []
        for k in blocks:
            done.append(kernel(k, [d[0] for d in done[-1:]]))
        return done

    def collect(parts):
        return [parts[0]] + [square.swap(parts[k], k) for k in range(1, 4)]

    d_top = square.spread(gradient.astype(BF16))
    saved = []
    for depth in range(layers):
        a_w, a_part = attn_w[depth]
        xs = square.spread(xhat)
        got = chain(
            lambda k, after: call(
                functools.partial(attention_forward, lens=lens),
                [(block, BF16)] * 2,
                [flags[k], xs[k], a_w],
                [scalars(), None, a_part],
                after=after,
            )
        )
        kept = [g[0] for g in got]
        es = collect([g[1] for g in got])
        if depth == 0:
            es, d_top = tie(es, d_top)
        before, (middle, xhat) = hidden, call(add_norm, normed, [hidden] + es)
        if depth > 0:
            xhat, third_w = tie(xhat, third_w)
        ms = square.spread(xhat)
        if depth < layers - 1:
            acts = chain(
                lambda k, after: call(
                    mlp_up, [((2,) + block, BF16)], [ms[k], first_w], [None, part(1)], after=after
                )
            )
            acts = [a[0] for a in acts]
            first_half = pl.BlockSpec((1,) + block, lambda *_: (0, 0, 0))
            parts = call(
                mlp_down, [(block, BF16)] * 3, acts[1:] + [second_w], [first_half] * 3 + [part(0)], after=acts[:1]
            )
            (own,) = call(
                mlp_down, [(block, BF16)], [acts[0], second_w], [first_half, part(0)], after=parts[:1]
            )
            parts = [own] + list(parts)
            saved.append((before, xs, kept, middle, ms, acts))
            hidden, xhat = call(add_norm, normed, [middle] + collect(parts))
        else:
            got = chain(
                lambda k, after: call(
                    mlp_both,
                    [(block, BF16)] * 3,
                    [ms[k], d_top[k], third_w, third_w],
                    [None, None, part(0), part(1)],
                    after=after,
                )
            )
            acts, dpres, backs = ([g[t] for g in got] for t in range(3))
            top_acts = acts
            saved.append((before, xs, kept, middle, ms, acts))

    def far_halves(x, y):
        half = x.shape[0] // 2
        return [square.swap(x[:half], 2), square.swap(y[half:], 1)]

    core1 = core.reshape(1).astype(jnp.int32)
    tall = 4 * (-(-rows // 32) * 32)

    def home(term):
        return lax.psum_scatter(term, "fsdp", scatter_dimension=0, tiled=False)

    homes_m, homes_a = [None] * layers, [None] * layers
    for depth in reversed(range(layers)):
        top = depth == layers - 1
        a_w, a_part = attn_w[depth]
        before, xs, kept, middle, ms, acts = saved[depth]
        ds = d_top if top else square.spread(low)
        if not top:
            second_half = pl.BlockSpec((1,) + block, lambda *_: (1, 0, 0))
            got = chain(
                lambda k, after: call(
                    mlp_backward,
                    [(block, BF16)] * 2,
                    [ds[k], acts[k], first_w, second_w],
                    [None, second_half, part(1), part(0)],
                    after=after or [homes_m[1]],
                )
            )
            dpres, backs = ([g[t] for g in got] for t in range(2))
        es = collect(backs)
        first_half = pl.BlockSpec((1,) + block, lambda *_: (0, 0, 0))
        (term,) = call(
            grads_mlp,
            [((8, 2 * LANES, width), BF16)],
            list(ms) + list(dpres) + list(acts) + list(ds),
            [None] * 8 + [None if top else first_half] * 4 + [None] * 4,
            scratch=[VMEM((tall, width), BF16)] * 2,
        )
        if top:
            near, term = tie(es[:3], term)
            homes_m[depth] = home(term)
            far, near, _ = tie(es[3], near, term)
            es = near + [far]
        else:
            es, term = tie_last(es, term)
            homes_m[depth] = home(term)
        d_middle, low = call(add_norm_backward, normed, [gradient] + es + [middle], limit=60)
        if not top:
            m, a = homes_m[1], homes_a[1]
            merged = jnp.concatenate([m[:LANES], a[:64], m[LANES:], a[64:]], axis=0)
        ds = square.spread(low)
        got = chain(
            lambda k, after: call(
                functools.partial(attention_backward, lens=lens),
                [((rows, 768), BF16), (block, BF16)],
                [flags[k], ds[k], kept[k], a_w],
                [scalars(), None, None, a_part],
                after=after or ([] if top else [merged]),
            )
        )
        dprojs = [g[0] for g in got]
        es = collect([g[1] for g in got])
        out_part = pl.BlockSpec((rows, 256), lambda *_: (0, 3))
        stacks = [VMEM((tall, width), BF16)] * 2 + [VMEM((tall, 256), BF16)]
        operands = list(xs) + dprojs + list(kept) + list(ds)
        specs = [None] * 8 + [out_part] * 4 + [None] * 4
        if top:
            *theirs, mine = call(
                grads_attention_sides,
                [((LANES, width), BF16)] * 4 + [((4, LANES, width), BF16)],
                [core1] + operands,
                [scalars()] + specs,
                scratch=stacks,
            )
            got = [over_fsdp(part, 1) for part in theirs]
            es, mine = tie_last(es, mine)
            (term,) = call(add_pair, [(mine.shape, BF16)], [mine] + got, after=[es[3]])
            es, term = tie(es, term)
            homes_a[depth] = lax.psum_scatter(
                term, "fsdp", scatter_dimension=0, tiled=False, axis_index_groups=[[0, 2, 4, 6], [1, 3, 5, 7]]
            )
            last_middle = middle
            gradient, low = call(add_norm_backward, normed, [d_middle] + es + [before], limit=60)
        else:
            near = [square.swap(merged, 1), square.swap(merged, 2)]
            (term,) = call(grads_attention, [((8, LANES + 32, width), BF16)], operands, specs, after=near, scratch=stacks)
            es, term = tie_last(es, term)
            anywhere = pl.BlockSpec(memory_space=pl.ANY)
            gradient, term = call(
                last_norm,
                [(block, F32), (term.shape, BF16)],
                [d_middle] + es + [before, mixing, term],
                [None] * 7 + [anywhere],
                out_specs=[whole(block), anywhere],
                aliases={7: 1},
                scratch=[VMEM((8, 32, width), BF16), pltpu.SemaphoreType.DMA((1,))],
            )
            homes_a[0] = home(term)

    merged = [merged, *near] + far_halves(*near)

    outs = call(
        output_parts, [(block, BF16)] * 4, top_acts + [third_w], [None] * 4 + [part(1)], after=[gradient]
    )
    (output,) = call(add_output, [(block, F32)], [last_middle] + collect(outs))
    homes_m[0], gradient = tie(homes_m[0], gradient)
    x, y = square.swap(homes_m[0], 1), square.swap(homes_m[0], 2)
    homes_m[0] = [homes_m[0], x, y] + far_halves(x, y)
    big = [None] * 6

    def finish(body, depth, args, shapes, prior):
        extra = [] if prior[0] is None else prior
        specs = [layer_of(a, depth) if a is w_up or a is w_qkv or a is gains_a or a is gains_m else None for a in args]
        return call(
            body,
            [(shape, F32) for shape in shapes],
            [who] + args + extra,
            [scalars()] + specs + [pl.BlockSpec(memory_space=pl.ANY)] * len(extra),
            aliases={1 + len(args) + t: t for t in range(len(extra))},
            out_specs=[
                layer_of(jax.ShapeDtypeStruct(shape, F32), depth) if len(shape) == 3 else whole(shape)
                for shape in shapes
            ],
        )

    def finish_m(depth, pieces):
        shapes = [w_up.shape, w_down.shape, gains_m.shape]
        body = functools.partial(finish_mlp, merged=depth > 0)
        big[3:] = finish(body, depth, pieces + [w_up, gains_m], shapes, big[3:])

    def finish_a(depth, pieces):
        keep, give = call(
            split_out, [((2, LANES, 256), BF16)] * 2, [who] + pieces, [scalars()] + [None] * len(pieces)
        )
        shapes = [w_qkv.shape, w_out.shape, gains_a.shape]
        body = functools.partial(finish_attention, count=len(pieces))
        args = pieces + [w_qkv, gains_a, keep, over_fsdp(give, 1)]
        if len(pieces) == 4:
            shapes = shapes + [(len_high, LANES)]
        big[:3] = finish(body, depth, args, shapes, big[:3])

    finish_m(1, merged)
    finish_a(1, merged)
    homes_a[0], homes_m[0], big, output = tie(homes_a[0], homes_m[0], big, output)
    pieces = square.spread(homes_a[0])
    finish_m(0, homes_m[0])
    pieces, big = tie(pieces, big)
    finish_a(0, pieces)
    d_table = big.pop(3)
    return (
        output,
        gradient,
        d_table,
        big[2].reshape(layers, LANES),
        big[0],
        big[1],
        big[5].reshape(layers, LANES),
        big[3],
        big[4],
    )


def solution(mesh):
    in_specs = (
        P(("dp", "fsdp"), None),
        P(None, "fsdp"),
        P(),
        P(),
        P(),
        P(None, "fsdp"),
        P(None, "fsdp", None),
        P(None, "fsdp", None),
        P(None, "fsdp"),
        P(None, "fsdp", None),
        P(None, "fsdp", None),
        P(("dp", "fsdp"), None),
    )
    out_specs = (
        P(("dp", "fsdp"), None),
        P(("dp", "fsdp"), None),
        P(None, "fsdp"),
        P(None, "fsdp"),
        P(None, "fsdp", None),
        P(None, "fsdp", None),
        P(None, "fsdp"),
        P(None, "fsdp", None),
        P(None, "fsdp", None),
    )
    fast = mesh.shape["dp"] == 4 and mesh.shape["fsdp"] == 8
    local = local_fast if fast else local_general
    return jax.shard_map(local, mesh=mesh, in_specs=in_specs, out_specs=out_specs, check_vma=False)
```

```python
import functools
import math

import jax
import jax.numpy as jnp
from jax import lax
from jax.experimental import pallas as pl
from jax.experimental.pallas import tpu as pltpu
from jax.sharding import PartitionSpec as P

HEADS = 16
EPS = 1e-06
NEG_FILL = -1e30
MIX_WEIGHTS = (0.5, 0.25, 0.125, 0.125)
BF16 = jnp.bfloat16
F32 = jnp.float32


def dot(a, b):
    return jnp.dot(a, b, preferred_element_type=F32)


def dot_t(a, b):
    return lax.dot_general(a, b, (((0,), (0,)), ((), ())), preferred_element_type=F32)


def dot_nt(a, b):
    return lax.dot_general(a, b, (((1,), (1,)), ((), ())), preferred_element_type=F32)


def normalize(hidden):
    center = hidden - jnp.mean(hidden, axis=-1, keepdims=True)
    rstd = lax.rsqrt(jnp.mean(center * center, axis=-1, keepdims=True) + EPS)
    return center * rstd, rstd


def norm_backward(e, xhat, rstd):
    return rstd * (
        e
        - jnp.mean(e, axis=-1, keepdims=True)
        - xhat * jnp.mean(e * xhat, axis=-1, keepdims=True)
    )


def gelu_exact(pre_act):
    return jax.nn.gelu(pre_act, approximate=False)


class Square:
    def __init__(self):
        self.count = lax.axis_size("dp")
        self.me = lax.axis_index("dp")
        self.pairs = self.count == 4

    def owners(self):
        if self.pairs:
            return [self.me ^ k for k in range(self.count)]
        return [jnp.int32(k) for k in range(self.count)]

    def swap(self, block, k):
        return lax.ppermute(block, "dp", [(i, i ^ k) for i in range(self.count)])

    def spread(self, block):
        if self.pairs:
            return [block] + [self.swap(block, k) for k in range(1, self.count)]
        full = lax.all_gather(block, "dp")
        return [full[k] for k in range(self.count)]

    def collect(self, parts):
        if self.pairs:
            total = parts[0].astype(F32)
            for k in range(1, self.count):
                total = total + self.swap(parts[k].astype(BF16), k).astype(F32)
            return total
        stacked = jnp.stack([part.astype(BF16) for part in parts])
        return lax.psum_scatter(stacked, "dp", scatter_dimension=0, tiled=False).astype(F32)

    def gather(self, piece):
        if not self.pairs:
            return lax.all_gather(piece, "dp")
        got = [piece] + [self.swap(piece, k) for k in range(1, self.count)]
        odd = (self.me & 1) == 1
        high = (self.me & 2) == 2
        low_pair = (jnp.where(odd, got[1], got[0]), jnp.where(odd, got[0], got[1]))
        far_pair = (jnp.where(odd, got[3], got[2]), jnp.where(odd, got[2], got[3]))
        return jnp.stack(
            [
                jnp.where(high, far_pair[0], low_pair[0]),
                jnp.where(high, far_pair[1], low_pair[1]),
                jnp.where(high, low_pair[0], far_pair[0]),
                jnp.where(high, low_pair[1], far_pair[1]),
            ]
        )

    def total(self, piece):
        if not self.pairs:
            return lax.psum(piece.astype(BF16), "dp").astype(F32)
        own = piece.astype(BF16)
        got = [own.astype(F32)] + [self.swap(own, k).astype(F32) for k in range(1, self.count)]
        return (got[0] + got[1]) + (got[2] + got[3])


def select(index, choices):
    out = choices[0]
    for k in range(1, len(choices)):
        out = jnp.where(index == k, choices[k], out)
    return out


def local_general(
    tokens,
    pos_table,
    index_lo,
    index_hi,
    resolution,
    gain_attn,
    w_qkv,
    w_out,
    gain_mlp,
    w_up,
    w_down,
    cotangent,
):
    row_count, width = tokens.shape
    layers, shard_rows, _ = w_qkv.shape
    hidden_units = w_up.shape[2]
    shard_count = lax.axis_size("fsdp")
    shard = lax.axis_index("fsdp")
    square = Square()
    group_count = square.count
    me = square.me
    head_size = width // HEADS
    my_heads = HEADS // group_count
    part = my_heads * head_size
    unit_part = hidden_units // group_count
    fine = square.pairs and shard_count * 2 == HEADS
    score_scale = 1.0 / math.sqrt(head_size)
    len_low = index_lo.shape[0]
    len_high = index_hi.shape[0]

    row_ids = jnp.arange(row_count, dtype=jnp.int32)

    def layout(flag):
        length = jnp.where(flag == 1, len_high, len_low).astype(jnp.int32)
        images = jnp.where(flag == 1, row_count // len_high, row_count // len_low).astype(jnp.int32)
        live = row_ids < images * length
        return live, jnp.where(live, row_ids // length, images)

    flag = resolution[me]
    live_rows, _ = layout(flag)
    block_ids = jnp.stack([layout(resolution[owner])[1] for owner in square.owners()])
    same_image = block_ids[:, :, None] == block_ids[:, None, :]
    picked = jnp.where(flag == 1, index_hi[row_ids % len_high], index_lo[row_ids % len_low])
    table_ids = jnp.arange(len_high, dtype=jnp.int32)
    mixing = jnp.zeros((row_count, len_high), F32)
    for slot in range(4):
        mixing = mixing + MIX_WEIGHTS[slot] * (
            picked[:, slot : slot + 1] == table_ids[None, :]
        ).astype(F32)
    mixing = (mixing * live_rows[:, None].astype(F32)).astype(BF16)
    high_groups = jnp.sum(resolution)
    tokens_low = (
        (group_count - high_groups) * shard_count * (row_count // len_low) * len_low
    ).astype(F32)
    tokens_high = (high_groups * shard_count * (row_count // len_high) * len_high).astype(F32)
    token_share = 2.0 * jnp.where(flag == 1, tokens_high, tokens_low) / (tokens_low + tokens_high)
    weight = jnp.where(live_rows, token_share, 0.0)

    half = shard_rows // 4
    core = shard % 2
    swap_core = [(j, j ^ 1) for j in range(shard_count)]
    pair_side, head_side = me & 1, (me >> 1) & 1

    def qkv_part(w):
        if fine:
            view = w.reshape(shard_rows, 3 * HEADS // 4, 2, 2, head_size)
            view = select(pair_side, [view[:, :, 0], view[:, :, 1]])
            view = select(head_side, [view[:, :, 0], view[:, :, 1]])
            return view.reshape(shard_rows, 3 * part)
        view = w.reshape(shard_rows, 3, group_count, part)
        return lax.dynamic_index_in_dim(view, me, 2, keepdims=False).reshape(shard_rows, 3 * part)

    def up_part(w):
        view = w.reshape(shard_rows, shard_count, group_count, unit_part // shard_count)
        return lax.dynamic_index_in_dim(view, me, 2, keepdims=False).reshape(shard_rows, unit_part)

    def down_part(w):
        rows = unit_part // shard_count
        return lax.dynamic_slice_in_dim(w, me * rows, rows, 0)

    def out_part(w):
        if fine:
            view = w.reshape(2, 2, half, width)
            mine = select(head_side, [view[0], view[1]])
            keep = select(core, [mine[0], mine[1]])
            give = select(core, [mine[1], mine[0]])
            got = lax.ppermute(give, "fsdp", swap_core)
            return jnp.where(core == pair_side, keep, got)
        return w

    def fetch(piece):
        return lax.all_gather(piece, "fsdp", axis=0, tiled=False)

    weights = []
    table = lax.all_gather(pos_table, "fsdp", axis=1, tiled=True)
    for depth in range(layers):
        gain_a = gain_attn[depth].astype(F32)[:, None]
        gain_m = gain_mlp[depth].astype(F32)[:, None]
        qkv = (qkv_part(w_qkv[depth]).astype(F32) * gain_a).astype(BF16)
        up = (up_part(w_up[depth]).astype(F32) * gain_m).astype(BF16)
        down = down_part(w_down[depth])
        out = out_part(w_out[depth])
        qkv_all = fetch(qkv).reshape(width, 3 * part)
        a = up.size // width
        b = a + down.shape[0]
        rest = fetch(jnp.concatenate([up.reshape(a, width), down, out], axis=0))
        up_all = rest[:, :a].reshape(width, unit_part)
        down_all = rest[:, a:b].reshape(unit_part, width)
        out_all = rest[:, b:].reshape(-1, width)
        if not fine:
            out_all = lax.dynamic_slice_in_dim(out_all, me * part, part, 0)
        weights.append((qkv_all, out_all, up_all, down_all))

    def split_heads(block):
        return block.reshape(group_count, row_count, my_heads, head_size)

    def scores_of(queries, key_rows):
        scores = (
            jnp.einsum("bqhd,bkhd->bhqk", queries, key_rows, preferred_element_type=F32)
            * score_scale
        )
        return jnp.where(same_image[:, None], scores, NEG_FILL)

    def spread(block):
        return jnp.concatenate(square.spread(block), axis=0)

    def collect(partial):
        return square.collect([partial[k * row_count : (k + 1) * row_count] for k in range(group_count)])

    hidden = tokens.astype(F32) + dot(mixing, table)
    saved = []
    for depth in range(layers):
        qkv_w, out_w, up_w, down_w = weights[depth]
        xhat_a, rstd_a = normalize(hidden)
        rows_a = spread(xhat_a.astype(BF16))
        projected = dot(rows_a, qkv_w).astype(BF16)
        queries = split_heads(projected[:, :part])
        key_rows = split_heads(projected[:, part : 2 * part])
        values = split_heads(projected[:, 2 * part :])
        scores = scores_of(queries, key_rows)
        row_max = jnp.max(scores, axis=-1, keepdims=True)
        powers = jnp.exp(scores - row_max)
        row_total = jnp.sum(powers, axis=-1, keepdims=True)
        log_total = row_max + jnp.log(row_total)
        probs = (powers / row_total).astype(BF16)
        attended = jnp.einsum("bhqk,bkhd->bqhd", probs, values, preferred_element_type=F32)
        attended = attended.reshape(group_count * row_count, part).astype(BF16)
        middle = hidden + collect(dot(attended, out_w).astype(BF16))
        xhat_m, rstd_m = normalize(middle)
        rows_m = spread(xhat_m.astype(BF16))
        pre_act = dot(rows_m, up_w)
        activated = gelu_exact(pre_act).astype(BF16)
        result = middle + collect(dot(activated, down_w).astype(BF16))
        saved.append(
            (xhat_a, rstd_a, rows_a, queries, key_rows, values, log_total, attended,
             xhat_m, rstd_m, rows_m, pre_act, activated)
        )
        hidden = result

    gradient = cotangent.astype(F32) * weight[:, None]
    shares = [None] * layers
    for depth in reversed(range(layers)):
        qkv_w, out_w, up_w, down_w = weights[depth]
        (xhat_a, rstd_a, rows_a, queries, key_rows, values, log_total, attended,
         xhat_m, rstd_m, rows_m, pre_act, activated) = saved[depth]
        d_result = spread(gradient.astype(BF16))
        grad_down = dot_t(activated, d_result).astype(BF16)
        d_activated = dot_nt(d_result, down_w)
        _, pullback = jax.vjp(gelu_exact, pre_act)
        d_pre = pullback(d_activated)[0].astype(BF16)
        grad_up = dot_t(rows_m, d_pre).astype(BF16)
        e = collect(dot_nt(d_pre, up_w).astype(BF16))
        d_middle = gradient + norm_backward(e, xhat_m, rstd_m)
        d_attn = spread(d_middle.astype(BF16))
        grad_out = dot_t(attended, d_attn).astype(BF16)
        d_attended = split_heads(dot_nt(d_attn, out_w).astype(BF16))
        probs = jnp.exp(scores_of(queries, key_rows) - log_total)
        d_values = jnp.einsum(
            "bhqk,bqhd->bkhd", probs.astype(BF16), d_attended, preferred_element_type=F32
        )
        d_probs = jnp.einsum("bqhd,bkhd->bhqk", d_attended, values, preferred_element_type=F32)
        centre = jnp.sum(probs * d_probs, axis=-1, keepdims=True)
        d_scores = (probs * (d_probs - centre)).astype(BF16)
        d_queries = (
            jnp.einsum("bhqk,bkhd->bqhd", d_scores, key_rows, preferred_element_type=F32)
            * score_scale
        )
        d_keys = (
            jnp.einsum("bhqk,bqhd->bkhd", d_scores, queries, preferred_element_type=F32)
            * score_scale
        )
        d_projected = jnp.concatenate(
            [x.astype(BF16).reshape(group_count * row_count, part) for x in (d_queries, d_keys, d_values)],
            axis=1,
        )
        grad_qkv = dot_t(rows_a, d_projected).astype(BF16)
        e = collect(dot_nt(d_projected, qkv_w).astype(BF16))
        gradient = d_middle + norm_backward(e, xhat_a, rstd_a)
        shares[depth] = (grad_qkv, grad_out, grad_up, grad_down)

    def home(term):
        return lax.psum_scatter(term, "fsdp", scatter_dimension=0, tiled=True)

    grads_qkv, grads_out, grads_up, grads_down, gains_a, gains_m = [], [], [], [], [], []
    for depth in reversed(range(layers)):
        grad_qkv, grad_out, grad_up, grad_down = shares[depth]
        rest = [
            grad_up.reshape(shard_count, -1, width),
            grad_down.reshape(shard_count, -1, width),
        ]
        if fine:
            rest.append(grad_out.reshape(shard_count, -1, width))
        else:
            full = jnp.zeros((width, width), BF16)
            full = lax.dynamic_update_slice_in_dim(full, grad_out, me * part, 0)
            rest.append(full.reshape(shard_count, -1, width))
        sizes = [x.shape[1] for x in rest]
        rest = home(jnp.concatenate(rest, axis=1))[0]
        qkv = square.gather(home(grad_qkv))
        if not fine:
            out = square.total(rest[sizes[0] + sizes[1] :])
            rest = rest[: sizes[0] + sizes[1]]
        rest = square.gather(rest)
        up = rest[:, : sizes[0]].reshape(group_count, shard_rows, shard_count, -1)
        up = up.transpose(1, 2, 0, 3).reshape(shard_rows, hidden_units).astype(F32)
        down = rest[:, sizes[0] : sizes[0] + sizes[1]].reshape(-1, width).astype(F32)
        if fine:
            pieces = rest[:, sizes[0] + sizes[1] :].reshape(2, 2, half, width)
            keep = select(core, [pieces[:, 0], pieces[:, 1]])
            give = select(core, [pieces[:, 1], pieces[:, 0]])
            got = lax.ppermute(give, "fsdp", swap_core)
            first = select(core, [keep, got])
            second = select(core, [got, keep])
            out = jnp.stack([first, second], axis=1).reshape(shard_rows, width).astype(F32)
            qkv = qkv.reshape(2, 2, shard_rows, 3 * my_heads, head_size).transpose(2, 3, 1, 0, 4)
        else:
            qkv = qkv.reshape(group_count, shard_rows, 3, part).transpose(1, 2, 0, 3)
        qkv = qkv.reshape(shard_rows, 3 * width).astype(F32)
        gains_a.append(jnp.sum(qkv * w_qkv[depth].astype(F32), axis=1))
        gains_m.append(jnp.sum(up * w_up[depth].astype(F32), axis=1))
        grads_qkv.append(qkv * gain_attn[depth].astype(F32)[:, None])
        grads_up.append(up * gain_mlp[depth].astype(F32)[:, None])
        grads_out.append(out)
        grads_down.append(down)

    high_part = gradient.astype(BF16)
    low_part = (gradient - high_part.astype(F32)).astype(BF16)
    table_term = dot_t(mixing, high_part) + dot_t(mixing, low_part)
    table_share = lax.psum_scatter(table_term.astype(BF16), "fsdp", scatter_dimension=1, tiled=True)
    d_table = square.total(table_share)
    return (
        hidden,
        gradient,
        d_table,
        jnp.stack(gains_a[::-1]),
        jnp.stack(grads_qkv[::-1]),
        jnp.stack(grads_out[::-1]),
        jnp.stack(gains_m[::-1]),
        jnp.stack(grads_up[::-1]),
        jnp.stack(grads_down[::-1]),
    )


VMEM = pltpu.VMEM
LANES = 128


def whole(shape):
    return pl.BlockSpec(tuple(shape), lambda *_: (0,) * len(shape))


def scalars():
    return pl.BlockSpec(memory_space=pltpu.SMEM)


def call(body, outs, args, specs=None, scratch=(), flops=0, reads=0, aliases=None, out_specs=None, limit=40, after=()):
    specs = [whole(a.shape) if s is None else s for a, s in zip(args, specs or [None] * len(args))]
    specs = specs + [pl.BlockSpec(memory_space=pl.ANY)] * len(after)
    count, extra = len(args), len(after)
    out_shape = [jax.ShapeDtypeStruct(shape, dtype) for shape, dtype in outs]
    moved = sum(math.prod(s) * jnp.dtype(d).itemsize for s, d in outs) + reads

    def run(*refs):
        body(*refs[:count], *refs[count + extra :])

    name = body.func.__name__ if isinstance(body, functools.partial) else body.__name__
    return pl.pallas_call(
        run,
        name=name,
        grid=(1,),
        in_specs=specs,
        out_specs=out_specs or [whole(shape) for shape, _ in outs],
        out_shape=out_shape,
        scratch_shapes=list(scratch),
        input_output_aliases=aliases or {},
        cost_estimate=pl.CostEstimate(flops=int(flops), bytes_accessed=int(moved), transcendentals=0),
        compiler_params=pltpu.CompilerParams(vmem_limit_bytes=limit << 20),
    )(*args, *after)


def diagonal(gain_row):
    r = lax.broadcasted_iota(jnp.int32, (LANES, LANES), 0)
    c = lax.broadcasted_iota(jnp.int32, (LANES, LANES), 1)
    return jnp.where(r == c, jnp.broadcast_to(gain_row.astype(F32), (LANES, LANES)), 0.0)


def lane_low(rows):
    return lax.broadcasted_iota(jnp.int32, (rows, LANES), 1) < LANES // 2


def lane_swap(block):
    return jnp.concatenate([block[:, LANES // 2 :], block[:, : LANES // 2]], axis=1)


def pack_attention(who_ref, w_ref, gain_row, keep, got, packed_ref, top):
    me, core = who_ref[0], who_ref[1]
    side, second = me & 1, me >> 1
    out = jnp.where(core == side, keep, got)
    diag = diagonal(gain_row).astype(BF16)
    low = lane_low(LANES)

    def head(t):
        chunk = pl.multiple_of(((t // 4) * 8 + 2 * (t % 4) + side) * LANES, LANES)
        got = dot(diag, w_ref[0, :, pl.ds(chunk, LANES)])
        turned = lane_swap(got)
        if t % 2 == 0:
            return jnp.where(second == 0, got, turned)
        return jnp.where(second == 0, turned, got)

    for u in range(6):
        pair = jnp.where(low, head(2 * u), head(2 * u + 1))
        packed_ref[top : top + LANES, u * LANES : (u + 1) * LANES] = pair.astype(BF16)
    for c in range(4):
        packed_ref[top + c * 32 : top + (c + 1) * 32, 768:1024] = out[:, c * 256 : (c + 1) * 256]


def pack_up(me, up_ref, gain_row, packed_ref, top):
    diag = diagonal(gain_row).astype(BF16)
    for j in range(8):
        chunk = pl.multiple_of((j * 4 + me) * LANES, LANES)
        packed_ref[top : top + LANES, j * LANES : (j + 1) * LANES] = dot(
            diag, up_ref[0, :, pl.ds(chunk, LANES)]
        ).astype(BF16)


def pack_down(me, down_ref, packed_ref, top):
    packed_ref[top : top + LANES, :] = down_ref[0, pl.ds(pl.multiple_of(me * LANES, LANES), LANES), :]


def prepare_first(who_ref, w_ref, gain_a, keep_ref, got_ref, up_ref, gain_m, packed_ref):
    pack_attention(who_ref, w_ref, gain_a[0:1, :], keep_ref[0], got_ref[0], packed_ref, 0)
    pack_up(who_ref[0], up_ref, gain_m[0:1, :], packed_ref, LANES)


def prepare_second(who_ref, w_ref, gain_a, keep_ref, got_ref, down_ref, packed_ref):
    pack_attention(who_ref, w_ref, gain_a[1:2, :], keep_ref[1], got_ref[1], packed_ref, LANES)
    pack_down(who_ref[0], down_ref, packed_ref, 0)


def prepare_third(who_ref, up_ref, gain_m, down_ref, packed_ref):
    pack_up(who_ref[0], up_ref, gain_m[1:2, :], packed_ref, 0)
    pack_down(who_ref[0], down_ref, packed_ref, LANES)


def image_numbers(rows, flag, lens):
    counts = [sum((rows >= t * n).astype(jnp.int32) for t in range(1, most + 1)) for n, most in lens]
    return jnp.where(flag == 1, counts[1], counts[0])


def make_mixing(flag_ref, low_ref, high_ref, mixing_ref, *, lens):
    rows = mixing_ref.shape[0]
    flag = flag_ref[0]

    def spread_rows(index_ref, length, most):
        count = index_ref.shape[0]
        columns = lax.broadcasted_iota(jnp.int32, (count, mixing_ref.shape[1]), 1)
        mix = jnp.zeros((count, mixing_ref.shape[1]), F32)
        for slot in range(4):
            mix = mix + MIX_WEIGHTS[slot] * (index_ref[:, slot : slot + 1] == columns).astype(F32)
        r = lax.broadcasted_iota(jnp.int32, (rows, count), 0)
        c = lax.broadcasted_iota(jnp.int32, (rows, count), 1)
        image = sum((r >= t * length).astype(jnp.int32) for t in range(1, most + 1))
        pick = ((r - image * length == c) & (r < most * length)).astype(BF16)
        return dot(pick, mix.astype(BF16))

    low = spread_rows(low_ref, *lens[0])
    high = spread_rows(high_ref, *lens[1])
    mixing_ref[...] = jnp.where(flag == 1, high, low).astype(BF16)


def write_norm(hidden, xhat_ref):
    xhat_ref[...] = normalize(hidden)[0].astype(BF16)


def join_table(z_ref, p0, p1, p2, p3, out_ref, table):
    for k, piece in enumerate((p0, p1, p2, p3)):
        table[:, pl.ds(pl.multiple_of((z_ref[0] ^ k) * 256, 256), 256)] = piece[...].astype(F32)
    out_ref[...] = table[...].astype(BF16)


def embed(who_ref, tokens_ref, mixing_ref, t0, t1, t2, t3, hidden_ref, xhat_ref, table):
    size = t0.shape[0]
    for k, piece in enumerate((t0, t1, t2, t3)):
        table[pl.ds(pl.multiple_of((who_ref[0] ^ k) * size, 8), size), :] = piece[...].astype(F32)
    rows = table[: mixing_ref.shape[1], :].astype(BF16)
    hidden = tokens_ref[...].astype(F32) + dot(mixing_ref[...], rows)
    hidden_ref[...] = hidden
    write_norm(hidden, xhat_ref)


def added(p0, r1, r2, r3):
    return (p0[...].astype(F32) + r1[...].astype(F32)) + (r2[...].astype(F32) + r3[...].astype(F32))


def add_norm(h_ref, p0, r1, r2, r3, middle_ref, xhat_ref):
    middle = h_ref[...] + added(p0, r1, r2, r3)
    middle_ref[...] = middle
    write_norm(middle, xhat_ref)


def output_parts(a0, a1, a2, a3, down_ref, *outs):
    down = down_ref[...].reshape(-1, down_ref.shape[2])
    for act_ref, out_ref in zip((a0, a1, a2, a3), outs):
        out_ref[...] = dot(act_ref[...], down).astype(BF16)


def add_output(h_ref, p0, r1, r2, r3, out_ref):
    out_ref[...] = h_ref[...] + added(p0, r1, r2, r3)


def add_norm_backward(g_ref, p0, r1, r2, r3, h_ref, d_ref, low_ref):
    d = g_ref[...] + norm_backward(added(p0, r1, r2, r3), *normalize(h_ref[...]))
    d_ref[...] = d
    low_ref[...] = d.astype(BF16)


def out_chunk(packed_ref, c):
    return packed_ref[:, c * 32 : (c + 1) * 32, 768:1024].reshape(256, 256)


def attention_forward(flag_ref, x_ref, w_ref, proj_ref, p_ref, *, lens):
    rows = x_ref.shape[0]
    flag = flag_ref[0]
    width = x_ref.shape[1]
    mask = image_numbers(lax.broadcasted_iota(jnp.int32, (rows, 1), 0), flag, lens) == image_numbers(
        lax.broadcasted_iota(jnp.int32, (1, rows), 1), flag, lens
    )
    for c in range(3):
        w = w_ref[:, :, c * 256 : (c + 1) * 256].reshape(width, 256)
        proj_ref[:, c * 256 : (c + 1) * 256] = dot(x_ref[...], w).astype(BF16)
    low = lane_low(rows)
    zero = jnp.zeros((), BF16)
    for u in range(2):
        q = proj_ref[:, u * LANES : (u + 1) * LANES] * jnp.asarray(0.125, BF16)
        k = proj_ref[:, 256 + u * LANES : 256 + (u + 1) * LANES]
        v = proj_ref[:, 512 + u * LANES : 512 + (u + 1) * LANES]
        total = None
        for keep in (low, ~low):
            s = dot_nt(jnp.where(keep, q, zero), k)
            s = jnp.where(mask, s, NEG_FILL)
            powers = jnp.exp(s - jnp.max(s, axis=-1, keepdims=True))
            probs = powers * (1.0 / jnp.sum(powers, axis=-1, keepdims=True))
            o = dot(probs.astype(BF16), jnp.where(keep, v, zero))
            total = o if total is None else total + o
        proj_ref[:, 768 + u * LANES : 768 + (u + 1) * LANES] = total.astype(BF16)
    for c in range(4):
        p_ref[:, c * 256 : (c + 1) * 256] = dot(proj_ref[:, 768:], out_chunk(w_ref, c)).astype(BF16)


def attention_backward(flag_ref, d_ref, proj_ref, w_ref, dproj_ref, p_ref, *, lens):
    rows, width = d_ref.shape
    flag = flag_ref[0]
    mask = image_numbers(lax.broadcasted_iota(jnp.int32, (rows, 1), 0), flag, lens) == image_numbers(
        lax.broadcasted_iota(jnp.int32, (1, rows), 1), flag, lens
    )
    d_o = sum(dot_nt(d_ref[:, c * 256 : (c + 1) * 256], out_chunk(w_ref, c)) for c in range(4))
    d_o = d_o.astype(BF16)
    low = lane_low(rows)
    zero = jnp.zeros((), BF16)
    scale = jnp.asarray(0.125, BF16)
    for u in range(2):
        q = proj_ref[:, u * LANES : (u + 1) * LANES] * scale
        k = proj_ref[:, 256 + u * LANES : 256 + (u + 1) * LANES]
        v = proj_ref[:, 512 + u * LANES : 512 + (u + 1) * LANES]
        g = d_o[:, u * LANES : (u + 1) * LANES]
        dq = dk = dv = None
        for keep in (low, ~low):
            k_own = jnp.where(keep, k, zero)
            s = jnp.where(mask, dot_nt(k_own, q), NEG_FILL)
            powers = jnp.exp(s - jnp.max(s, axis=0, keepdims=True))
            probs = powers * (1.0 / jnp.sum(powers, axis=0, keepdims=True))
            d_probs = dot_nt(jnp.where(keep, v, zero), g)
            centre = jnp.sum(probs * d_probs, axis=0, keepdims=True)
            d_scores = (probs * (d_probs - centre)).astype(BF16)
            terms = (
                dot_t(d_scores, k_own),
                dot(d_scores, jnp.where(keep, q, zero)),
                dot(probs.astype(BF16), jnp.where(keep, g, zero)),
            )
            dq, dk, dv = terms if dq is None else (dq + terms[0], dk + terms[1], dv + terms[2])
        dproj_ref[:, u * LANES : (u + 1) * LANES] = (dq * 0.125).astype(BF16)
        dproj_ref[:, 256 + u * LANES : 256 + (u + 1) * LANES] = dk.astype(BF16)
        dproj_ref[:, 512 + u * LANES : 512 + (u + 1) * LANES] = dv.astype(BF16)
    total = None
    for c in range(3):
        w = w_ref[:, :, c * 256 : (c + 1) * 256].reshape(width, 256)
        term = dot_nt(dproj_ref[:, c * 256 : (c + 1) * 256], w)
        total = term if total is None else total + term
    p_ref[...] = total.astype(BF16)


def gelu_parts(pre):
    upto = 0.5 * (1.0 + lax.erf(pre * math.sqrt(0.5)))
    density = jnp.exp(-0.5 * pre * pre) * (1.0 / math.sqrt(2.0 * math.pi))
    return pre * upto, upto + pre * density


def mlp_up(x_ref, up_ref, both_ref):
    width = x_ref.shape[1]
    for c in range(4):
        cols = slice(c * 256, (c + 1) * 256)
        act, slope = gelu_parts(dot(x_ref[...], up_ref[:, :, cols].reshape(width, 256)))
        both_ref[0, :, cols] = act.astype(BF16)
        both_ref[1, :, cols] = slope.astype(BF16)


def mlp_down(*refs):
    count = len(refs) // 2
    down = refs[count][...].reshape(-1, refs[count].shape[2])
    for act_ref, out_ref in zip(refs[:count], refs[count + 1 :]):
        out_ref[...] = dot(act_ref[0], down).astype(BF16)


def mlp_backward(d_ref, slope_ref, up_ref, down_ref, dpre_ref, p_ref):
    width = d_ref.shape[1]
    for c in range(4):
        cols = slice(c * 256, (c + 1) * 256)
        d_act = dot_nt(d_ref[...], down_ref[2 * c : 2 * c + 2].reshape(256, width))
        dpre_ref[:, cols] = (d_act * slope_ref[0, :, cols].astype(F32)).astype(BF16)
    p_ref[...] = dot_nt(dpre_ref[...], up_ref[...].reshape(width, width)).astype(BF16)


def mlp_both(x_ref, d_ref, up_ref, down_ref, act_ref, dpre_ref, back_ref):
    width = x_ref.shape[1]
    for c in range(4):
        cols = slice(c * 256, (c + 1) * 256)
        act, slope = gelu_parts(dot(x_ref[...], up_ref[:, :, cols].reshape(width, 256)))
        act_ref[:, cols] = act.astype(BF16)
        d_act = dot_nt(d_ref[...], down_ref[2 * c : 2 * c + 2].reshape(256, width))
        dpre_ref[:, cols] = (d_act * slope).astype(BF16)
    back_ref[...] = dot_nt(dpre_ref[...], up_ref[...].reshape(width, width)).astype(BF16)


def summed(left, right, rows, cols=slice(None)):
    total = None
    for a, b in zip(left, right):
        term = dot_t(a[:, rows], b[:, cols])
        total = term if total is None else total + term
    return total


def stack_rows(blocks, out_ref):
    rows = blocks[0].shape[0]
    tall = -(-rows // 32) * 32
    for k, block in enumerate(blocks):
        out_ref[k * tall + rows // 16 * 16 : (k + 1) * tall, :] = jnp.zeros(
            (tall - rows // 16 * 16, out_ref.shape[1]), BF16
        )
        out_ref[k * tall : k * tall + rows, :] = block


def grads_mlp(*refs):
    x, dpre, act, d, out_ref, left, right = refs[:4], refs[4:8], refs[8:12], refs[12:16], *refs[16:]
    acts = [a[0] if len(a.shape) == 3 else a[...] for a in act]
    pairs = (([a[...] for a in x], dpre), (acts, d))
    for half, (first, second) in enumerate(pairs):
        stack_rows(first, left)
        stack_rows([b[...] for b in second], right)
        for t in range(4):
            total = dot_t(left[:, t * 256 : (t + 1) * 256], right[...]).astype(BF16)
            out_ref[2 * t : 2 * t + 2, half * LANES : (half + 1) * LANES, :] = total.reshape(2, LANES, -1)


def stack_attention(refs, left, right, narrow):
    x, dproj, kept, d = refs[:4], refs[4:8], refs[8:12], refs[12:16]
    stack_rows([a[...] for a in x], left)
    stack_rows([a[...] for a in dproj], right.at[:, :768])
    stack_rows([a[...] for a in kept], narrow)


def grads_attention(*refs):
    out_ref, left, right, narrow = refs[16:]
    stack_attention(refs, left, right, narrow)
    for t in range(4):
        total = dot_t(left[:, t * 256 : (t + 1) * 256], right[:, :768]).astype(BF16)
        out_ref[2 * t : 2 * t + 2, :LANES, :768] = total.reshape(2, LANES, -1)
    stack_rows([a[...] for a in refs[12:16]], right)
    for c in range(4):
        total = dot_t(narrow[...], right[:, c * 256 : (c + 1) * 256])
        out_ref[:, c * 32 : (c + 1) * 32, 768:1024] = total.astype(BF16).reshape(8, 32, 256)


def rows_of(j):
    return pl.ds(pl.multiple_of(j * LANES, LANES), LANES)


def grads_attention_sides(core_ref, *refs):
    theirs, mine, (left, right, narrow) = refs[16:20], refs[20], refs[21:]
    core = core_ref[0]
    stack_attention(refs, left, right, narrow)
    for z in range(4):
        theirs[z][:, :768] = dot_t(left[:, rows_of(z * 2 + 1 - core)], right[:, :768]).astype(BF16)
    for z in range(4):
        mine[z, :, :768] = dot_t(left[:, rows_of(z * 2 + core)], right[:, :768]).astype(BF16)
    stack_rows([a[...] for a in refs[12:16]], right)
    for c in range(4):
        total = dot_t(narrow[...], right[:, c * 256 : (c + 1) * 256]).astype(BF16).reshape(8, 32, 256)
        rows = slice(c * 32, (c + 1) * 32)
        for z in range(4):
            first, second = total[2 * z], total[2 * z + 1]
            theirs[z][rows, 768:1024] = jnp.where(core == 0, second, first)
            mine[z, rows, 768:1024] = jnp.where(core == 0, first, second)


def add_pair(mine_ref, *refs):
    for z in range(4):
        refs[4][z] = (mine_ref[z].astype(F32) + refs[z][...].astype(F32)).astype(BF16)


def last_norm(g_ref, p0, r1, r2, r3, h_ref, mixing_ref, term_ref, d_ref, out_ref, packed, sem):
    d = g_ref[...] + norm_backward(added(p0, r1, r2, r3), *normalize(h_ref[...]))
    d_ref[...] = d
    high = d.astype(BF16)
    low = (d - high.astype(F32)).astype(BF16)
    table = dot_t(mixing_ref[...], high) + dot_t(mixing_ref[...], low)
    packed[...] = jnp.zeros(packed.shape, BF16)
    for j in range(8):
        for c in range(-(-table.shape[0] // 32)):
            size = min(32, table.shape[0] - 32 * c)
            part = table[32 * c : 32 * c + size, j * LANES : (j + 1) * LANES]
            packed[j, :size, c * LANES : (c + 1) * LANES] = part.astype(BF16)
    copy = pltpu.make_async_copy(packed, out_ref.at[:, LANES : LANES + 32, :], sem.at[0])
    copy.start()
    copy.wait()


def unpack_table(refs, out_ref):
    g = [ref[LANES : LANES + 32, :].astype(F32) for ref in refs]
    total = (g[0] + g[1]) + (g[2] + g[3])
    for c in range(-(-out_ref.shape[0] // 32)):
        size = min(32, out_ref.shape[0] - 32 * c)
        out_ref[32 * c : 32 * c + size, :] = total[:size, c * LANES : (c + 1) * LANES]


def finish_mlp(me_ref, *refs, merged):
    g, up_ref, gain_ref, dup_ref, ddown_ref, dgain_ref = refs[:5], refs[5], refs[6], *refs[-3:]
    me = me_ref[0]
    low = 192 if merged else LANES
    column = jnp.sum(diagonal(gain_ref[0]), axis=1, keepdims=True)
    total = jnp.zeros((LANES, LANES), F32)
    downs = [piece[low : low + LANES, :] for piece in g[:3]] + [g[4][:LANES, :]]
    for k, piece in enumerate(downs):
        rows = pl.ds(pl.multiple_of((me ^ k) * LANES, LANES), LANES)
        ddown_ref[0, rows, :] = piece.astype(F32)
    ups = [piece[:LANES, :] for piece in g[:4]]
    for i in range(4):
        got = jnp.where(
            me == i, ups[0], jnp.where(me == i ^ 1, ups[1], jnp.where(me == i ^ 2, ups[2], ups[3]))
        ).astype(F32)
        for j in range(8):
            cols = slice((j * 4 + i) * LANES, (j * 4 + i + 1) * LANES)
            part = got[:, j * LANES : (j + 1) * LANES]
            dup_ref[0, :, cols] = part * column
            total = total + part * up_ref[0, :, cols].astype(F32)
    dgain_ref[0] = jnp.sum(total.T, axis=0, keepdims=True)


def attention_rows(refs):
    if len(refs) == 4:
        return [ref[:LANES, :] for ref in refs]
    rows = [jnp.concatenate([ref[128:192, :], ref[320:384, :]], axis=0) for ref in refs[:3]]
    return rows + [jnp.concatenate([ref[128:192, :] for ref in refs[3:]], axis=0)]


def by_owner(me, pieces, i):
    g0, g1, g2, g3 = pieces
    return jnp.where(me == i, g0, jnp.where(me == i ^ 1, g1, jnp.where(me == i ^ 2, g2, g3)))


def split_out(who_ref, *refs):
    keep_ref, give_ref = refs[-2:]
    packed = [piece[:, 768:] for piece in attention_rows(refs[:-2])]
    me, core = who_ref[0], who_ref[1]
    for second in range(2):
        even, odd = by_owner(me, packed, 2 * second), by_owner(me, packed, 2 * second + 1)
        keep_ref[second] = jnp.where(core == 0, even, odd)
        give_ref[second] = jnp.where(core == 0, odd, even)


def finish_attention(who_ref, *refs, count):
    g, (w_ref, gain_ref, keep_ref, got_ref) = refs[:count], refs[count : count + 4]
    if count == 4:
        unpack_table(g, refs[-1])
        refs = refs[:-1]
    dqkv_ref, dout_ref, dgain_ref = refs[-3:]
    me, core = who_ref[0], who_ref[1]
    column = jnp.sum(diagonal(gain_ref[0]), axis=1, keepdims=True)
    total = jnp.zeros((LANES, LANES), F32)
    low = lane_low(LANES)
    rows = [piece[:, :768] for piece in attention_rows(g)]
    owned = [by_owner(me, rows, i).astype(F32) for i in range(4)]
    for t in range(12):
        u = t // 2
        for side in range(2):
            first = owned[side][:, u * LANES : (u + 1) * LANES]
            second = owned[side + 2][:, u * LANES : (u + 1) * LANES]
            if t % 2 == 0:
                part = jnp.where(low, first, lane_swap(second))
            else:
                part = jnp.where(low, lane_swap(first), second)
            chunk = (t // 4) * 8 + 2 * (t % 4) + side
            cols = slice(chunk * LANES, (chunk + 1) * LANES)
            dqkv_ref[0, :, cols] = part * column
            total = total + part * w_ref[0, :, cols].astype(F32)
    dgain_ref[0] = jnp.sum(total.T, axis=0, keepdims=True)
    for second in range(2):
        keep, got = keep_ref[second], got_ref[second]
        halves = (jnp.where(core == 0, keep, got), jnp.where(core == 0, got, keep))
        for h, part in enumerate(halves):
            for c in range(4):
                top = (2 * second + h) * 32
                dout_ref[0, top : top + 32, c * 256 : (c + 1) * 256] = part[c * 32 : (c + 1) * 32, :].astype(F32)


def local_fast(
    tokens,
    pos_table,
    index_lo,
    index_hi,
    resolution,
    gain_attn,
    w_qkv,
    w_out,
    gain_mlp,
    w_up,
    w_down,
    cotangent,
):
    rows, width = tokens.shape
    layers = w_qkv.shape[0]
    square = Square()
    me = square.me
    me1 = me.reshape(1).astype(jnp.int32)
    shard = lax.axis_index("fsdp")
    core, deep = shard % 2, shard // 2
    deep1 = deep.reshape(1).astype(jnp.int32)
    len_low, len_high = index_lo.shape[0], index_hi.shape[0]
    lens = ((len_low, rows // len_low), (len_high, rows // len_high))
    block = (rows, width)
    blocks = range(4)

    def over_fsdp(x, k):
        return lax.ppermute(x, "fsdp", [(j, j ^ k) for j in range(8)])

    def layer_of(array, depth):
        return pl.BlockSpec((1,) + array.shape[1:], lambda *_: (depth,) + (0,) * (array.ndim - 1))

    who = jnp.stack([me, core]).astype(jnp.int32)
    head_side = me >> 1

    def out_rows(half):
        return lax.dynamic_slice(w_out, (0, (head_side * 2 + half) * 32, 0), (layers, 32, width))

    keep, got = out_rows(core), over_fsdp(out_rows(1 - core), 1)
    gains_a = gain_attn.reshape(layers, 1, LANES)
    gains_m = gain_mlp.reshape(layers, 1, LANES)

    def part(top):
        return pl.BlockSpec((8, LANES, width), lambda *_: (0, top, 0))

    def fetch(body, args, specs, after=()):
        (packed,) = call(
            body, [((2 * LANES, width), BF16)], [who] + args, [scalars()] + specs, after=after, limit=60
        )
        return lax.all_gather(packed, "fsdp", axis=0, tiled=False)

    first_w = fetch(
        prepare_first,
        [w_qkv, gain_attn, keep, got, w_up, gain_mlp],
        [layer_of(w_qkv, 0), None, None, None, layer_of(w_up, 0), None],
    )

    flag = resolution[me]
    flag1 = flag.reshape(1)
    flags = [resolution[owner].reshape(1) for owner in square.owners()]
    shard_count, group_count = 8, resolution.shape[0]
    high_groups = jnp.sum(resolution)
    tokens_low = ((group_count - high_groups) * shard_count * lens[0][1] * len_low).astype(F32)
    tokens_high = (high_groups * shard_count * lens[1][1] * len_high).astype(F32)
    token_share = 2.0 * jnp.where(flag == 1, tokens_high, tokens_low) / (tokens_low + tokens_high)
    live = jnp.where(flag == 1, lens[1][1] * len_high, lens[0][1] * len_low)
    weight = jnp.where(jnp.arange(rows, dtype=jnp.int32) < live, token_share, 0.0)
    gradient = cotangent.astype(F32) * weight[:, None]

    normed = [(block, F32), (block, BF16)]
    size = -(-len_high // 32) * 8
    mine = lax.dynamic_slice(
        jnp.pad(pos_table, ((0, 4 * size - len_high), (0, 0))), (me * size, 0), (size, LANES)
    )
    other = over_fsdp(mine, 1)
    pair = jnp.concatenate([jnp.where(core == 0, mine, other), jnp.where(core == 0, other, mine)], axis=1)
    pieces = [pair] + [over_fsdp(pair, 2 * k) for k in range(1, 4)]
    (mine,) = call(
        join_table,
        [((size, width), BF16)],
        [deep1] + pieces,
        [scalars()] + [None] * 4,
        scratch=[VMEM((size, width), F32)],
    )
    (mixing,) = call(
        functools.partial(make_mixing, lens=lens),
        [((rows, len_high), BF16)],
        [flag1, index_lo, index_hi],
        [scalars(), None, None],
    )
    hidden, xhat = call(
        embed,
        normed,
        [who, tokens, mixing] + square.spread(mine),
        [scalars()] + [None] * 6,
        scratch=[VMEM((4 * size, width), F32)],
    )
    second_w = fetch(
        prepare_second,
        [w_qkv, gain_attn, keep, got, w_down],
        [layer_of(w_qkv, 1), None, None, None, layer_of(w_down, 0)],
        [xhat],
    )
    third_w = fetch(
        prepare_third,
        [w_up, gain_mlp, w_down],
        [layer_of(w_up, 1), None, layer_of(w_down, 1)],
        [xhat],
    )
    attn_w = [(first_w, part(0)), (second_w, part(1))]

    def tie(*values):
        return lax.optimization_barrier(values)

    def tie_last(es, term):
        near, term = tie(es[:3], term)
        far, near, term = tie(es[3], near, term)
        return near + [far], term

    def chain(kernel):
        done = []
        for k in blocks:
            done.append(kernel(k, [d[0] for d in done[-1:]]))
        return done

    def collect(parts):
        return [parts[0]] + [square.swap(parts[k], k) for k in range(1, 4)]

    d_top = square.spread(gradient.astype(BF16))
    saved = []
    for depth in range(layers):
        a_w, a_part = attn_w[depth]
        xs = square.spread(xhat)
        got = chain(
            lambda k, after: call(
                functools.partial(attention_forward, lens=lens),
                [(block, BF16)] * 2,
                [flags[k], xs[k], a_w],
                [scalars(), None, a_part],
                after=after,
            )
        )
        kept = [g[0] for g in got]
        es = collect([g[1] for g in got])
        if depth == 0:
            es, d_top = tie(es, d_top)
        before, (middle, xhat) = hidden, call(add_norm, normed, [hidden] + es)
        if depth > 0:
            xhat, third_w = tie(xhat, third_w)
        ms = square.spread(xhat)
        if depth < layers - 1:
            acts = chain(
                lambda k, after: call(
                    mlp_up, [((2,) + block, BF16)], [ms[k], first_w], [None, part(1)], after=after
                )
            )
            acts = [a[0] for a in acts]
            first_half = pl.BlockSpec((1,) + block, lambda *_: (0, 0, 0))
            parts = call(
                mlp_down, [(block, BF16)] * 3, acts[1:] + [second_w], [first_half] * 3 + [part(0)], after=acts[:1]
            )
            (own,) = call(
                mlp_down, [(block, BF16)], [acts[0], second_w], [first_half, part(0)], after=parts[:1]
            )
            parts = [own] + list(parts)
            saved.append((before, xs, kept, middle, ms, acts))
            hidden, xhat = call(add_norm, normed, [middle] + collect(parts))
        else:
            got = chain(
                lambda k, after: call(
                    mlp_both,
                    [(block, BF16)] * 3,
                    [ms[k], d_top[k], third_w, third_w],
                    [None, None, part(0), part(1)],
                    after=after,
                )
            )
            acts, dpres, backs = ([g[t] for g in got] for t in range(3))
            top_acts = acts
            saved.append((before, xs, kept, middle, ms, acts))

    def far_halves(x, y):
        half = x.shape[0] // 2
        return [square.swap(x[:half], 2), square.swap(y[half:], 1)]

    core1 = core.reshape(1).astype(jnp.int32)
    tall = 4 * (-(-rows // 32) * 32)

    def home(term):
        return lax.psum_scatter(term, "fsdp", scatter_dimension=0, tiled=False)

    homes_m, homes_a = [None] * layers, [None] * layers
    for depth in reversed(range(layers)):
        top = depth == layers - 1
        a_w, a_part = attn_w[depth]
        before, xs, kept, middle, ms, acts = saved[depth]
        ds = d_top if top else square.spread(low)
        if not top:
            second_half = pl.BlockSpec((1,) + block, lambda *_: (1, 0, 0))
            got = chain(
                lambda k, after: call(
                    mlp_backward,
                    [(block, BF16)] * 2,
                    [ds[k], acts[k], first_w, second_w],
                    [None, second_half, part(1), part(0)],
                    after=after or [homes_m[1]],
                )
            )
            dpres, backs = ([g[t] for g in got] for t in range(2))
        es = collect(backs)
        first_half = pl.BlockSpec((1,) + block, lambda *_: (0, 0, 0))
        (term,) = call(
            grads_mlp,
            [((8, 2 * LANES, width), BF16)],
            list(ms) + list(dpres) + list(acts) + list(ds),
            [None] * 8 + [None if top else first_half] * 4 + [None] * 4,
            scratch=[VMEM((tall, width), BF16)] * 2,
        )
        if top:
            near, term = tie(es[:3], term)
            homes_m[depth] = home(term)
            far, near, _ = tie(es[3], near, term)
            es = near + [far]
        else:
            es, term = tie_last(es, term)
            homes_m[depth] = home(term)
        d_middle, low = call(add_norm_backward, normed, [gradient] + es + [middle], limit=60)
        if not top:
            m, a = homes_m[1], homes_a[1]
            merged = jnp.concatenate([m[:LANES], a[:64], m[LANES:], a[64:]], axis=0)
        ds = square.spread(low)
        got = chain(
            lambda k, after: call(
                functools.partial(attention_backward, lens=lens),
                [((rows, 768), BF16), (block, BF16)],
                [flags[k], ds[k], kept[k], a_w],
                [scalars(), None, None, a_part],
                after=after or ([] if top else [merged]),
            )
        )
        dprojs = [g[0] for g in got]
        es = collect([g[1] for g in got])
        out_part = pl.BlockSpec((rows, 256), lambda *_: (0, 3))
        stacks = [VMEM((tall, width), BF16)] * 2 + [VMEM((tall, 256), BF16)]
        operands = list(xs) + dprojs + list(kept) + list(ds)
        specs = [None] * 8 + [out_part] * 4 + [None] * 4
        if top:
            *theirs, mine = call(
                grads_attention_sides,
                [((LANES, width), BF16)] * 4 + [((4, LANES, width), BF16)],
                [core1] + operands,
                [scalars()] + specs,
                scratch=stacks,
            )
            got = [over_fsdp(part, 1) for part in theirs]
            es, mine = tie_last(es, mine)
            (term,) = call(add_pair, [(mine.shape, BF16)], [mine] + got, after=[es[3]])
            es, term = tie(es, term)
            homes_a[depth] = lax.psum_scatter(
                term, "fsdp", scatter_dimension=0, tiled=False, axis_index_groups=[[0, 2, 4, 6], [1, 3, 5, 7]]
            )
            last_middle = middle
            gradient, low = call(add_norm_backward, normed, [d_middle] + es + [before], limit=60)
        else:
            near = [square.swap(merged, 1), square.swap(merged, 2)]
            (term,) = call(grads_attention, [((8, LANES + 32, width), BF16)], operands, specs, after=near, scratch=stacks)
            es, term = tie_last(es, term)
            anywhere = pl.BlockSpec(memory_space=pl.ANY)
            gradient, term = call(
                last_norm,
                [(block, F32), (term.shape, BF16)],
                [d_middle] + es + [before, mixing, term],
                [None] * 7 + [anywhere],
                out_specs=[whole(block), anywhere],
                aliases={7: 1},
                limit=60,
                scratch=[VMEM((8, 32, width), BF16), pltpu.SemaphoreType.DMA((1,))],
            )
            homes_a[0] = home(term)

    merged = [merged, *near] + far_halves(*near)

    outs = call(
        output_parts, [(block, BF16)] * 4, top_acts + [third_w], [None] * 4 + [part(1)], after=[gradient]
    )
    (output,) = call(add_output, [(block, F32)], [last_middle] + collect(outs))
    homes_m[0], gradient = tie(homes_m[0], gradient)
    x, y = square.swap(homes_m[0], 1), square.swap(homes_m[0], 2)
    homes_m[0] = [homes_m[0], x, y] + far_halves(x, y)
    big = [None] * 6

    def finish(body, depth, args, shapes, prior):
        extra = [] if prior[0] is None else prior
        specs = [layer_of(a, depth) if a is w_up or a is w_qkv or a is gains_a or a is gains_m else None for a in args]
        return call(
            body,
            [(shape, F32) for shape in shapes],
            [who] + args + extra,
            [scalars()] + specs + [pl.BlockSpec(memory_space=pl.ANY)] * len(extra),
            aliases={1 + len(args) + t: t for t in range(len(extra))},
            out_specs=[
                layer_of(jax.ShapeDtypeStruct(shape, F32), depth) if len(shape) == 3 else whole(shape)
                for shape in shapes
            ],
        )

    def finish_m(depth, pieces):
        shapes = [w_up.shape, w_down.shape, gains_m.shape]
        body = functools.partial(finish_mlp, merged=depth > 0)
        big[3:] = finish(body, depth, pieces + [w_up, gains_m], shapes, big[3:])

    def finish_a(depth, pieces):
        keep, give = call(
            split_out, [((2, LANES, 256), BF16)] * 2, [who] + pieces, [scalars()] + [None] * len(pieces)
        )
        shapes = [w_qkv.shape, w_out.shape, gains_a.shape]
        body = functools.partial(finish_attention, count=len(pieces))
        args = pieces + [w_qkv, gains_a, keep, over_fsdp(give, 1)]
        if len(pieces) == 4:
            shapes = shapes + [(len_high, LANES)]
        big[:3] = finish(body, depth, args, shapes, big[:3])

    finish_m(1, merged)
    finish_a(1, merged)
    homes_a[0], homes_m[0], big, output = tie(homes_a[0], homes_m[0], big, output)
    pieces = square.spread(homes_a[0])
    finish_m(0, homes_m[0])
    pieces, big = tie(pieces, big)
    finish_a(0, pieces)
    d_table = big.pop(3)
    return (
        output,
        gradient,
        d_table,
        big[2].reshape(layers, LANES),
        big[0],
        big[1],
        big[5].reshape(layers, LANES),
        big[3],
        big[4],
    )


def solution(mesh):
    in_specs = (
        P(("dp", "fsdp"), None),
        P(None, "fsdp"),
        P(),
        P(),
        P(),
        P(None, "fsdp"),
        P(None, "fsdp", None),
        P(None, "fsdp", None),
        P(None, "fsdp"),
        P(None, "fsdp", None),
        P(None, "fsdp", None),
        P(("dp", "fsdp"), None),
    )
    out_specs = (
        P(("dp", "fsdp"), None),
        P(("dp", "fsdp"), None),
        P(None, "fsdp"),
        P(None, "fsdp"),
        P(None, "fsdp", None),
        P(None, "fsdp", None),
        P(None, "fsdp"),
        P(None, "fsdp", None),
        P(None, "fsdp", None),
    )
    fast = mesh.shape["dp"] == 4 and mesh.shape["fsdp"] == 8
    local = local_fast if fast else local_general
    return jax.shard_map(local, mesh=mesh, in_specs=in_specs, out_specs=out_specs, check_vma=False)
```
